32 devices in a mesh: row: 4 (over x, core), col: 8 (over z, y).
Axes of the slice: x: 2, y: 2, z: 4, core: 2. Of those that a mesh axis runs over, the one named last changes fastest.
Arguments:
- tokens: bfloat16 [8, 768, 1024], P('col', 'row'), may hold values from -6 to 6
- gain_one: float32 [768], replicated, may hold values from 0.5 to 1.5
- gain_two: float32 [768], replicated, may hold values from 0.5 to 1.5
- w_query: bfloat16 [768, 768], P('row', 'col'), may hold values from -0.21875 to 0.21875
- w_key: bfloat16 [768, 768], P('row', 'col'), may hold values from -0.21875 to 0.21875
- w_value: bfloat16 [768, 768], P('row', 'col'), may hold values from -0.21875 to 0.21875
- w_out: bfloat16 [768, 768], P('row', 'col'), may hold values from -3.5 to 3.5
- w_router: bfloat16 [768, 32], P('row', 'col'), may hold values from -0.15625 to 0.15625
- w_in: bfloat16 [768, 98304], P('row', 'col'), may hold values from -0.21875 to 0.21875
- w_expert_out: bfloat16 [3072, 24576], P('row', 'col'), may hold values from -3.5 to 3.5
- bias_table: float32 [32, 12], replicated, may hold values from -4 to 4
- segment: int32 [8, 1024], P('col'), may hold values from 0 to 3, never falling along the last dimension, each value on 1 to 768 neighbouring positions
- expert: int32 [8, 1024, 1], P('col'), may hold values from 0 to 31; in each aligned block of 1024 rows (0 to 1023, 1024 to 2047, ..., all dimensions but the last counted through in order) at most 48 rows name the same one
- bucket: int32 [8, 1024, 1024], P('col', 'row'), may hold values from 0 to 31
- cotangent: bfloat16 [8, 768, 1024], P('col', 'row'), may hold values from -6 to 6
Outputs:
- layer_out: bfloat16 [8, 768, 1024], P('col', 'row')
- grad_tokens: bfloat16 [8, 768, 1024], P('col', 'row')
- grad_gain_one: float32 [768], replicated
- grad_gain_two: float32 [768], replicated
- grad_query: float32 [768, 768], P('row', 'col')
- grad_key: float32 [768, 768], P('row', 'col')
- grad_value: float32 [768, 768], P('row', 'col')
- grad_out: float32 [768, 768], P('row', 'col')
- grad_router: float32 [768, 32], P('row', 'col')
- grad_in: float32 [768, 98304], P('row', 'col')
- grad_expert_out: float32 [3072, 24576], P('row', 'col')
- grad_table: float32 [32, 12], replicated
The draws below stay inside these ranges and needn't reach their ends.
Inputs may be any that keep to these rules, and one draw needn't show every extreme that they name: Within a sequence at most 48 tokens name the same expert. `segment`: never falls along a sequence.
All inputs are finite; a program needn't handle non-finite values.
Results may differ from the reference program's by a relative error of at most 0.014.
Values may be sent and summed in bfloat16 or wider, within the bound.
No kernel may reach another device: no remote copies, remote signals or barrier semaphores. Data moves between devices by JAX's collectives and lax.ppermute only.
A program may use at most 448 MiB of HBM per device.

```python
import math
import jax
import jax.numpy as jnp
import numpy as np
from jax import lax

D = 768
HEADS = 12
FF = 3072
EXPERTS = 32
BUCKETS = 32
SEQ = 1024
CAPACITY = 48
SEQS = 8


def place_ends(values, stream_key, low, top_value):
    index_at = [jax.random.randint(jax.random.fold_in(stream_key, axis), (), 0, length) for axis, length in enumerate(values.shape)]
    main_axis = values.shape.index(max(values.shape))
    next_to = index_at[:main_axis] + [(index_at[main_axis] + 1) % values.shape[main_axis]] + index_at[main_axis + 1:]
    return values.at[tuple(index_at)].set(low).at[tuple(next_to)].set(top_value)


def levels(key, extent, shards, smallest, high):
    def one(axis_at, parts):
        steps = jax.random.uniform(jax.random.fold_in(jax.random.fold_in(key, 6), axis_at), (parts,), jnp.float32, smallest / len(shards), high / len(shards))
        return jnp.repeat(jnp.exp(steps), extent[axis_at] // parts).reshape((-1,) + (1,) * (len(extent) - axis_at - 1))

    level = one(*shards[0])
    for cut in shards[1:]:
        level = level * one(*cut)
    return level


def profile(count, total, bound, skew):
    loads = [(1 << 20) // math.isqrt(grade ** skew) + 1 for grade in range(2, count + 1)]
    spare, counts = total - bound - (count - 1), [1] * (count - 1)
    while spare > 0:
        movable = [i for i in range(count - 1) if counts[i] < bound]
        whole, budget = sum([loads[i] for i in movable]), spare
        for i in movable:
            extra = min(bound - counts[i], max(1, budget * loads[i] // whole), spare)
            counts[i] = counts[i] + extra
            spare = spare - extra
    return np.array([bound] + counts)


def ragged_sizes(key, amount, total, limit, lean):
    if amount == 2:
        one = jax.random.randint(key, (), max(1, total - limit), min(limit, total - 1) + 1)
        return jnp.stack([one, total - one])
    lengths = jnp.asarray(profile(amount, total, limit, lean), jnp.int32)
    pairs = (amount - 1) // 2
    giver, receiver = lengths[1:1 + 2 * pairs:2], lengths[2:2 + 2 * pairs:2]
    slack = jnp.minimum(giver - 1, limit - receiver)
    moved = jax.random.randint(jax.random.fold_in(key, 1), (pairs,), 0, 1 << 20) % (slack + 1)
    lengths = lengths.at[1:1 + 2 * pairs:2].set(giver - moved).at[2:2 + 2 * pairs:2].set(receiver + moved)
    return lengths[jax.random.permutation(jax.random.fold_in(key, 2), amount)]


def deal_out(rng, own, number, rows, number_of, top, limit, lean):
    order = jax.random.permutation(rng, number_of)
    crowded, common = load_shares(number_of, rows * top, limit, lean, True), load_shares(number_of, rows * top, limit, lean, False)
    places = jnp.arange(number_of)

    def named(lengths, offset_by):
        used = int((lengths > 0).sum())
        fixed = max(1, used // 4)
        shifted = fixed + (places - fixed + offset_by * (used - fixed)) % max(1, number_of - fixed)
        return jnp.zeros((number_of,), jnp.int32).at[order[jnp.where(places < fixed, places, shifted)]].set(jnp.asarray(lengths, jnp.int32))

    lengths = jnp.where(number % 4 == 0, named(crowded, number // 4), named(common, number - number // 4 - 1))
    mixed = jax.random.permutation(jax.random.fold_in(own, 3), number_of)
    source_of, taker = mixed[0:number_of // 2 * 2:2], mixed[1:number_of // 2 * 2:2]
    margin = jnp.minimum(lengths[source_of] - 1, limit - lengths[taker]) // 2
    margin = jnp.where((source_of == order[0]) | (taker == order[0]) | (lengths[taker] == 0), 0, jnp.maximum(margin, 0))
    shifted = jax.random.randint(jax.random.fold_in(own, 4), (number_of // 2,), 0, 1 << 20) % (margin + 1)
    lengths = lengths.at[source_of].add(-shifted).at[taker].add(shifted)
    labels = jnp.searchsorted(jnp.cumsum(lengths), jnp.arange(rows * top), side="right").astype(jnp.int32)
    listing = labels.reshape(top, rows).T
    listing = listing[jax.random.permutation(jax.random.fold_in(own, 1), rows)]
    offset_by = jax.random.randint(jax.random.fold_in(own, 2), (rows, 1), 0, top)
    return jnp.take_along_axis(listing, (jnp.arange(top)[None, :] + offset_by) % top, axis=1)


def load_shares(number_of, total, reach, skew, full):
    weights = [(1 << 20) // math.isqrt(standing ** skew) + 1 for standing in range(1, number_of + 1)]
    largest = reach if full else min(reach, max(-(-total // number_of), total * weights[0] // sum(weights)))
    least = 1 if total - largest >= number_of - 1 else 0
    holding, spare = [largest] + [least] * (number_of - 1), total - largest - least * (number_of - 1)
    while spare > 0:
        candidates = [i for i in range(1, number_of) if holding[i] < largest] or [i for i in range(1, number_of) if holding[i] < reach]
        whole, remaining = sum([weights[i] for i in candidates]), spare
        for i in candidates:
            extra = min(reach - holding[i], max(1, remaining * weights[i] // whole), spare)
            holding[i] = holding[i] + extra
            spare = spare - extra
    return np.array(holding)


def bell_draw(stream_key, dims, scale, most, split=(), kind=jnp.bfloat16):
    array = scale * jax.random.normal(stream_key, dims, jnp.float32)
    if split:
        array = array * levels(stream_key, dims, split, -0.22, 0.18)
    return jnp.clip(array, -most, most).astype(kind)


def setup_inputs(seed: int = 0) -> dict:
    splits = jax.random.split(jax.random.key(seed), 16)
    tokens = bell_draw(splits[0], (SEQS, D, SEQ), 1.0, 6.0, ((0, 8), (1, 4)))
    gain_one = jnp.clip(1.0 + 0.1 * jax.random.normal(splits[1], (D,), jnp.float32), 0.5, 1.5)
    gain_two = jnp.clip(1.0 + 0.1 * jax.random.normal(splits[2], (D,), jnp.float32), 0.5, 1.5)
    w_query = bell_draw(splits[3], (D, D), D ** -0.5, 0.21875, ((0, 4), (1, 8)))
    w_key = bell_draw(splits[4], (D, D), D ** -0.5, 0.21875, ((0, 4), (1, 8)))
    w_value = bell_draw(splits[5], (D, D), D ** -0.5, 0.21875, ((0, 4), (1, 8)))
    w_out = bell_draw(splits[6], (D, D), (max(1, D // 256)) ** -0.5, 3.5, ((0, 4), (1, 8)))
    w_router = bell_draw(splits[7], (D, EXPERTS), (2 * D) ** -0.5, 0.15625, ((0, 4), (1, 8)))
    w_in = bell_draw(splits[8], (D, EXPERTS * FF), D ** -0.5, 0.21875, ((0, 4), (1, 8)))
    w_expert_out = bell_draw(splits[9], (FF, EXPERTS * D), (max(1, FF // EXPERTS // EXPERTS)) ** -0.5, 3.5, ((0, 4), (1, 8)))
    bias_table = bell_draw(splits[10], (BUCKETS, HEADS), 1.0, 4.0, (), jnp.float32)
    segment = jax.vmap(lambda own: jnp.searchsorted(jnp.cumsum(ragged_sizes(own, max(2, SEQ // 256), SEQ, SEQ * 3 // 4, 2)), jnp.arange(SEQ), side="right"))(jax.random.split(splits[11], SEQS)).reshape((SEQS, SEQ)).astype(jnp.int32)
    expert_keys = jax.random.split(jax.random.fold_in(splits[12], 1), SEQS * SEQ // SEQ)
    expert_turns = jax.random.permutation(jax.random.fold_in(splits[12], 3), SEQS * SEQ // SEQ)
    expert = jax.vmap(lambda own, number: deal_out(jax.random.fold_in(splits[12], 2), own, number, SEQ, EXPERTS, 1, CAPACITY, 1))(expert_keys, expert_turns).reshape((SEQS, SEQ, 1))
    bucket = place_ends(jax.random.randint(splits[13], (SEQS, SEQ, SEQ), 0, BUCKETS), jax.random.fold_in(splits[13], 1), 0, BUCKETS - 1).astype(jnp.int32)
    cotangent = bell_draw(splits[14], (SEQS, D, SEQ), 1.0, 6.0, ((0, 8), (1, 4)))
    return dict(tokens=tokens, gain_one=gain_one, gain_two=gain_two, w_query=w_query, w_key=w_key, w_value=w_value, w_out=w_out, w_router=w_router, w_in=w_in, w_expert_out=w_expert_out, bias_table=bias_table, segment=segment, expert=expert, bucket=bucket, cotangent=cotangent)


NORM_EPS = 1e-06
NEG_FILL = -1e+30

@jax.custom_vjp
def low(v):
    return lax.optimization_barrier(v.astype(jnp.bfloat16)).astype(jnp.float32)

@jax.custom_vjp
def low_back(v):
    return v

def low_keep(v):
    return (low(v), None)

def low_pass(kept, grad):
    return (grad,)

def back_keep(v):
    return (v, None)

def back_low(kept, grad):
    return (low(grad),)
low.defvjp(low_keep, low_pass)
low_back.defvjp(back_keep, back_low)

def product(left, right):
    return jnp.dot(left, right, precision=lax.Precision.HIGHEST)

def sequence_layer(tok_seq, doc_seq, exp_seq, buck_seq, gain_one, gain_two, w_query, w_key, w_value, w_out, w_router, w_in, w_expert_out, bias_table):
    seq_len = tok_seq.shape[0]
    model_width = tok_seq.shape[1]
    head_count = bias_table.shape[1]
    head_dim = model_width // head_count
    experts = w_router.shape[1]
    ffn_width = w_expert_out.shape[0]
    in_three = w_in.reshape(model_width, experts, ffn_width)
    out_three = w_expert_out.reshape(ffn_width, experts, model_width)
    inverse_one = lax.rsqrt(lax.optimization_barrier(jnp.mean(tok_seq * tok_seq, axis=1, keepdims=True)) + NORM_EPS)
    normed_one = low(tok_seq * inverse_one * gain_one)
    queries = low_back(low(product(normed_one, w_query))).reshape(seq_len, head_count, head_dim)
    keys_seq = low_back(low(product(normed_one, w_key))).reshape(seq_len, head_count, head_dim)
    values = low_back(low(product(normed_one, w_value))).reshape(seq_len, head_count, head_dim)
    raw_scores = low_back(jnp.einsum('ihd,jhd->hij', queries, keys_seq, precision=lax.Precision.HIGHEST) * head_dim ** (-0.5))
    pair_bias = jnp.transpose(bias_table[buck_seq], (2, 0, 1))
    allowed = doc_seq[:, None] == doc_seq[None, :]
    scores = jnp.where(allowed[None], raw_scores + pair_bias, NEG_FILL)
    attn_probs = low(jax.nn.softmax(scores, axis=2))
    attended = jnp.einsum('hij,jhd->ihd', attn_probs, values, precision=lax.Precision.HIGHEST).reshape(seq_len, model_width)
    attended = low_back(low(attended))
    residual = tok_seq + low_back(product(attended, w_out))
    inverse_two = lax.rsqrt(lax.optimization_barrier(jnp.mean(residual * residual, axis=1, keepdims=True)) + NORM_EPS)
    normed_two = low(residual * inverse_two * gain_two)
    logits = low_back(product(normed_two, w_router))
    gate_probs = jax.nn.softmax(logits, axis=1)
    picked = (exp_seq[:, None] == jnp.arange(experts, dtype=jnp.int32)[None, :]).astype(jnp.int32)
    slot_rank = lax.optimization_barrier(jnp.sum((jnp.cumsum(picked, axis=0) - 1) * picked, axis=1))
    slot_index = (exp_seq * CAPACITY + slot_rank).astype(jnp.int32)
    token_gate = lax.optimization_barrier(jnp.sum(gate_probs * picked.astype(gate_probs.dtype), axis=1))
    slots_in = jnp.zeros((experts * CAPACITY, model_width), tok_seq.dtype).at[slot_index].set(normed_two)
    slots_in = slots_in.reshape(experts, CAPACITY, model_width)
    pre_act = low_back(jnp.einsum('ecd,def->ecf', slots_in, in_three, precision=lax.Precision.HIGHEST))
    hidden = low(jax.nn.gelu(pre_act))
    expert_rows = low_back(jnp.einsum('ecf,fed->ecd', hidden, out_three, precision=lax.Precision.HIGHEST))
    expert_rows = expert_rows.reshape(experts * CAPACITY, model_width)
    return residual + token_gate[:, None] * expert_rows[slot_index]

def reference(tokens, gain_one, gain_two, w_query, w_key, w_value, w_out, w_router, w_in, w_expert_out, bias_table, segment, expert, bucket, cotangent):
    floats = jax.tree.map(lambda member: member.astype(jnp.float32), (tokens, gain_one, gain_two, w_query, w_key, w_value, w_out, w_router, w_in, w_expert_out, bias_table))

    def whole_layer(tokens_f, gain_one_f, gain_two_f, query_f, key_f, value_f, out_f, router_f, in_f, expert_out_f, table_f):

        def one_seq(inputs_seq):
            tok_seq, doc_seq, exp_seq, buck_seq = inputs_seq
            result = sequence_layer(jnp.transpose(tok_seq), doc_seq, exp_seq, buck_seq, gain_one_f, gain_two_f, query_f, key_f, value_f, out_f, router_f, in_f, expert_out_f, table_f)
            return jnp.transpose(result)
        return lax.map(jax.checkpoint(one_seq), (tokens_f, segment, expert[:, :, 0], bucket))
    primal, pullback = jax.vjp(whole_layer, *floats)
    gradients = pullback(cotangent.astype(jnp.float32))
    return (primal.astype(jnp.bfloat16), gradients[0].astype(jnp.bfloat16), gradients[1], gradients[2], gradients[3], gradients[4], gradients[5], gradients[6], gradients[7], gradients[8], gradients[9], gradients[10])
```

```python
import functools

import jax
import jax.numpy as jnp
from jax import lax
from jax.experimental import pallas as pl
from jax.experimental.pallas import tpu as pltpu
from jax.sharding import PartitionSpec as P

EXPERTS = 32
CAPACITY = 48


NORM_EPS = 1e-06
NEG_FILL = -1e30


def row_totals(partial_values):
    return lax.psum(partial_values, "row")


def feature_split(partial_rows):
    return lax.psum_scatter(partial_rows, "row", scatter_dimension=1, tiled=True)


def feature_join(rows_low):
    return lax.all_gather(rows_low, "row", axis=1, tiled=True)


def norm_back(grad_normed, inputs_f, inverse_rms, gain_part, model_width):
    inner_sum = row_totals(jnp.sum(gain_part * grad_normed * inputs_f, axis=1))
    return (
        inverse_rms[:, None] * gain_part * grad_normed
        - inputs_f * (inverse_rms**3 / model_width * inner_sum)[:, None]
    )


def block_scores(
    query_heads, keys_all, bucket_rows, query_docs, doc_ids, bias_table, number, key_block
):
    head_count = bias_table.shape[1]
    head_dim = query_heads.shape[2]
    offset = number * key_block
    key_rows = lax.dynamic_slice_in_dim(keys_all, offset, key_block, 0).reshape(
        key_block, head_count, head_dim
    )
    bucket_cols = lax.dynamic_slice_in_dim(bucket_rows, offset, key_block, 1)
    key_docs = lax.dynamic_slice_in_dim(doc_ids, offset, key_block, 0)
    raw_scores = jnp.einsum(
        "ihd,jhd->hij", query_heads, key_rows, preferred_element_type=jnp.float32
    ) * head_dim ** (-0.5)
    one_hot = (bucket_cols[:, :, None] == jnp.arange(bias_table.shape[0], dtype=jnp.int32)).astype(
        jnp.float32
    )
    pair_bias = jnp.einsum("ijb,bh->hij", one_hot, bias_table, precision=lax.Precision.HIGHEST)
    allowed = (query_docs[:, None] == key_docs[None, :])[None]
    return (raw_scores + pair_bias, allowed, one_hot)


def attend_blocks(query_heads, keys_all, values_all, bucket_rows, query_docs, doc_ids, bias_table):
    tok_rows, head_count, head_dim = query_heads.shape
    seq_len = keys_all.shape[0]
    key_block = min(seq_len, 512)
    blocks = seq_len // key_block

    def first_pass(status, number):
        row_peak, row_total = status
        scores, allowed, one_hot = block_scores(
            query_heads, keys_all, bucket_rows, query_docs, doc_ids, bias_table, number, key_block
        )
        masked = jnp.where(allowed, scores, NEG_FILL)
        new_peak = jnp.maximum(row_peak, jnp.max(masked, axis=2))
        weights = jnp.where(allowed, jnp.exp(masked - new_peak[:, :, None]), 0.0)
        row_total = row_total * jnp.exp(row_peak - new_peak) + jnp.sum(weights, axis=2)
        return ((new_peak, row_total), None)

    start_status = (
        jnp.full((head_count, tok_rows), NEG_FILL, jnp.float32),
        jnp.zeros((head_count, tok_rows), jnp.float32),
    )
    (row_peak, row_total), unused = lax.scan(first_pass, start_status, jnp.arange(blocks))
    log_total = row_peak + jnp.log(row_total)

    def second_pass(running, number):
        scores, allowed, one_hot = block_scores(
            query_heads, keys_all, bucket_rows, query_docs, doc_ids, bias_table, number, key_block
        )
        soft_weights = jnp.where(allowed, jnp.exp(scores - log_total[:, :, None]), 0.0).astype(
            jnp.bfloat16
        )
        value_rows = lax.dynamic_slice_in_dim(values_all, number * key_block, key_block, 0).reshape(
            key_block, head_count, head_dim
        )
        return (
            running
            + jnp.einsum(
                "hij,jhd->ihd", soft_weights, value_rows, preferred_element_type=jnp.float32
            ),
            None,
        )

    start_acc = jnp.zeros((tok_rows, head_count, head_dim), jnp.float32)
    attended, unused = lax.scan(second_pass, start_acc, jnp.arange(blocks))
    return (attended, log_total)


def attend_blocks_back(
    query_heads,
    keys_all,
    values_all,
    bucket_rows,
    query_docs,
    doc_ids,
    bias_table,
    log_total,
    grad_heads,
    grad_dot,
):
    tok_rows, head_count, head_dim = query_heads.shape
    seq_len = keys_all.shape[0]
    model_width = head_count * head_dim
    key_block = min(seq_len, 512)
    blocks = seq_len // key_block
    scaling = head_dim ** (-0.5)

    def step_back(status, number):
        grad_query, grad_table = status
        scores, allowed, one_hot = block_scores(
            query_heads, keys_all, bucket_rows, query_docs, doc_ids, bias_table, number, key_block
        )
        key_rows = lax.dynamic_slice_in_dim(keys_all, number * key_block, key_block, 0).reshape(
            key_block, head_count, head_dim
        )
        value_rows = lax.dynamic_slice_in_dim(values_all, number * key_block, key_block, 0).reshape(
            key_block, head_count, head_dim
        )
        soft_weights = jnp.where(allowed, jnp.exp(scores - log_total[:, :, None]), 0.0)
        weights_low = soft_weights.astype(jnp.bfloat16)
        grad_soft = jnp.einsum(
            "ihd,jhd->hij", grad_heads, value_rows, preferred_element_type=jnp.float32
        )
        grad_scores = soft_weights * (grad_soft - grad_dot[:, :, None])
        grad_table = grad_table + jnp.einsum(
            "ijb,hij->bh", one_hot, grad_scores, precision=lax.Precision.HIGHEST
        )
        scores_low = grad_scores.astype(jnp.bfloat16)
        grad_query = grad_query + scaling * jnp.einsum(
            "hij,jhd->ihd", scores_low, key_rows, preferred_element_type=jnp.float32
        )
        grad_key = scaling * jnp.einsum(
            "hij,ihd->jhd", scores_low, query_heads, preferred_element_type=jnp.float32
        )
        grad_value = jnp.einsum(
            "hij,ihd->jhd", weights_low, grad_heads, preferred_element_type=jnp.float32
        )
        stacked = jnp.concatenate(
            [grad_key.reshape(key_block, model_width), grad_value.reshape(key_block, model_width)],
            axis=1,
        )
        return ((grad_query, grad_table), stacked)

    start_status = (
        jnp.zeros((tok_rows, head_count, head_dim), jnp.float32),
        jnp.zeros(bias_table.shape, jnp.float32),
    )
    (grad_query, grad_table), kv_terms = lax.scan(step_back, start_status, jnp.arange(blocks))
    return (grad_query, grad_table, kv_terms.reshape(seq_len, 2 * model_width))


def general_plan(
    tokens,
    gain_one,
    gain_two,
    w_query,
    w_key,
    w_value,
    w_out,
    w_router,
    w_in,
    w_expert_out,
    bias_table,
    segment,
    expert,
    bucket,
    cotangent,
):
    seq_len = tokens.shape[2]
    dim_rows = tokens.shape[1]
    row_count = lax.axis_size("row")
    model_width = dim_rows * row_count
    tok_rows = seq_len // row_count
    experts = EXPERTS
    hid_rows = w_expert_out.shape[0]
    ffn_width = hid_rows * row_count
    head_count = bias_table.shape[1]
    head_dim = model_width // head_count
    row_index = lax.axis_index("row")
    gathered = (
        lax.all_gather(w_query, "col", axis=1, tiled=True),
        lax.all_gather(w_key, "col", axis=1, tiled=True),
        lax.all_gather(w_value, "col", axis=1, tiled=True),
        lax.all_gather(w_out, "col", axis=1, tiled=True),
        lax.all_gather(w_router, "col", axis=1, tiled=True),
        lax.all_gather(w_in, "col", axis=1, tiled=True),
        lax.all_gather(w_expert_out, "col", axis=1, tiled=True),
    )
    query_full, key_full, value_full, out_proj_full, router_full, in_flat, out_flat = gathered
    in_full = in_flat.reshape(dim_rows, experts, ffn_width)
    out_full = out_flat.reshape(hid_rows, experts, model_width)
    stacked_weights = jnp.concatenate([query_full, key_full, value_full], axis=1)
    tok_float = jnp.transpose(tokens[0].astype(jnp.float32))
    doc_ids = segment[0]
    query_docs = lax.dynamic_slice_in_dim(doc_ids, row_index * tok_rows, tok_rows, 0)
    bucket_rows = bucket[0]
    expert_ids = expert[0, :, 0]
    gain_part_one = lax.dynamic_slice_in_dim(gain_one, row_index * dim_rows, dim_rows, 0)
    gain_part_two = lax.dynamic_slice_in_dim(gain_two, row_index * dim_rows, dim_rows, 0)
    inverse_one = lax.rsqrt(
        row_totals(jnp.sum(tok_float * tok_float, axis=1)) / model_width + NORM_EPS
    )
    normed_one = (tok_float * inverse_one[:, None] * gain_part_one).astype(jnp.bfloat16)
    projected = lax.psum_scatter(
        jnp.dot(normed_one, stacked_weights, preferred_element_type=jnp.float32),
        "row",
        scatter_dimension=0,
        tiled=True,
    ).astype(jnp.bfloat16)
    queries_low = projected[:, :model_width]
    keys_low = projected[:, model_width : 2 * model_width]
    values_low = projected[:, 2 * model_width :]
    keys_all, values_all = (
        lax.all_gather(keys_low, "row", axis=0, tiled=True),
        lax.all_gather(values_low, "row", axis=0, tiled=True),
    )
    query_heads = queries_low.reshape(tok_rows, head_count, head_dim)
    attended, log_total = attend_blocks(
        query_heads, keys_all, values_all, bucket_rows, query_docs, doc_ids, bias_table
    )
    attn_low = attended.reshape(tok_rows, model_width).astype(jnp.bfloat16)
    heads_home = lax.all_to_all(attn_low, "row", split_axis=1, concat_axis=0, tiled=True)
    attn_rows = feature_split(
        jnp.dot(heads_home, out_proj_full, preferred_element_type=jnp.float32)
    )
    residual = tok_float + attn_rows
    inverse_two = lax.rsqrt(
        row_totals(jnp.sum(residual * residual, axis=1)) / model_width + NORM_EPS
    )
    normed_two = (residual * inverse_two[:, None] * gain_part_two).astype(jnp.bfloat16)
    logits = row_totals(jnp.dot(normed_two, router_full, preferred_element_type=jnp.float32))
    gate_probs = jax.nn.softmax(logits, axis=1)
    picked = (expert_ids[:, None] == jnp.arange(experts, dtype=jnp.int32)[None, :]).astype(
        jnp.int32
    )
    picked_float = picked.astype(jnp.float32)
    slot_rank = jnp.sum((jnp.cumsum(picked, axis=0) - 1) * picked, axis=1)
    slot_index = expert_ids * CAPACITY + slot_rank
    token_gate = jnp.sum(gate_probs * picked_float, axis=1)
    slots_in = (
        jnp.zeros((experts * CAPACITY, dim_rows), jnp.bfloat16).at[slot_index].set(normed_two)
    )
    slots_own = slots_in.reshape(experts, CAPACITY, dim_rows)
    lead_count = slots_own.shape[0]
    slot_count = slots_own.shape[1]
    pre_partial = jnp.einsum("ecd,def->ecf", slots_own, in_full, preferred_element_type=jnp.float32)
    pre_act = feature_split(pre_partial.reshape(lead_count * slot_count, ffn_width))
    hidden = jax.nn.gelu(pre_act).astype(jnp.bfloat16)
    hidden_three = hidden.reshape(lead_count, slot_count, hid_rows)
    out_partial = jnp.einsum(
        "ecf,fed->ecd", hidden_three, out_full, preferred_element_type=jnp.float32
    )
    expert_local = feature_split(out_partial.reshape(lead_count * slot_count, model_width))
    expert_tok = expert_local[slot_index]
    layer_out = (residual + token_gate[:, None] * expert_tok).astype(jnp.bfloat16)
    grad_final = jnp.transpose(cotangent[0].astype(jnp.float32))
    grad_gate = row_totals(jnp.sum(grad_final * expert_tok, axis=1))
    grad_expert_tok = (token_gate[:, None] * grad_final).astype(jnp.bfloat16)
    grad_slots = (
        jnp.zeros((experts * CAPACITY, dim_rows), jnp.bfloat16).at[slot_index].set(grad_expert_tok)
    )
    grad_slots_local = grad_slots.reshape(experts, CAPACITY, dim_rows)
    grad_slots_full = feature_join(
        grad_slots_local.reshape(lead_count * slot_count, dim_rows)
    ).reshape(lead_count, slot_count, model_width)
    grad_hidden = jnp.einsum(
        "ecd,fed->ecf", grad_slots_full, out_full, preferred_element_type=jnp.float32
    )
    grad_out_weight = jnp.einsum(
        "ecf,ecd->fed", hidden_three, grad_slots_full, preferred_element_type=jnp.float32
    )
    unused, gelu_back = jax.vjp(jax.nn.gelu, pre_act)
    grad_pre = gelu_back(grad_hidden.reshape(lead_count * slot_count, hid_rows))[0].astype(
        jnp.bfloat16
    )
    grad_pre_full = feature_join(grad_pre).reshape(lead_count, slot_count, ffn_width)
    grad_slots_in = jnp.einsum(
        "ecf,def->ecd", grad_pre_full, in_full, preferred_element_type=jnp.float32
    )
    grad_in_weight = jnp.einsum(
        "ecd,ecf->def", slots_own, grad_pre_full, preferred_element_type=jnp.float32
    )
    grad_logits = ((grad_gate * token_gate)[:, None] * (picked_float - gate_probs)).astype(
        jnp.bfloat16
    )
    router_back = lax.dot_general(
        grad_logits, router_full, (((1,), (1,)), ((), ())), preferred_element_type=jnp.float32
    )
    grad_normed_two = grad_slots_in.reshape(experts * CAPACITY, dim_rows)[slot_index] + router_back
    grad_router = lax.dot_general(
        normed_two, grad_logits, (((0,), (0,)), ((), ())), preferred_element_type=jnp.float32
    )
    grad_res = grad_final + norm_back(
        grad_normed_two, residual, inverse_two, gain_part_two, model_width
    )
    grad_gain_two = jnp.sum(grad_normed_two * residual * inverse_two[:, None], axis=0)
    grad_attn_full = feature_join(grad_res.astype(jnp.bfloat16))
    grad_heads_home = lax.dot_general(
        grad_attn_full, out_proj_full, (((1,), (1,)), ((), ())), preferred_element_type=jnp.float32
    ).astype(jnp.bfloat16)
    grad_out_proj = lax.dot_general(
        heads_home, grad_attn_full, (((0,), (0,)), ((), ())), preferred_element_type=jnp.float32
    )
    grad_attn = lax.all_to_all(grad_heads_home, "row", split_axis=0, concat_axis=1, tiled=True)
    grad_heads = grad_attn.reshape(tok_rows, head_count, head_dim)
    grad_dot = jnp.einsum("ihd,ihd->hi", grad_heads.astype(jnp.float32), attended)
    grad_query, grad_table, kv_terms = attend_blocks_back(
        query_heads,
        keys_all,
        values_all,
        bucket_rows,
        query_docs,
        doc_ids,
        bias_table,
        log_total,
        grad_heads,
        grad_dot,
    )
    key_value_grads = lax.psum_scatter(kv_terms, "row", scatter_dimension=0, tiled=True)
    grad_qkv = jnp.concatenate(
        [
            grad_query.reshape(tok_rows, model_width).astype(jnp.bfloat16),
            key_value_grads.astype(jnp.bfloat16),
        ],
        axis=1,
    )
    portion = lax.all_gather(grad_qkv, "row", axis=0, tiled=True)
    grad_part = lax.dot_general(
        portion, stacked_weights, (((1,), (1,)), ((), ())), preferred_element_type=jnp.float32
    )
    grad_weights = lax.dot_general(
        normed_one, portion, (((0,), (0,)), ((), ())), preferred_element_type=jnp.float32
    )
    grad_input = grad_res + norm_back(grad_part, tok_float, inverse_one, gain_part_one, model_width)
    grad_gain_one = jnp.sum(grad_part * tok_float * inverse_one[:, None], axis=0)
    summed = (
        lax.psum_scatter(grad_weights[:, :model_width], "col", scatter_dimension=1, tiled=True),
        lax.psum_scatter(
            grad_weights[:, model_width : 2 * model_width], "col", scatter_dimension=1, tiled=True
        ),
        lax.psum_scatter(
            grad_weights[:, 2 * model_width :], "col", scatter_dimension=1, tiled=True
        ),
        lax.psum_scatter(grad_out_proj, "col", scatter_dimension=1, tiled=True),
        lax.psum_scatter(grad_router, "col", scatter_dimension=1, tiled=True),
        lax.psum_scatter(
            grad_in_weight.reshape(dim_rows, experts * ffn_width),
            "col",
            scatter_dimension=1,
            tiled=True,
        ),
        lax.psum_scatter(
            grad_out_weight.reshape(hid_rows, experts * model_width),
            "col",
            scatter_dimension=1,
            tiled=True,
        ),
    )
    grad_query_w, grad_key_w, grad_value_w, grad_out_w, grad_router_w, grad_in_w, grad_expert_w = (
        summed
    )
    place_one = lax.dynamic_update_slice_in_dim(
        jnp.zeros((model_width,), jnp.float32), grad_gain_one, row_index * dim_rows, 0
    )
    place_two = lax.dynamic_update_slice_in_dim(
        jnp.zeros((model_width,), jnp.float32), grad_gain_two, row_index * dim_rows, 0
    )
    gain_one_grad, gain_two_grad, table_grad = lax.psum(
        (place_one, place_two, grad_table), ("row", "col")
    )
    layer_out_t = jnp.transpose(layer_out)[None]
    grad_input_t = jnp.transpose(grad_input.astype(jnp.bfloat16))[None]
    return (
        layer_out_t,
        grad_input_t,
        gain_one_grad,
        gain_two_grad,
        grad_query_w,
        grad_key_w,
        grad_value_w,
        grad_out_w,
        grad_router_w,
        grad_in_w,
        grad_expert_w,
        table_grad,
    )


BF16 = jnp.bfloat16
F32 = jnp.float32
I32 = jnp.int32
NT = (((1,), (1,)), ((), ()))
NN = (((1,), (0,)), ((), ()))
TN = (((0,), (0,)), ((), ()))
LANES = 128
PAIR_ROWS = 16
LOW_BINS = 8
GELU_SCALE = 0.7978845608028654
GELU_CUBE = 0.044715
QUICK = pl.CostEstimate(flops=0, bytes_accessed=0, transcendentals=0)


def mm(left, right, dims):
    return lax.dot_general(left, right, dims, preferred_element_type=F32)


def two_parts(values):
    high = values.astype(BF16)
    return high, (values - high.astype(F32)).astype(BF16)


def attend_kernel(heads, head_dim, q_ref, k_ref, v_ref, idx_ref, tab_ref, o_ref, p_ref):
    rows, keys = idx_ref.shape
    idx = idx_ref[...].astype(F32).astype(I32)
    for h in range(heads):
        span = slice(h * head_dim, (h + 1) * head_dim)
        table = jnp.broadcast_to(tab_ref[h : h + 1, :], (rows, LANES))
        bias = jnp.concatenate(
            [
                jnp.take_along_axis(table, idx[:, c : c + LANES], axis=1)
                for c in range(0, keys, LANES)
            ],
            axis=1,
        )
        scores = mm(q_ref[span, :], k_ref[span, :], TN) * head_dim**-0.5 + bias
        weights = jnp.exp(scores - jnp.max(scores, axis=1, keepdims=True))
        soft = (weights * (1.0 / jnp.sum(weights, axis=1, keepdims=True))).astype(BF16)
        p_ref[h] = soft
        o_ref[span, :] = mm(v_ref[span, :], soft, NT)


def attend(q, k, v, idx, tab, heads, tile):
    width, keys = q.shape
    whole = lambda a: pl.BlockSpec(a.shape, lambda i: (0, 0))
    return pl.pallas_call(
        functools.partial(attend_kernel, heads, width // heads),
        grid=(keys // tile,),
        in_specs=[
            pl.BlockSpec((width, tile), lambda i: (0, i)),
            whole(k),
            whole(v),
            pl.BlockSpec((tile, keys), lambda i: (i, 0)),
            whole(tab),
        ],
        out_specs=[
            pl.BlockSpec((width, tile), lambda i: (0, i)),
            pl.BlockSpec((heads, tile, keys), lambda i: (0, i, 0)),
        ],
        out_shape=[
            jax.ShapeDtypeStruct((width, keys), F32),
            jax.ShapeDtypeStruct((heads, keys, keys), BF16),
        ],
        compiler_params=pltpu.CompilerParams(vmem_limit_bytes=48 * 2**20),
        cost_estimate=QUICK,
    )(q, k, v, idx, tab)


def back_kernel(
    heads,
    count,
    experts,
    cols,
    place_ref,
    q_ref,
    k_ref,
    v_ref,
    idx_ref,
    p_ref,
    o_ref,
    slot_ref,
    h1_ref,
    row_ref,
    col_ref,
    x_ref,
    n1_ref,
    ofull_ref,
    w_ref,
    gain_two_ref,
    *refs,
):
    pieces = refs[:count]
    layer_ref, da_ref, proj_ref = refs[count : count + 3]
    dn1_refs = refs[count + 3 : 2 * count + 3]
    g_aug, v_aug, dqkv, dk_acc, dv_acc, hist, router_acc, dn1_acc = refs[2 * count + 3 :]
    step, steps = pl.program_id(0), pl.num_programs(0)
    me = place_ref[0]
    part, tile = q_ref.shape
    keys = k_ref.shape[1]
    head_dim = part // heads
    aug = g_aug.shape[0] // heads
    width = x_ref.shape[0]
    slots = pieces[0].shape[0]
    scale = head_dim**-0.5

    @pl.when(step == 0)
    def _():
        dk_acc[...] = jnp.zeros_like(dk_acc)
        dv_acc[...] = jnp.zeros_like(dv_acc)
        hist[...] = jnp.zeros_like(hist)
        placed = jnp.zeros((3 * part, keys), F32)
        router = jnp.zeros((part, 2 * experts), F32)
        slot_row = lax.broadcasted_iota(I32, (slots, keys), 0)
        for k in range(count):
            spread = jnp.where(slot_row + (me ^ k) * slots == slot_ref[...], 1.0, 0.0).astype(BF16)
            placed = placed + mm(pieces[k][:, : 3 * part], spread, TN)
            router = router + pieces[k][:part, 3 * part :].astype(F32)
        router_acc[...] = router[:, :experts] + router[:, experts:]
        layer_ref[...] = (h1_ref[...] + row_ref[1:2, :] * placed[:part]).astype(BF16)
        da_ref[...] = placed[part : 2 * part].astype(BF16)
        fill = jnp.zeros((PAIR_ROWS - 2, keys), F32)
        ones = jnp.concatenate([jnp.ones((2, keys), F32), fill], axis=0).astype(BF16)
        for h in range(heads):
            span = slice(h * head_dim, (h + 1) * head_dim)
            do = placed[2 * part + h * head_dim : 2 * part + (h + 1) * head_dim]
            delta = jnp.sum(do * o_ref[span, :], axis=0, keepdims=True)
            high = delta.astype(BF16).astype(F32)
            rest = jnp.concatenate([-high, high - delta, fill], axis=0).astype(BF16)
            g_aug[h * aug : h * aug + head_dim, :] = do.astype(BF16)
            g_aug[h * aug + head_dim : (h + 1) * aug, :] = rest
            v_aug[h * aug : h * aug + head_dim, :] = v_ref[span, :]
            v_aug[h * aug + head_dim : (h + 1) * aug, :] = ones

    lanes = pl.ds(pl.multiple_of(step * tile, tile), tile)
    slopes = []
    for h in range(heads):
        span = slice(h * head_dim, (h + 1) * head_dim)
        soft = p_ref[h]
        g_part = g_aug[h * aug : (h + 1) * aug, lanes]
        diff = mm(g_part, v_aug[h * aug : (h + 1) * aug, :], TN)
        slope = (soft.astype(F32) * diff).astype(BF16)
        slopes.append(slope)
        dqkv[span, lanes] = (mm(k_ref[span, :], slope, NT) * scale).astype(BF16)
        dk_acc[span, :] += mm(q_ref[span, :], slope, NN) * scale
        dv_acc[span, :] += mm(g_part[:head_dim], soft, NN)
    idx = idx_ref[...].astype(F32).astype(I32)
    high = (idx // LOW_BINS).astype(F32).astype(BF16)
    low = (idx % LOW_BINS).astype(F32).astype(BF16)
    high_bins = hist.shape[1] // (heads * PAIR_ROWS)
    one = jnp.ones((), BF16)
    zero = jnp.zeros((), BF16)
    total = hist[...]
    for s in range(0, tile, PAIR_ROWS):
        rows = slice(s, s + PAIR_ROWS)
        left = jnp.concatenate(
            [jnp.where(low[rows] == n, one, zero) for n in range(LOW_BINS)], axis=0
        )
        right = jnp.concatenate(
            [
                jnp.where(high[rows] == n, slopes[h][rows], zero)
                for h in range(heads)
                for n in range(high_bins)
            ],
            axis=0,
        )
        total = total + mm(left, right, NT)
    hist[...] = total

    @pl.when(step == steps - 1)
    def _():
        dqkv[part : 2 * part, :] = dk_acc[...].astype(BF16)
        dqkv[2 * part :, :] = dv_acc[...].astype(BF16)
        r1 = row_ref[0:1, :]
        inner = jnp.zeros((1, keys), F32)
        gain_rows = []
        for d in range(count):
            rows = slice(d * part, (d + 1) * part)
            dn1 = mm(w_ref[rows, :], dqkv[...], NN)
            dn1_acc[d] = dn1.astype(BF16)
            dn1_x = dn1 * x_ref[rows, :].astype(F32)
            inner = inner + jnp.sum(dn1_x * col_ref[rows, :], axis=0, keepdims=True)
            gain_rows.append(
                lax.dot_general(
                    jnp.broadcast_to(r1, (8, keys)),
                    dn1_x,
                    NT,
                    precision=lax.Precision.HIGHEST,
                    preferred_element_type=F32,
                )[:1]
            )
        cells = hist[...]
        same = lax.broadcasted_iota(I32, cells.shape, 0) % PAIR_ROWS == (
            lax.broadcasted_iota(I32, cells.shape, 1) % PAIR_ROWS
        )
        cells = jnp.where(same, cells, 0.0)
        low_rows = (LOW_BINS, cells.shape[0])
        sum_rows = jnp.where(
            lax.broadcasted_iota(I32, low_rows, 1) // PAIR_ROWS
            == lax.broadcasted_iota(I32, low_rows, 0),
            1.0,
            0.0,
        )
        lane_cols = (cells.shape[1], LANES)
        bins = heads * high_bins
        sum_cols = jnp.where(
            lax.broadcasted_iota(I32, lane_cols, 0) // PAIR_ROWS + me * bins
            == lax.broadcasted_iota(I32, lane_cols, 1),
            1.0,
            0.0,
        )
        exact = functools.partial(
            lax.dot_general,
            dimension_numbers=NN,
            precision=lax.Precision.HIGHEST,
            preferred_element_type=F32,
        )
        table = exact(exact(sum_rows, cells), sum_cols)
        table_row = jnp.concatenate([table[n : n + 1] for n in range(LOW_BINS)], axis=1)
        pad = jnp.zeros((1, keys - width), F32)
        gain_row = jnp.concatenate(gain_rows + [pad], axis=1)
        gain_two_row = jnp.concatenate([gain_two_ref[...], pad], axis=1)
        extra = jnp.concatenate([inner, gain_row, gain_two_row, table_row], axis=0)
        extra_high = extra.astype(BF16).astype(F32)
        extra = jnp.concatenate(
            [extra_high, extra - extra_high, jnp.zeros((PAIR_ROWS - 8, keys), F32)], axis=0
        ).astype(BF16)
        for k in range(count):
            dn1_refs[k][:part, :] = dn1_acc[me ^ k]
            dn1_refs[k][part:, :] = extra
        router = jnp.transpose(router_acc[...])
        router_high = router.astype(BF16).astype(F32)
        router_low = router - router_high
        band = width // cols
        share = experts // cols
        blank = jnp.zeros((PAIR_ROWS - 2 * share, width), F32)
        pad = jnp.zeros((share, width - part), F32)
        dqkv_all, da_all = dqkv[...], da_ref[...]
        for c in range(cols):
            rows = slice(c * band, (c + 1) * band)
            proj_ref[c, :band, : 3 * part] = mm(n1_ref[rows, :], dqkv_all, NT).astype(BF16)
            proj_ref[c, :band, 3 * part :] = mm(ofull_ref[rows, :], da_all, NT).astype(BF16)
            own = slice(c * share, (c + 1) * share)
            proj_ref[c, band:, :] = jnp.concatenate(
                [
                    jnp.concatenate([router_high[own], pad], axis=1),
                    jnp.concatenate([router_low[own], pad], axis=1),
                    blank,
                ],
                axis=0,
            ).astype(BF16)


def attend_back(
    place, q, k, v, idx, p, o, slot, h1, row_facts, gain, x, n1, o_full, w, gain_two, pieces, cols, buckets, tile
):
    part, keys = q.shape
    width = x.shape[0]
    count = len(pieces)
    heads = p.shape[0]
    experts = (pieces[0].shape[1] - 3 * part) // 2
    aug_width = part + heads * PAIR_ROWS
    hist_shape = (LOW_BINS * PAIR_ROWS, heads * (buckets // LOW_BINS) * PAIR_ROWS)
    fixed = lambda a: pl.BlockSpec(a.shape, lambda i, m: (0,) * len(a.shape))
    outs = [
        jax.ShapeDtypeStruct((part, keys), BF16),
        jax.ShapeDtypeStruct((part, keys), BF16),
        jax.ShapeDtypeStruct((cols, width // cols + PAIR_ROWS, width), BF16),
    ] + [jax.ShapeDtypeStruct((part + PAIR_ROWS, keys), BF16)] * count
    rest = (o, slot, h1, row_facts, gain, x, n1, o_full, w, gain_two, *pieces)
    out = pl.pallas_call(
        functools.partial(back_kernel, heads, count, experts, cols),
        grid_spec=pltpu.PrefetchScalarGridSpec(
            num_scalar_prefetch=1,
            grid=(keys // tile,),
            in_specs=[
                pl.BlockSpec((part, tile), lambda i, m: (0, i)),
                fixed(k),
                fixed(v),
                pl.BlockSpec((tile, keys), lambda i, m: (i, 0)),
                pl.BlockSpec((heads, tile, keys), lambda i, m: (0, i, 0)),
            ]
            + [fixed(a) for a in rest],
            out_specs=[fixed(a) for a in outs],
            scratch_shapes=[
                pltpu.VMEM((aug_width, keys), BF16),
                pltpu.VMEM((aug_width, keys), BF16),
                pltpu.VMEM((3 * part, keys), BF16),
                pltpu.VMEM((part, keys), F32),
                pltpu.VMEM((part, keys), F32),
                pltpu.VMEM(hist_shape, F32),
                pltpu.VMEM((part, experts), F32),
                pltpu.VMEM((count, part, keys), BF16),
            ],
        ),
        out_shape=outs,
        compiler_params=pltpu.CompilerParams(vmem_limit_bytes=56 * 2**20),
        cost_estimate=QUICK,
    )(place, q, k, v, idx, p, *rest)
    return out[0], out[1], out[2], out[3:]


def expert_kernel(count, place_ref, x_ref, dy_ref, router_ref, *refs):
    in_refs, eout_refs = refs[:count], refs[count : 2 * count]
    back_ref = refs[2 * count]
    gi_refs = refs[2 * count + 1 : 3 * count + 1]
    ge_refs = refs[3 * count + 1 : 4 * count + 1]
    win, eout, dys, y_acc, dx_acc, gi = refs[4 * count + 1 :]
    step = pl.program_id(0)
    me = place_ref[0]
    part = in_refs[0].shape[0]

    @pl.when(step == 0)
    def _():
        logits = mm(x_ref[...], router_ref[...], NN)
        probs = jnp.exp(logits - jnp.max(logits, axis=1, keepdims=True))
        own = lax.broadcasted_iota(I32, logits.shape, 1) == place_ref[1]
        gate = jnp.sum(jnp.where(own, probs, 0.0), axis=1, keepdims=True)
        gate = gate / jnp.sum(probs, axis=1, keepdims=True)
        dys[...] = (gate * dy_ref[...].astype(F32)).astype(BF16)
        y_acc[...] = jnp.zeros_like(y_acc)
        dx_acc[...] = jnp.zeros_like(dx_acc)

    for k in range(count):
        win[pl.ds(pl.multiple_of((me ^ k) * part, part), part), :] = in_refs[k][...]

        @pl.when(step == k)
        def _(k=k):
            eout[...] = eout_refs[k][...]

    pre = mm(x_ref[...], win[...], NN)
    square = pre * pre
    curve = jnp.tanh(GELU_SCALE * pre * (1.0 + GELU_CUBE * square))
    half = 0.5 * (1.0 + curve)
    hidden = (pre * half).astype(BF16)
    slope = half + 0.5 * pre * (1.0 - curve * curve) * (
        GELU_SCALE * (1.0 + 3.0 * GELU_CUBE * square)
    )
    dpre = (mm(dys[...], eout[...], NT) * slope).astype(BF16)
    y_acc[...] += mm(hidden, eout[...], NN)
    dx_acc[...] += mm(dpre, win[...], NT)
    ge = mm(hidden, dys[...], TN).astype(BF16)
    gi[...] = mm(x_ref[...], dpre, TN).astype(BF16)
    for k in range(count):
        gi_refs[k][...] = gi[pl.ds(pl.multiple_of((me ^ k) * part, part), part), :]

        @pl.when(step == k)
        def _(k=k):
            ge_refs[k][...] = ge

    @pl.when(step == count - 1)
    def _():
        width = y_acc.shape[1]
        back_ref[:, :width] = y_acc[...].astype(BF16)
        back_ref[:, width:] = dx_acc[...].astype(BF16)


def expert_work(place, x, dy, router, in_held, eout_held):
    count = len(in_held)
    slots, width = x.shape
    part, hidden_width = in_held[0].shape
    chunk = hidden_width // count
    fixed = lambda a: pl.BlockSpec(a.shape, lambda i, m: (0, 0))
    lanes = pl.BlockSpec((part, chunk), lambda i, m: (0, m[0] ^ i))
    shape = lambda s: jax.ShapeDtypeStruct(s, BF16)
    out = pl.pallas_call(
        functools.partial(expert_kernel, count),
        grid_spec=pltpu.PrefetchScalarGridSpec(
            num_scalar_prefetch=1,
            grid=(count,),
            in_specs=[fixed(x), fixed(dy), fixed(router)]
            + [lanes] * count
            + [fixed(eout_held[0])] * count,
            out_specs=[pl.BlockSpec((slots, 2 * width), lambda i, m: (0, 0))] + [lanes] * count + [fixed(eout_held[0])] * count,
            scratch_shapes=[
                pltpu.VMEM((width, chunk), BF16),
                pltpu.VMEM((chunk, width), BF16),
                pltpu.VMEM((slots, width), BF16),
                pltpu.VMEM((slots, width), F32),
                pltpu.VMEM((slots, width), F32),
                pltpu.VMEM((width, chunk), BF16),
            ],
        ),
        out_shape=[shape((slots, 2 * width))]
        + [shape((part, hidden_width))] * count
        + [shape((chunk, width))] * count,
        compiler_params=pltpu.CompilerParams(vmem_limit_bytes=56 * 2**20),
        cost_estimate=QUICK,
    )(place, x, dy, router, *in_held, *eout_held)
    return out[0], out[1 : 1 + count], out[1 + count :]


def slot_kernel(
    count,
    experts,
    place_ref,
    home_ref,
    dy_ref,
    n2_ref,
    h1_ref,
    scalar_ref,
    router_ref,
    out_ref,
    gain_ref,
    parcel_ref,
    gain_part_ref,
):
    me = place_ref[0]
    slots, width = dy_ref.shape
    part = width // count
    y = home_ref[:, :width]
    dy = dy_ref[...].astype(F32)
    h1 = h1_ref[...].astype(F32)
    scalars = scalar_ref[...]
    probs, gate, r2 = scalars[:, :experts], scalars[:, experts : experts + 1], scalars[:, experts + 1 :]
    dgate = jnp.sum(dy * y.astype(F32), axis=1, keepdims=True)
    row = lax.broadcasted_iota(I32, (slots, experts), 0)
    lane = lax.broadcasted_iota(I32, (slots, experts), 1)
    hot = jnp.where(row // CAPACITY * count + me == lane, 1.0, 0.0)
    dlogits = ((dgate * gate) * (hot - probs)).astype(BF16)
    dn2 = home_ref[:, width:].astype(F32) + mm(dlogits, router_ref[...], NT)
    scaled = dn2 * gain_ref[...]
    inner = jnp.sum(scaled * h1, axis=1, keepdims=True)
    dh1 = dy + r2 * scaled - h1 * (r2 * r2 * r2 * (1.0 / width) * inner)
    gain_part_ref[...] = jnp.sum(dn2 * h1 * r2, axis=0, keepdims=True)
    da = dh1.astype(BF16)
    do = mm(da, out_ref[...], NT).astype(BF16)
    router_high, router_low = two_parts(mm(n2_ref[...], dlogits, TN))
    fill = jnp.zeros((slots - part, 2 * experts), BF16)
    for d in range(count):
        span = slice(d * part, (d + 1) * part)
        router = jnp.concatenate([router_high[span], router_low[span]], axis=1)
        router = jnp.concatenate([router, fill], axis=0)
        parcel_ref[me ^ d] = jnp.concatenate(
            [y[:, span], da[:, span], do[:, span], router], axis=1
        )


def slot_work(place, home, dy, n2, h1, scalars, router, out_proj, gain, count):
    slots, width = dy.shape
    experts = router.shape[1]
    lanes = 3 * width // count + 2 * experts
    fixed = lambda a: pl.BlockSpec(a.shape, lambda i, m: (0,) * len(a.shape))
    ins = (home, dy, n2, h1, scalars, router, out_proj, gain)
    outs = [
        jax.ShapeDtypeStruct((count, slots, lanes), BF16),
        jax.ShapeDtypeStruct((1, width), F32),
    ]
    return pl.pallas_call(
        functools.partial(slot_kernel, count, experts),
        grid_spec=pltpu.PrefetchScalarGridSpec(
            num_scalar_prefetch=1,
            grid=(1,),
            in_specs=[fixed(a) for a in ins],
            out_specs=[fixed(a) for a in outs],
        ),
        out_shape=outs,
        compiler_params=pltpu.CompilerParams(vmem_limit_bytes=48 * 2**20),
        cost_estimate=QUICK,
    )(place, *ins)


def row_gather(block):
    me = lax.axis_index("row")
    count = lax.axis_size("row")
    far = lax.ppermute(block, "row", [(i, i ^ 2) for i in range(count)])
    near = lax.ppermute(jnp.stack([block, far]), "row", [(i, i ^ 1) for i in range(count)])
    held = jnp.stack([block, near[0], far, near[1]])
    return jnp.concatenate(
        [lax.dynamic_index_in_dim(held, p ^ me, 0, keepdims=True) for p in range(count)]
    )


def swap(blocks, axis):
    return lax.all_to_all(blocks, axis, 0, 0)


def col_gather(block):
    count = lax.axis_size("col")
    return swap(jnp.broadcast_to(block[None], (count,) + block.shape), "col")


def trade(piece_for):
    me = lax.axis_index("row")
    count = lax.axis_size("row")
    away = [k for k in (2, 3, 1)]
    held = {
        k: lax.ppermute(piece_for(me ^ k), "row", [(i, i ^ k) for i in range(count)]) for k in away
    }
    return [piece_for(me)] + [held[k] for k in range(1, count)]


def trade_pieces(pieces):
    count = len(pieces)
    held = {
        k: lax.ppermute(pieces[k], "row", [(i, i ^ k) for i in range(count)]) for k in (2, 3, 1)
    }
    return [pieces[0]] + [held[k] for k in range(1, count)]


def lay(held):
    me = lax.axis_index("row")
    out = jnp.zeros((len(held),) + held[0].shape, held[0].dtype)
    for k, piece in enumerate(held):
        out = lax.dynamic_update_slice_in_dim(out, piece[None], me ^ k, 0)
    return out


def after(value, *earlier):
    return lax.optimization_barrier((value,) + earlier)[0]


def fill_kernel(count, me_ref, *refs):
    step = pl.program_id(1)
    for k in range(count):

        @pl.when(step == k)
        def _(k=k):
            refs[count][...] = refs[k][...].astype(F32)


def fill_columns(held, splits):
    count = len(held)
    height, width = held[0].shape
    block = height // splits
    me = lax.axis_index("row").astype(I32).reshape(1)
    return pl.pallas_call(
        functools.partial(fill_kernel, count),
        grid_spec=pltpu.PrefetchScalarGridSpec(
            num_scalar_prefetch=1,
            grid=(splits, count),
            in_specs=[pl.BlockSpec((block, width), lambda i, k, m: (i, 0))] * count,
            out_specs=pl.BlockSpec((block, width), lambda i, k, m: (i, m[0] ^ k)),
        ),
        out_shape=jax.ShapeDtypeStruct((height, count * width), F32),
        compiler_params=pltpu.CompilerParams(vmem_limit_bytes=48 * 2**20),
        cost_estimate=QUICK,
    )(me, *held)


def own_rows(array, me, count):
    return lax.dynamic_slice_in_dim(array, me * count, count, 0)


def expert_plan(
    tokens,
    gain_one,
    gain_two,
    w_query,
    w_key,
    w_value,
    w_out,
    w_router,
    w_in,
    w_expert_out,
    bias_table,
    segment,
    expert,
    bucket,
    cotangent,
):
    rows, cols = lax.axis_size("row"), lax.axis_size("col")
    me, col = lax.axis_index("row"), lax.axis_index("col")
    part, seq_len = tokens.shape[1:]
    width = part * rows
    tok_rows = seq_len // rows
    buckets, all_heads = bias_table.shape
    heads = all_heads // rows
    head_dim = width // all_heads
    experts = w_router.shape[1] * cols
    hidden_width = w_expert_out.shape[0] * rows
    slots = (experts // rows) * CAPACITY
    out_cols = w_query.shape[1]
    share = cols // rows

    doc_ids = segment[0]
    expert_ids = expert[0, :, 0]

    tok_low = row_gather(tokens[0]).reshape(width, seq_len)
    qkv_part = jnp.concatenate([w_query, w_key, w_value], axis=1)
    qkv_cols = col_gather(qkv_part)
    qkv_cols = qkv_cols.reshape(rows, share, part, 3 * out_cols)
    qkv_rows = lay(trade(lambda d: lax.dynamic_index_in_dim(qkv_cols, d, 0, keepdims=False)))
    qkv_own = jnp.transpose(
        qkv_rows.reshape(rows, share, part, 3, out_cols), (0, 2, 3, 1, 4)
    ).reshape(width, 3 * part)
    same_doc = own_rows(doc_ids, me, tok_rows)[:, None] == doc_ids[None, :]
    masked = jnp.where(same_doc, bucket[0], buckets).astype(BF16)
    idx = row_gather(masked).reshape(seq_len, seq_len)
    low_cols = col_gather(after(jnp.concatenate([w_out, w_router], axis=1), qkv_cols))
    out_rows = jnp.transpose(low_cols[:, :, :out_cols], (1, 0, 2)).reshape(part, width)
    router_rows = jnp.transpose(low_cols[:, :, out_cols:], (1, 0, 2)).reshape(part, experts)
    out_router = row_gather(jnp.concatenate([out_rows, router_rows], axis=1)).reshape(
        width, width + experts
    )
    out_full, router_full = out_router[:, :width], out_router[:, width:]
    cot_low = row_gather(after(cotangent[0], qkv_rows, idx)).reshape(width, seq_len)
    lane_cut = lambda array, count: lambda d: lax.dynamic_slice_in_dim(array, d * count, count, 1)
    w_in = after(w_in, qkv_rows)
    in_held = trade(lane_cut(w_in, hidden_width))

    picked = expert_ids[None, :] == jnp.arange(experts, dtype=I32)[:, None]
    picked_float = picked.astype(F32)
    steps = jnp.arange(seq_len, dtype=I32)
    upper = (steps[:, None] <= steps[None, :]).astype(BF16)
    ranks = mm(picked.astype(BF16), upper, NN) - 1.0
    slot_rank = jnp.sum(ranks * picked_float, axis=0).astype(I32)
    slot = (expert_ids % rows) * slots + (expert_ids // rows) * CAPACITY + slot_rank
    choose = (jnp.arange(slots, dtype=I32)[:, None] + me * slots == slot[None, :]).astype(BF16)

    x = tok_low.astype(F32)
    r1 = lax.rsqrt(jnp.mean(x * x, axis=0) + NORM_EPS)
    n1 = (x * r1 * gain_one[:, None]).astype(BF16)
    qkv = mm(qkv_own, n1, TN).astype(BF16)
    q, k, v = qkv[:part], qkv[part : 2 * part], qkv[2 * part :]
    table = lax.dynamic_slice_in_dim(jnp.transpose(bias_table), me * heads, heads, 0)
    table = jnp.pad(
        table, ((0, 8 - heads), (0, LANES - buckets)), constant_values=NEG_FILL
    )
    o32, p = attend(q, k, v, idx, table, heads, 128)
    o_full = row_gather(o32.astype(BF16)).reshape(width, seq_len)
    w_expert_out = after(w_expert_out, o_full)
    eout_held = trade(lane_cut(w_expert_out, width))
    h1 = x + mm(out_full, o_full, TN)
    r2 = lax.rsqrt(jnp.mean(h1 * h1, axis=0) + NORM_EPS)
    n2 = (h1 * r2 * gain_two[:, None]).astype(BF16)
    logits = mm(router_full, n2, TN)
    g = jax.nn.softmax(logits, axis=0)
    gate = jnp.sum(g * picked_float, axis=0)

    expert_at = lambda a: swap(a.reshape(cols, CAPACITY, width), "col").reshape(slots, width)
    dy_low = mm(choose, cot_low, NT).astype(BF16)
    dy_slots = expert_at(dy_low)
    n2_low = mm(choose, n2, NT).astype(BF16)
    slots_in = expert_at(n2_low)
    place = jnp.stack([me, col * rows + me]).astype(I32)
    back, in_pieces, eout_pieces = expert_work(
        place, slots_in, dy_slots, router_full, in_held, eout_held
    )
    grad_eout_held = trade_pieces(eout_pieces)
    home = swap(back.reshape(cols, CAPACITY, 2 * width), "col").reshape(slots, 2 * width)

    h1_s = mm(choose, h1.astype(BF16), NT).astype(BF16)
    scalars = lax.dot_general(
        choose.astype(F32),
        jnp.concatenate([g, gate[None], r2[None]], axis=0),
        NT,
        precision=lax.Precision.HIGHEST,
        preferred_element_type=F32,
    )
    parcel, gain_two_part = slot_work(
        place, home, dy_low, n2_low, h1_s, scalars, router_full, out_full, gain_two[None], rows
    )
    parcel = trade_pieces([parcel[k] for k in range(rows)])
    grad_in_held = trade_pieces([after(piece, parcel[2]) for piece in in_pieces])

    layer_out, da, proj_parcel, dn1_parcel = attend_back(
        place,
        q,
        k,
        v,
        idx,
        p,
        o32,
        slot[None],
        own_rows(h1, me, part),
        jnp.stack([r1, gate]),
        gain_one[:, None],
        tok_low,
        n1,
        o_full,
        qkv_own,
        gain_two_part,
        parcel,
        cols,
        buckets,
        128,
    )
    dn1_sum = sum(piece.astype(F32) for piece in trade_pieces(dn1_parcel))
    dn1 = dn1_sum[:part]
    extra_sum = dn1_sum[part : part + 4] + dn1_sum[part + 4 : part + 8]
    inner_one = extra_sum[0]
    proj_came = swap(proj_parcel, "col")
    small = jnp.sum(col_gather(after(extra_sum[1:], proj_came)), axis=0)
    gain_one_grad, gain_two_grad = small[0, :width], small[1, :width]
    table_grad = jnp.transpose(
        small[2].reshape(LOW_BINS, LANES)[:, : bias_table.size // LOW_BINS].reshape(
            LOW_BINS, all_heads, buckets // LOW_BINS
        ),
        (2, 0, 1),
    ).reshape(bias_table.shape)
    gain_own = own_rows(gain_one, me, part)
    grad_tokens = (
        da.astype(F32)
        + r1 * gain_own[:, None] * dn1
        - own_rows(x, me, part) * (r1**3 / width * inner_one)
    ).astype(BF16)

    band = width // cols
    proj_sum = jnp.sum(proj_came.astype(F32), axis=0)
    router_rows = experts // cols
    grad_router = jnp.transpose(
        proj_sum[band : band + router_rows, :part]
        + proj_sum[band + router_rows : band + 2 * router_rows, :part]
    )
    proj_own = jnp.transpose(
        proj_sum[:band].reshape(band, 4, share, out_cols), (2, 0, 1, 3)
    ).reshape(share, band, 4 * out_cols)
    pieces = []
    for turn in range(share):
        moves = [
            (r * cols + c, (c // share) * cols + share * r + (c + turn) % share)
            for r in range(rows)
            for c in range(cols)
        ]
        piece = lax.dynamic_index_in_dim(proj_own, (col + turn) % share, 0, keepdims=False)
        pieces.append(lax.ppermute(piece, ("row", "col"), moves))
    pieces = jnp.stack(pieces)
    grad_four = jnp.concatenate(
        [
            lax.dynamic_index_in_dim(pieces, (col - half) % share, 0, keepdims=False)
            for half in range(share)
        ],
        axis=0,
    )
    grad_query, grad_key, grad_value, grad_out = [
        grad_four[:, w * out_cols : (w + 1) * out_cols] for w in range(4)
    ]
    grad_in, grad_eout = fill_columns(grad_in_held, 4), fill_columns(grad_eout_held, 4)
    return (
        layer_out[None],
        grad_tokens[None],
        gain_one_grad,
        gain_two_grad,
        grad_query,
        grad_key,
        grad_value,
        grad_out,
        grad_router,
        grad_in,
        grad_eout,
        table_grad,
    )


def solution(mesh):
    rows, cols = mesh.shape["row"], mesh.shape["col"]
    paired = rows == 4 and cols == 2 * rows and EXPERTS == rows * cols
    return jax.shard_map(
        expert_plan if paired else general_plan,
        mesh=mesh,
        in_specs=(
            P("col", "row", None),
            P(),
            P(),
            P("row", "col"),
            P("row", "col"),
            P("row", "col"),
            P("row", "col"),
            P("row", "col"),
            P("row", "col"),
            P("row", "col"),
            P(),
            P("col", None),
            P("col", None, None),
            P("col", "row", None),
            P("col", "row", None),
        ),
        out_specs=(
            P("col", "row", None),
            P("col", "row", None),
            P(),
            P(),
            P("row", "col"),
            P("row", "col"),
            P("row", "col"),
            P("row", "col"),
            P("row", "col"),
            P("row", "col"),
            P("row", "col"),
            P(),
        ),
        check_vma=False,
    )
```

```python
import functools

import jax
import jax.numpy as jnp
from jax import lax
from jax.experimental import pallas as pl
from jax.experimental.pallas import tpu as pltpu
from jax.sharding import PartitionSpec as P

EXPERTS = 32
CAPACITY = 48


NORM_EPS = 1e-06
NEG_FILL = -1e30


def row_totals(partial_values):
    return lax.psum(partial_values, "row")


def feature_split(partial_rows):
    return lax.psum_scatter(partial_rows, "row", scatter_dimension=1, tiled=True)


def feature_join(rows_low):
    return lax.all_gather(rows_low, "row", axis=1, tiled=True)


def norm_back(grad_normed, inputs_f, inverse_rms, gain_part, model_width):
    inner_sum = row_totals(jnp.sum(gain_part * grad_normed * inputs_f, axis=1))
    return (
        inverse_rms[:, None] * gain_part * grad_normed
        - inputs_f * (inverse_rms**3 / model_width * inner_sum)[:, None]
    )


def block_scores(
    query_heads, keys_all, bucket_rows, query_docs, doc_ids, bias_table, number, key_block
):
    head_count = bias_table.shape[1]
    head_dim = query_heads.shape[2]
    offset = number * key_block
    key_rows = lax.dynamic_slice_in_dim(keys_all, offset, key_block, 0).reshape(
        key_block, head_count, head_dim
    )
    bucket_cols = lax.dynamic_slice_in_dim(bucket_rows, offset, key_block, 1)
    key_docs = lax.dynamic_slice_in_dim(doc_ids, offset, key_block, 0)
    raw_scores = jnp.einsum(
        "ihd,jhd->hij", query_heads, key_rows, preferred_element_type=jnp.float32
    ) * head_dim ** (-0.5)
    one_hot = (bucket_cols[:, :, None] == jnp.arange(bias_table.shape[0], dtype=jnp.int32)).astype(
        jnp.float32
    )
    pair_bias = jnp.einsum("ijb,bh->hij", one_hot, bias_table, precision=lax.Precision.HIGHEST)
    allowed = (query_docs[:, None] == key_docs[None, :])[None]
    return (raw_scores + pair_bias, allowed, one_hot)


def attend_blocks(query_heads, keys_all, values_all, bucket_rows, query_docs, doc_ids, bias_table):
    tok_rows, head_count, head_dim = query_heads.shape
    seq_len = keys_all.shape[0]
    key_block = min(seq_len, 512)
    blocks = seq_len // key_block

    def first_pass(status, number):
        row_peak, row_total = status
        scores, allowed, one_hot = block_scores(
            query_heads, keys_all, bucket_rows, query_docs, doc_ids, bias_table, number, key_block
        )
        masked = jnp.where(allowed, scores, NEG_FILL)
        new_peak = jnp.maximum(row_peak, jnp.max(masked, axis=2))
        weights = jnp.where(allowed, jnp.exp(masked - new_peak[:, :, None]), 0.0)
        row_total = row_total * jnp.exp(row_peak - new_peak) + jnp.sum(weights, axis=2)
        return ((new_peak, row_total), None)

    start_status = (
        jnp.full((head_count, tok_rows), NEG_FILL, jnp.float32),
        jnp.zeros((head_count, tok_rows), jnp.float32),
    )
    (row_peak, row_total), unused = lax.scan(first_pass, start_status, jnp.arange(blocks))
    log_total = row_peak + jnp.log(row_total)

    def second_pass(running, number):
        scores, allowed, one_hot = block_scores(
            query_heads, keys_all, bucket_rows, query_docs, doc_ids, bias_table, number, key_block
        )
        soft_weights = jnp.where(allowed, jnp.exp(scores - log_total[:, :, None]), 0.0).astype(
            jnp.bfloat16
        )
        value_rows = lax.dynamic_slice_in_dim(values_all, number * key_block, key_block, 0).reshape(
            key_block, head_count, head_dim
        )
        return (
            running
            + jnp.einsum(
                "hij,jhd->ihd", soft_weights, value_rows, preferred_element_type=jnp.float32
            ),
            None,
        )

    start_acc = jnp.zeros((tok_rows, head_count, head_dim), jnp.float32)
    attended, unused = lax.scan(second_pass, start_acc, jnp.arange(blocks))
    return (attended, log_total)


def attend_blocks_back(
    query_heads,
    keys_all,
    values_all,
    bucket_rows,
    query_docs,
    doc_ids,
    bias_table,
    log_total,
    grad_heads,
    grad_dot,
):
    tok_rows, head_count, head_dim = query_heads.shape
    seq_len = keys_all.shape[0]
    model_width = head_count * head_dim
    key_block = min(seq_len, 512)
    blocks = seq_len // key_block
    scaling = head_dim ** (-0.5)

    def step_back(status, number):
        grad_query, grad_table = status
        scores, allowed, one_hot = block_scores(
            query_heads, keys_all, bucket_rows, query_docs, doc_ids, bias_table, number, key_block
        )
        key_rows = lax.dynamic_slice_in_dim(keys_all, number * key_block, key_block, 0).reshape(
            key_block, head_count, head_dim
        )
        value_rows = lax.dynamic_slice_in_dim(values_all, number * key_block, key_block, 0).reshape(
            key_block, head_count, head_dim
        )
        soft_weights = jnp.where(allowed, jnp.exp(scores - log_total[:, :, None]), 0.0)
        weights_low = soft_weights.astype(jnp.bfloat16)
        grad_soft = jnp.einsum(
            "ihd,jhd->hij", grad_heads, value_rows, preferred_element_type=jnp.float32
        )
        grad_scores = soft_weights * (grad_soft - grad_dot[:, :, None])
        grad_table = grad_table + jnp.einsum(
            "ijb,hij->bh", one_hot, grad_scores, precision=lax.Precision.HIGHEST
        )
        scores_low = grad_scores.astype(jnp.bfloat16)
        grad_query = grad_query + scaling * jnp.einsum(
            "hij,jhd->ihd", scores_low, key_rows, preferred_element_type=jnp.float32
        )
        grad_key = scaling * jnp.einsum(
            "hij,ihd->jhd", scores_low, query_heads, preferred_element_type=jnp.float32
        )
        grad_value = jnp.einsum(
            "hij,ihd->jhd", weights_low, grad_heads, preferred_element_type=jnp.float32
        )
        stacked = jnp.concatenate(
            [grad_key.reshape(key_block, model_width), grad_value.reshape(key_block, model_width)],
            axis=1,
        )
        return ((grad_query, grad_table), stacked)

    start_status = (
        jnp.zeros((tok_rows, head_count, head_dim), jnp.float32),
        jnp.zeros(bias_table.shape, jnp.float32),
    )
    (grad_query, grad_table), kv_terms = lax.scan(step_back, start_status, jnp.arange(blocks))
    return (grad_query, grad_table, kv_terms.reshape(seq_len, 2 * model_width))


def general_plan(
    tokens,
    gain_one,
    gain_two,
    w_query,
    w_key,
    w_value,
    w_out,
    w_router,
    w_in,
    w_expert_out,
    bias_table,
    segment,
    expert,
    bucket,
    cotangent,
):
    seq_len = tokens.shape[2]
    dim_rows = tokens.shape[1]
    row_count = lax.axis_size("row")
    model_width = dim_rows * row_count
    tok_rows = seq_len // row_count
    experts = EXPERTS
    hid_rows = w_expert_out.shape[0]
    ffn_width = hid_rows * row_count
    head_count = bias_table.shape[1]
    head_dim = model_width // head_count
    row_index = lax.axis_index("row")
    gathered = (
        lax.all_gather(w_query, "col", axis=1, tiled=True),
        lax.all_gather(w_key, "col", axis=1, tiled=True),
        lax.all_gather(w_value, "col", axis=1, tiled=True),
        lax.all_gather(w_out, "col", axis=1, tiled=True),
        lax.all_gather(w_router, "col", axis=1, tiled=True),
        lax.all_gather(w_in, "col", axis=1, tiled=True),
        lax.all_gather(w_expert_out, "col", axis=1, tiled=True),
    )
    query_full, key_full, value_full, out_proj_full, router_full, in_flat, out_flat = gathered
    in_full = in_flat.reshape(dim_rows, experts, ffn_width)
    out_full = out_flat.reshape(hid_rows, experts, model_width)
    stacked_weights = jnp.concatenate([query_full, key_full, value_full], axis=1)
    tok_float = jnp.transpose(tokens[0].astype(jnp.float32))
    doc_ids = segment[0]
    query_docs = lax.dynamic_slice_in_dim(doc_ids, row_index * tok_rows, tok_rows, 0)
    bucket_rows = bucket[0]
    expert_ids = expert[0, :, 0]
    gain_part_one = lax.dynamic_slice_in_dim(gain_one, row_index * dim_rows, dim_rows, 0)
    gain_part_two = lax.dynamic_slice_in_dim(gain_two, row_index * dim_rows, dim_rows, 0)
    inverse_one = lax.rsqrt(
        row_totals(jnp.sum(tok_float * tok_float, axis=1)) / model_width + NORM_EPS
    )
    normed_one = (tok_float * inverse_one[:, None] * gain_part_one).astype(jnp.bfloat16)
    projected = lax.psum_scatter(
        jnp.dot(normed_one, stacked_weights, preferred_element_type=jnp.float32),
        "row",
        scatter_dimension=0,
        tiled=True,
    ).astype(jnp.bfloat16)
    queries_low = projected[:, :model_width]
    keys_low = projected[:, model_width : 2 * model_width]
    values_low = projected[:, 2 * model_width :]
    keys_all, values_all = (
        lax.all_gather(keys_low, "row", axis=0, tiled=True),
        lax.all_gather(values_low, "row", axis=0, tiled=True),
    )
    query_heads = queries_low.reshape(tok_rows, head_count, head_dim)
    attended, log_total = attend_blocks(
        query_heads, keys_all, values_all, bucket_rows, query_docs, doc_ids, bias_table
    )
    attn_low = attended.reshape(tok_rows, model_width).astype(jnp.bfloat16)
    heads_home = lax.all_to_all(attn_low, "row", split_axis=1, concat_axis=0, tiled=True)
    attn_rows = feature_split(
        jnp.dot(heads_home, out_proj_full, preferred_element_type=jnp.float32)
    )
    residual = tok_float + attn_rows
    inverse_two = lax.rsqrt(
        row_totals(jnp.sum(residual * residual, axis=1)) / model_width + NORM_EPS
    )
    normed_two = (residual * inverse_two[:, None] * gain_part_two).astype(jnp.bfloat16)
    logits = row_totals(jnp.dot(normed_two, router_full, preferred_element_type=jnp.float32))
    gate_probs = jax.nn.softmax(logits, axis=1)
    picked = (expert_ids[:, None] == jnp.arange(experts, dtype=jnp.int32)[None, :]).astype(
        jnp.int32
    )
    picked_float = picked.astype(jnp.float32)
    slot_rank = jnp.sum((jnp.cumsum(picked, axis=0) - 1) * picked, axis=1)
    slot_index = expert_ids * CAPACITY + slot_rank
    token_gate = jnp.sum(gate_probs * picked_float, axis=1)
    slots_in = (
        jnp.zeros((experts * CAPACITY, dim_rows), jnp.bfloat16).at[slot_index].set(normed_two)
    )
    slots_own = slots_in.reshape(experts, CAPACITY, dim_rows)
    lead_count = slots_own.shape[0]
    slot_count = slots_own.shape[1]
    pre_partial = jnp.einsum("ecd,def->ecf", slots_own, in_full, preferred_element_type=jnp.float32)
    pre_act = feature_split(pre_partial.reshape(lead_count * slot_count, ffn_width))
    hidden = jax.nn.gelu(pre_act).astype(jnp.bfloat16)
    hidden_three = hidden.reshape(lead_count, slot_count, hid_rows)
    out_partial = jnp.einsum(
        "ecf,fed->ecd", hidden_three, out_full, preferred_element_type=jnp.float32
    )
    expert_local = feature_split(out_partial.reshape(lead_count * slot_count, model_width))
    expert_tok = expert_local[slot_index]
    layer_out = (residual + token_gate[:, None] * expert_tok).astype(jnp.bfloat16)
    grad_final = jnp.transpose(cotangent[0].astype(jnp.float32))
    grad_gate = row_totals(jnp.sum(grad_final * expert_tok, axis=1))
    grad_expert_tok = (token_gate[:, None] * grad_final).astype(jnp.bfloat16)
    grad_slots = (
        jnp.zeros((experts * CAPACITY, dim_rows), jnp.bfloat16).at[slot_index].set(grad_expert_tok)
    )
    grad_slots_local = grad_slots.reshape(experts, CAPACITY, dim_rows)
    grad_slots_full = feature_join(
        grad_slots_local.reshape(lead_count * slot_count, dim_rows)
    ).reshape(lead_count, slot_count, model_width)
    grad_hidden = jnp.einsum(
        "ecd,fed->ecf", grad_slots_full, out_full, preferred_element_type=jnp.float32
    )
    grad_out_weight = jnp.einsum(
        "ecf,ecd->fed", hidden_three, grad_slots_full, preferred_element_type=jnp.float32
    )
    unused, gelu_back = jax.vjp(jax.nn.gelu, pre_act)
    grad_pre = gelu_back(grad_hidden.reshape(lead_count * slot_count, hid_rows))[0].astype(
        jnp.bfloat16
    )
    grad_pre_full = feature_join(grad_pre).reshape(lead_count, slot_count, ffn_width)
    grad_slots_in = jnp.einsum(
        "ecf,def->ecd", grad_pre_full, in_full, preferred_element_type=jnp.float32
    )
    grad_in_weight = jnp.einsum(
        "ecd,ecf->def", slots_own, grad_pre_full, preferred_element_type=jnp.float32
    )
    grad_logits = ((grad_gate * token_gate)[:, None] * (picked_float - gate_probs)).astype(
        jnp.bfloat16
    )
    router_back = lax.dot_general(
        grad_logits, router_full, (((1,), (1,)), ((), ())), preferred_element_type=jnp.float32
    )
    grad_normed_two = grad_slots_in.reshape(experts * CAPACITY, dim_rows)[slot_index] + router_back
    grad_router = lax.dot_general(
        normed_two, grad_logits, (((0,), (0,)), ((), ())), preferred_element_type=jnp.float32
    )
    grad_res = grad_final + norm_back(
        grad_normed_two, residual, inverse_two, gain_part_two, model_width
    )
    grad_gain_two = jnp.sum(grad_normed_two * residual * inverse_two[:, None], axis=0)
    grad_attn_full = feature_join(grad_res.astype(jnp.bfloat16))
    grad_heads_home = lax.dot_general(
        grad_attn_full, out_proj_full, (((1,), (1,)), ((), ())), preferred_element_type=jnp.float32
    ).astype(jnp.bfloat16)
    grad_out_proj = lax.dot_general(
        heads_home, grad_attn_full, (((0,), (0,)), ((), ())), preferred_element_type=jnp.float32
    )
    grad_attn = lax.all_to_all(grad_heads_home, "row", split_axis=0, concat_axis=1, tiled=True)
    grad_heads = grad_attn.reshape(tok_rows, head_count, head_dim)
    grad_dot = jnp.einsum("ihd,ihd->hi", grad_heads.astype(jnp.float32), attended)
    grad_query, grad_table, kv_terms = attend_blocks_back(
        query_heads,
        keys_all,
        values_all,
        bucket_rows,
        query_docs,
        doc_ids,
        bias_table,
        log_total,
        grad_heads,
        grad_dot,
    )
    key_value_grads = lax.psum_scatter(kv_terms, "row", scatter_dimension=0, tiled=True)
    grad_qkv = jnp.concatenate(
        [
            grad_query.reshape(tok_rows, model_width).astype(jnp.bfloat16),
            key_value_grads.astype(jnp.bfloat16),
        ],
        axis=1,
    )
    portion = lax.all_gather(grad_qkv, "row", axis=0, tiled=True)
    grad_part = lax.dot_general(
        portion, stacked_weights, (((1,), (1,)), ((), ())), preferred_element_type=jnp.float32
    )
    grad_weights = lax.dot_general(
        normed_one, portion, (((0,), (0,)), ((), ())), preferred_element_type=jnp.float32
    )
    grad_input = grad_res + norm_back(grad_part, tok_float, inverse_one, gain_part_one, model_width)
    grad_gain_one = jnp.sum(grad_part * tok_float * inverse_one[:, None], axis=0)
    summed = (
        lax.psum_scatter(grad_weights[:, :model_width], "col", scatter_dimension=1, tiled=True),
        lax.psum_scatter(
            grad_weights[:, model_width : 2 * model_width], "col", scatter_dimension=1, tiled=True
        ),
        lax.psum_scatter(
            grad_weights[:, 2 * model_width :], "col", scatter_dimension=1, tiled=True
        ),
        lax.psum_scatter(grad_out_proj, "col", scatter_dimension=1, tiled=True),
        lax.psum_scatter(grad_router, "col", scatter_dimension=1, tiled=True),
        lax.psum_scatter(
            grad_in_weight.reshape(dim_rows, experts * ffn_width),
            "col",
            scatter_dimension=1,
            tiled=True,
        ),
        lax.psum_scatter(
            grad_out_weight.reshape(hid_rows, experts * model_width),
            "col",
            scatter_dimension=1,
            tiled=True,
        ),
    )
    grad_query_w, grad_key_w, grad_value_w, grad_out_w, grad_router_w, grad_in_w, grad_expert_w = (
        summed
    )
    place_one = lax.dynamic_update_slice_in_dim(
        jnp.zeros((model_width,), jnp.float32), grad_gain_one, row_index * dim_rows, 0
    )
    place_two = lax.dynamic_update_slice_in_dim(
        jnp.zeros((model_width,), jnp.float32), grad_gain_two, row_index * dim_rows, 0
    )
    gain_one_grad, gain_two_grad, table_grad = lax.psum(
        (place_one, place_two, grad_table), ("row", "col")
    )
    layer_out_t = jnp.transpose(layer_out)[None]
    grad_input_t = jnp.transpose(grad_input.astype(jnp.bfloat16))[None]
    return (
        layer_out_t,
        grad_input_t,
        gain_one_grad,
        gain_two_grad,
        grad_query_w,
        grad_key_w,
        grad_value_w,
        grad_out_w,
        grad_router_w,
        grad_in_w,
        grad_expert_w,
        table_grad,
    )


BF16 = jnp.bfloat16
F32 = jnp.float32
I32 = jnp.int32
NT = (((1,), (1,)), ((), ()))
NN = (((1,), (0,)), ((), ()))
TN = (((0,), (0,)), ((), ()))
LANES = 128
PAIR_ROWS = 16
LOW_BINS = 8
GELU_SCALE = 0.7978845608028654
GELU_CUBE = 0.044715
QUICK = pl.CostEstimate(flops=0, bytes_accessed=0, transcendentals=0)


def mm(left, right, dims):
    return lax.dot_general(left, right, dims, preferred_element_type=F32)


def two_parts(values):
    high = values.astype(BF16)
    return high, (values - high.astype(F32)).astype(BF16)


def attend_kernel(heads, head_dim, q_ref, k_ref, v_ref, idx_ref, tab_ref, o_ref, p_ref):
    rows, keys = idx_ref.shape
    idx = idx_ref[...].astype(F32).astype(I32)
    for h in range(heads):
        span = slice(h * head_dim, (h + 1) * head_dim)
        table = jnp.broadcast_to(tab_ref[h : h + 1, :], (rows, LANES))
        bias = jnp.concatenate(
            [
                jnp.take_along_axis(table, idx[:, c : c + LANES], axis=1)
                for c in range(0, keys, LANES)
            ],
            axis=1,
        )
        scores = mm(q_ref[span, :], k_ref[span, :], TN) * head_dim**-0.5 + bias
        weights = jnp.exp(scores - jnp.max(scores, axis=1, keepdims=True))
        soft = (weights * (1.0 / jnp.sum(weights, axis=1, keepdims=True))).astype(BF16)
        p_ref[h] = soft
        o_ref[span, :] = mm(v_ref[span, :], soft, NT)


def attend(q, k, v, idx, tab, heads, tile):
    width, keys = q.shape
    whole = lambda a: pl.BlockSpec(a.shape, lambda i: (0, 0))
    return pl.pallas_call(
        functools.partial(attend_kernel, heads, width // heads),
        grid=(keys // tile,),
        in_specs=[
            pl.BlockSpec((width, tile), lambda i: (0, i)),
            whole(k),
            whole(v),
            pl.BlockSpec((tile, keys), lambda i: (i, 0)),
            whole(tab),
        ],
        out_specs=[
            pl.BlockSpec((width, tile), lambda i: (0, i)),
            pl.BlockSpec((heads, tile, keys), lambda i: (0, i, 0)),
        ],
        out_shape=[
            jax.ShapeDtypeStruct((width, keys), F32),
            jax.ShapeDtypeStruct((heads, keys, keys), BF16),
        ],
        compiler_params=pltpu.CompilerParams(vmem_limit_bytes=48 * 2**20),
        cost_estimate=QUICK,
    )(q, k, v, idx, tab)


def back_kernel(
    heads,
    count,
    experts,
    cols,
    place_ref,
    q_ref,
    k_ref,
    v_ref,
    idx_ref,
    p_ref,
    o_ref,
    slot_ref,
    h1_ref,
    row_ref,
    col_ref,
    x_ref,
    n1_ref,
    ofull_ref,
    w_ref,
    gain_two_ref,
    *refs,
):
    pieces = refs[:count]
    layer_ref, da_ref, proj_ref = refs[count : count + 3]
    dn1_refs = refs[count + 3 : 2 * count + 3]
    g_aug, v_aug, dqkv, dk_acc, dv_acc, hist, router_acc, dn1_acc = refs[2 * count + 3 :]
    step, steps = pl.program_id(0), pl.num_programs(0)
    me = place_ref[0]
    part, tile = q_ref.shape
    keys = k_ref.shape[1]
    head_dim = part // heads
    aug = g_aug.shape[0] // heads
    width = x_ref.shape[0]
    slots = pieces[0].shape[0]
    scale = head_dim**-0.5

    @pl.when(step == 0)
    def _():
        dk_acc[...] = jnp.zeros_like(dk_acc)
        dv_acc[...] = jnp.zeros_like(dv_acc)
        hist[...] = jnp.zeros_like(hist)
        placed = jnp.zeros((3 * part, keys), F32)
        router = jnp.zeros((part, 2 * experts), F32)
        slot_row = lax.broadcasted_iota(I32, (slots, keys), 0)
        for k in range(count):
            spread = jnp.where(slot_row + (me ^ k) * slots == slot_ref[...], 1.0, 0.0).astype(BF16)
            placed = placed + mm(pieces[k][:, : 3 * part], spread, TN)
            router = router + pieces[k][:part, 3 * part :].astype(F32)
        router_acc[...] = router[:, :experts] + router[:, experts:]
        layer_ref[...] = (h1_ref[...] + row_ref[1:2, :] * placed[:part]).astype(BF16)
        da_ref[...] = placed[part : 2 * part].astype(BF16)
        fill = jnp.zeros((PAIR_ROWS - 2, keys), F32)
        ones = jnp.concatenate([jnp.ones((2, keys), F32), fill], axis=0).astype(BF16)
        for h in range(heads):
            span = slice(h * head_dim, (h + 1) * head_dim)
            do = placed[2 * part + h * head_dim : 2 * part + (h + 1) * head_dim]
            delta = jnp.sum(do * o_ref[span, :], axis=0, keepdims=True)
            high = delta.astype(BF16).astype(F32)
            rest = jnp.concatenate([-high, high - delta, fill], axis=0).astype(BF16)
            g_aug[h * aug : h * aug + head_dim, :] = do.astype(BF16)
            g_aug[h * aug + head_dim : (h + 1) * aug, :] = rest
            v_aug[h * aug : h * aug + head_dim, :] = v_ref[span, :]
            v_aug[h * aug + head_dim : (h + 1) * aug, :] = ones

    lanes = pl.ds(pl.multiple_of(step * tile, tile), tile)
    slopes = []
    for h in range(heads):
        span = slice(h * head_dim, (h + 1) * head_dim)
        soft = p_ref[h]
        g_part = g_aug[h * aug : (h + 1) * aug, lanes]
        diff = mm(g_part, v_aug[h * aug : (h + 1) * aug, :], TN)
        slope = (soft.astype(F32) * diff).astype(BF16)
        slopes.append(slope)
        dqkv[span, lanes] = (mm(k_ref[span, :], slope, NT) * scale).astype(BF16)
        dk_acc[span, :] += mm(q_ref[span, :], slope, NN) * scale
        dv_acc[span, :] += mm(g_part[:head_dim], soft, NN)
    idx = idx_ref[...].astype(F32).astype(I32)
    high = (idx // LOW_BINS).astype(F32).astype(BF16)
    low = (idx % LOW_BINS).astype(F32).astype(BF16)
    high_bins = hist.shape[1] // (heads * PAIR_ROWS)
    one = jnp.ones((), BF16)
    zero = jnp.zeros((), BF16)
    total = hist[...]
    for s in range(0, tile, PAIR_ROWS):
        rows = slice(s, s + PAIR_ROWS)
        left = jnp.concatenate(
            [jnp.where(low[rows] == n, one, zero) for n in range(LOW_BINS)], axis=0
        )
        right = jnp.concatenate(
            [
                jnp.where(high[rows] == n, slopes[h][rows], zero)
                for h in range(heads)
                for n in range(high_bins)
            ],
            axis=0,
        )
        total = total + mm(left, right, NT)
    hist[...] = total

    @pl.when(step == steps - 1)
    def _():
        dqkv[part : 2 * part, :] = dk_acc[...].astype(BF16)
        dqkv[2 * part :, :] = dv_acc[...].astype(BF16)
        r1 = row_ref[0:1, :]
        inner = jnp.zeros((1, keys), F32)
        gain_rows = []
        for d in range(count):
            rows = slice(d * part, (d + 1) * part)
            dn1 = mm(w_ref[rows, :], dqkv[...], NN)
            dn1_acc[d] = dn1.astype(BF16)
            dn1_x = dn1 * x_ref[rows, :].astype(F32)
            inner = inner + jnp.sum(dn1_x * col_ref[rows, :], axis=0, keepdims=True)
            gain = jnp.sum(dn1_x * r1, axis=1, keepdims=True)
            gain_rows.append(jnp.transpose(jnp.broadcast_to(gain, (part, LANES)))[:1])
        cells = hist[...]
        same = lax.broadcasted_iota(I32, cells.shape, 0) % PAIR_ROWS == (
            lax.broadcasted_iota(I32, cells.shape, 1) % PAIR_ROWS
        )
        cells = jnp.where(same, cells, 0.0)
        low_rows = (LOW_BINS, cells.shape[0])
        sum_rows = jnp.where(
            lax.broadcasted_iota(I32, low_rows, 1) // PAIR_ROWS
            == lax.broadcasted_iota(I32, low_rows, 0),
            1.0,
            0.0,
        )
        lane_cols = (cells.shape[1], LANES)
        bins = heads * high_bins
        sum_cols = jnp.where(
            lax.broadcasted_iota(I32, lane_cols, 0) // PAIR_ROWS + me * bins
            == lax.broadcasted_iota(I32, lane_cols, 1),
            1.0,
            0.0,
        )
        exact = functools.partial(
            lax.dot_general,
            dimension_numbers=NN,
            precision=lax.Precision.HIGHEST,
            preferred_element_type=F32,
        )
        table = exact(exact(sum_rows, cells), sum_cols)
        half = LOW_BINS // 2
        tail = jnp.zeros((1, width - half * LANES), F32)
        table_rows = [
            jnp.concatenate([table[n + m : n + m + 1] for m in range(half)] + [tail], axis=1)
            for n in (0, half)
        ]
        small = jnp.concatenate(
            [jnp.concatenate(gain_rows, axis=1), gain_two_ref[...]] + table_rows, axis=0
        )
        inner_high = inner.astype(BF16).astype(F32)
        extra = jnp.concatenate(
            [inner_high, inner - inner_high, jnp.zeros((PAIR_ROWS - 2, keys), F32)], axis=0
        ).astype(BF16)
        for k in range(count):
            dn1_refs[k][:part, :] = dn1_acc[me ^ k]
            dn1_refs[k][part:, :] = extra
        router = jnp.transpose(router_acc[...])
        band = width // cols
        share = experts // cols
        pad = jnp.zeros((share, width - part), F32)
        pieces_of = lambda a, first: a[first : first + band, :]
        halves = part // band
        for b in range(halves):
            three = jnp.concatenate(
                [pieces_of(dqkv, w * part + b * band) for w in range(3)], axis=0
            )
            da_part = pieces_of(da_ref, b * band)
            for c in range(cols):
                rows = slice(c * band, (c + 1) * band)
                proj_ref[c, :band, b * 4 * band : (b + 1) * 4 * band] = jnp.concatenate(
                    [mm(n1_ref[rows, :], three, NT), mm(ofull_ref[rows, :], da_part, NT)], axis=1
                ).astype(BF16)
        for c in range(cols):
            own = jnp.concatenate([router[c * share : (c + 1) * share], pad], axis=1)
            facts = jnp.concatenate([own, small], axis=0)
            facts_high = facts.astype(BF16).astype(F32)
            proj_ref[c, band:, :] = jnp.concatenate(
                [facts_high, facts - facts_high], axis=0
            ).astype(BF16)


def attend_back(
    place, q, k, v, idx, p, o, slot, h1, row_facts, gain, x, n1, o_full, w, gain_two, pieces, cols, buckets, tile
):
    part, keys = q.shape
    width = x.shape[0]
    count = len(pieces)
    heads = p.shape[0]
    experts = (pieces[0].shape[1] - 3 * part) // 2
    aug_width = part + heads * PAIR_ROWS
    hist_shape = (LOW_BINS * PAIR_ROWS, heads * (buckets // LOW_BINS) * PAIR_ROWS)
    fixed = lambda a: pl.BlockSpec(a.shape, lambda i, m: (0,) * len(a.shape))
    outs = [
        jax.ShapeDtypeStruct((part, keys), BF16),
        jax.ShapeDtypeStruct((part, keys), BF16),
        jax.ShapeDtypeStruct((cols, width // cols + PAIR_ROWS, width), BF16),
    ] + [jax.ShapeDtypeStruct((part + PAIR_ROWS, keys), BF16)] * count
    rest = (o, slot, h1, row_facts, gain, x, n1, o_full, w, gain_two, *pieces)
    out = pl.pallas_call(
        functools.partial(back_kernel, heads, count, experts, cols),
        grid_spec=pltpu.PrefetchScalarGridSpec(
            num_scalar_prefetch=1,
            grid=(keys // tile,),
            in_specs=[
                pl.BlockSpec((part, tile), lambda i, m: (0, i)),
                fixed(k),
                fixed(v),
                pl.BlockSpec((tile, keys), lambda i, m: (i, 0)),
                pl.BlockSpec((heads, tile, keys), lambda i, m: (0, i, 0)),
            ]
            + [fixed(a) for a in rest],
            out_specs=[fixed(a) for a in outs],
            scratch_shapes=[
                pltpu.VMEM((aug_width, keys), BF16),
                pltpu.VMEM((aug_width, keys), BF16),
                pltpu.VMEM((3 * part, keys), BF16),
                pltpu.VMEM((part, keys), F32),
                pltpu.VMEM((part, keys), F32),
                pltpu.VMEM(hist_shape, F32),
                pltpu.VMEM((part, experts), F32),
                pltpu.VMEM((count, part, keys), BF16),
            ],
        ),
        out_shape=outs,
        compiler_params=pltpu.CompilerParams(vmem_limit_bytes=56 * 2**20),
        cost_estimate=QUICK,
    )(place, q, k, v, idx, p, *rest)
    return out[0], out[1], out[2], out[3:]


def fill_rows(place_ref, places, in_refs, win, part):
    for in_ref, (k, offset) in zip(in_refs, places):
        first = pl.multiple_of((place_ref[0] ^ k) * part + offset, PAIR_ROWS)
        win[pl.ds(first, in_ref.shape[0]), :] = in_ref[...]


def inner_kernel(count, places, place_ref, x_ref, dy_ref, router_ref, *refs):
    in_refs, refs = refs[: len(places)], refs[len(places) :]
    dys_ref, hidden_ref, slope_ref = refs[:3]
    ge_refs, win = refs[3 : 3 + count], refs[3 + count]
    step = pl.program_id(0)

    @pl.when(step == 0)
    def _():
        logits = mm(x_ref[...], router_ref[...], NN)
        probs = jnp.exp(logits - jnp.max(logits, axis=1, keepdims=True))
        own = lax.broadcasted_iota(I32, logits.shape, 1) == place_ref[1]
        gate = jnp.sum(jnp.where(own, probs, 0.0), axis=1, keepdims=True)
        gate = gate / jnp.sum(probs, axis=1, keepdims=True)
        dys_ref[...] = (gate * dy_ref[...].astype(F32)).astype(BF16)

    fill_rows(place_ref, places, in_refs, win, win.shape[0] // count)
    pre = mm(x_ref[...], win[...], NN)
    square = pre * pre
    curve = jnp.tanh(GELU_SCALE * pre * (1.0 + GELU_CUBE * square))
    half = 0.5 * (1.0 + curve)
    hidden = (pre * half).astype(BF16)
    hidden_ref[...] = hidden
    slope = half + 0.5 * pre * (1.0 - curve * curve) * (
        GELU_SCALE * (1.0 + 3.0 * GELU_CUBE * square)
    )
    slope_ref[...] = slope.astype(BF16)
    ge = mm(hidden, dys_ref[...], TN).astype(BF16)
    for k in range(count):

        @pl.when(step == k)
        def _(k=k):
            ge_refs[k][...] = ge


def outer_kernel(count, places, place_ref, x_ref, dys_ref, hidden_ref, slope_ref, *refs):
    in_refs, refs = refs[: len(places)], refs[len(places) :]
    eout_refs, back_ref = refs[:count], refs[count]
    gi_refs = refs[count + 1 : 2 * count + 1]
    win, eout, y_acc, dx_acc, gi = refs[2 * count + 1 :]
    step = pl.program_id(0)
    part = gi_refs[0].shape[0]

    @pl.when(step == 0)
    def _():
        y_acc[...] = jnp.zeros_like(y_acc)
        dx_acc[...] = jnp.zeros_like(dx_acc)

    fill_rows(place_ref, places, in_refs, win, part)
    for k in range(count):

        @pl.when(step == k)
        def _(k=k):
            eout[...] = eout_refs[k][...]

    y_acc[...] += mm(hidden_ref[...], eout[...], NN)
    dpre = (mm(dys_ref[...], eout[...], NT) * slope_ref[...].astype(F32)).astype(BF16)
    dx_acc[...] += mm(dpre, win[...], NT)
    gi[...] = mm(x_ref[...], dpre, TN).astype(BF16)
    for k in range(count):
        gi_refs[k][...] = gi[pl.ds(pl.multiple_of((place_ref[0] ^ k) * part, part), part), :]

    @pl.when(step == count - 1)
    def _():
        width = y_acc.shape[1]
        back_ref[:, :width] = y_acc[...].astype(BF16)
        back_ref[:, width:] = dx_acc[...].astype(BF16)


def expert_inner(place, x, dy, router, in_held, places, count):
    slots, width = x.shape
    hidden_width = in_held[0].shape[1]
    chunk = hidden_width // count
    fixed = lambda shape: pl.BlockSpec(shape, lambda i, m: (0, 0))
    wide = pl.BlockSpec((slots, chunk), lambda i, m: (0, i))
    shape = lambda s: jax.ShapeDtypeStruct(s, BF16)
    out = pl.pallas_call(
        functools.partial(inner_kernel, count, places),
        grid_spec=pltpu.PrefetchScalarGridSpec(
            num_scalar_prefetch=1,
            grid=(count,),
            in_specs=[fixed(x.shape), fixed(dy.shape), fixed(router.shape)]
            + [pl.BlockSpec((a.shape[0], chunk), lambda i, m: (0, m[0] ^ i)) for a in in_held],
            out_specs=[fixed(x.shape), wide, wide] + [fixed((chunk, width))] * count,
            scratch_shapes=[pltpu.VMEM((width, chunk), BF16)],
        ),
        out_shape=[shape(x.shape)]
        + [shape((slots, hidden_width))] * 2
        + [shape((chunk, width))] * count,
        compiler_params=pltpu.CompilerParams(vmem_limit_bytes=56 * 2**20),
        cost_estimate=QUICK,
    )(place, x, dy, router, *in_held)
    return out[0], out[1], out[2], out[3:]


def expert_outer(place, x, dys, hidden, slope, in_held, places, eout_held):
    count = len(eout_held)
    slots, width = x.shape
    hidden_width = in_held[0].shape[1]
    part = width // count
    chunk = hidden_width // count
    fixed = lambda shape: pl.BlockSpec(shape, lambda i, m: (0, 0))
    wide = pl.BlockSpec((slots, chunk), lambda i, m: (0, i))
    lanes = lambda rows: pl.BlockSpec((rows, chunk), lambda i, m: (0, m[0] ^ i))
    out = pl.pallas_call(
        functools.partial(outer_kernel, count, places),
        grid_spec=pltpu.PrefetchScalarGridSpec(
            num_scalar_prefetch=1,
            grid=(count,),
            in_specs=[fixed(x.shape), fixed(x.shape), wide, wide]
            + [lanes(a.shape[0]) for a in in_held]
            + [fixed((chunk, width))] * count,
            out_specs=[fixed((slots, 2 * width))] + [lanes(part)] * count,
            scratch_shapes=[
                pltpu.VMEM((width, chunk), BF16),
                pltpu.VMEM((chunk, width), BF16),
                pltpu.VMEM((slots, width), F32),
                pltpu.VMEM((slots, width), F32),
                pltpu.VMEM((width, chunk), BF16),
            ],
        ),
        out_shape=[jax.ShapeDtypeStruct((slots, 2 * width), BF16)]
        + [jax.ShapeDtypeStruct((part, hidden_width), BF16)] * count,
        compiler_params=pltpu.CompilerParams(vmem_limit_bytes=56 * 2**20),
        cost_estimate=QUICK,
    )(place, x, dys, hidden, slope, *in_held, *eout_held)
    return out[0], out[1:]


def slot_kernel(
    count,
    experts,
    place_ref,
    home_ref,
    dy_ref,
    n2_ref,
    h1_ref,
    scalar_ref,
    router_ref,
    out_ref,
    gain_ref,
    gain_part_ref,
    *refs,
):
    me = place_ref[0]
    parcel_refs, parcel = refs[:count], refs[count]
    slots, width = dy_ref.shape
    part = width // count
    y = home_ref[:, :width]
    dy = dy_ref[...].astype(F32)
    h1 = h1_ref[...].astype(F32)
    scalars = scalar_ref[...]
    probs, gate, r2 = scalars[:, :experts], scalars[:, experts : experts + 1], scalars[:, experts + 1 :]
    dgate = jnp.sum(dy * y.astype(F32), axis=1, keepdims=True)
    row = lax.broadcasted_iota(I32, (slots, experts), 0)
    lane = lax.broadcasted_iota(I32, (slots, experts), 1)
    hot = jnp.where(row // CAPACITY * count + me == lane, 1.0, 0.0)
    dlogits = ((dgate * gate) * (hot - probs)).astype(BF16)
    dn2 = home_ref[:, width:].astype(F32) + mm(dlogits, router_ref[...], NT)
    scaled = dn2 * gain_ref[...]
    inner = jnp.sum(scaled * h1, axis=1, keepdims=True)
    dh1 = dy + r2 * scaled - h1 * (r2 * r2 * r2 * (1.0 / width) * inner)
    gain_part_ref[...] = jnp.sum(dn2 * h1 * r2, axis=0, keepdims=True)
    da = dh1.astype(BF16)
    do = mm(da, out_ref[...], NT).astype(BF16)
    router_high, router_low = two_parts(mm(n2_ref[...], dlogits, TN))
    fill = jnp.zeros((slots - part, 2 * experts), BF16)
    for d in range(count):
        span = slice(d * part, (d + 1) * part)
        router = jnp.concatenate([router_high[span], router_low[span]], axis=1)
        router = jnp.concatenate([router, fill], axis=0)
        parcel[me ^ d] = jnp.concatenate([y[:, span], da[:, span], do[:, span], router], axis=1)
    for k in range(count):
        parcel_refs[k][...] = parcel[k]


def slot_work(place, home, dy, n2, h1, scalars, router, out_proj, gain, count):
    slots, width = dy.shape
    experts = router.shape[1]
    lanes = 3 * width // count + 2 * experts
    fixed = lambda a: pl.BlockSpec(a.shape, lambda i, m: (0,) * len(a.shape))
    ins = (home, dy, n2, h1, scalars, router, out_proj, gain)
    outs = [jax.ShapeDtypeStruct((1, width), F32)]
    outs += [jax.ShapeDtypeStruct((slots, lanes), BF16)] * count
    out = pl.pallas_call(
        functools.partial(slot_kernel, count, experts),
        grid_spec=pltpu.PrefetchScalarGridSpec(
            num_scalar_prefetch=1,
            grid=(1,),
            in_specs=[fixed(a) for a in ins],
            out_specs=[fixed(a) for a in outs],
            scratch_shapes=[pltpu.VMEM((count, slots, lanes), BF16)],
        ),
        out_shape=outs,
        compiler_params=pltpu.CompilerParams(vmem_limit_bytes=48 * 2**20),
        cost_estimate=QUICK,
    )(place, *ins)
    return out[1:], out[0]


def send(piece, offset):
    count = lax.axis_size("row")
    return lax.ppermute(piece, "row", [(i, i ^ offset) for i in range(count)])


def row_join(block, far):
    me = lax.axis_index("row")
    count = lax.axis_size("row")
    near = send(jnp.stack([block, far]), 1)
    held = jnp.stack([block, near[0], far, near[1]])
    return jnp.concatenate(
        [lax.dynamic_index_in_dim(held, p ^ me, 0, keepdims=True) for p in range(count)]
    )


def row_gather(block):
    return row_join(block, send(block, 2))


def swap(blocks, axis):
    return lax.all_to_all(blocks, axis, 0, 0)


def col_gather(block):
    count = lax.axis_size("col")
    return swap(jnp.broadcast_to(block[None], (count,) + block.shape), "col")


def trade(piece_for):
    me = lax.axis_index("row")
    return trade_pieces([piece_for(me ^ k) for k in range(lax.axis_size("row"))])


def trade_pieces(pieces):
    count = len(pieces)
    held = {k: send(pieces[k], k) for k in (2, 3, 1)}
    return [pieces[0]] + [held[k] for k in range(1, count)]


def lay(held):
    me = lax.axis_index("row")
    out = jnp.zeros((len(held),) + held[0].shape, held[0].dtype)
    for k, piece in enumerate(held):
        out = lax.dynamic_update_slice_in_dim(out, piece[None], me ^ k, 0)
    return out


def after(value, *earlier):
    return lax.optimization_barrier((value,) + earlier)[0]


def fill_kernel(count, me_ref, *refs):
    step = pl.program_id(1)
    for k in range(count):

        @pl.when(step == k)
        def _(k=k):
            refs[count][...] = refs[k][...].astype(F32)


def fill_columns(held, splits):
    count = len(held)
    height, width = held[0].shape
    block = height // splits
    me = lax.axis_index("row").astype(I32).reshape(1)
    return pl.pallas_call(
        functools.partial(fill_kernel, count),
        grid_spec=pltpu.PrefetchScalarGridSpec(
            num_scalar_prefetch=1,
            grid=(splits, count),
            in_specs=[pl.BlockSpec((block, width), lambda i, k, m: (i, 0))] * count,
            out_specs=pl.BlockSpec((block, width), lambda i, k, m: (i, m[0] ^ k)),
        ),
        out_shape=jax.ShapeDtypeStruct((height, count * width), F32),
        compiler_params=pltpu.CompilerParams(vmem_limit_bytes=48 * 2**20),
        cost_estimate=QUICK,
    )(me, *held)


def own_rows(array, me, count):
    return lax.dynamic_slice_in_dim(array, me * count, count, 0)


def expert_plan(
    tokens,
    gain_one,
    gain_two,
    w_query,
    w_key,
    w_value,
    w_out,
    w_router,
    w_in,
    w_expert_out,
    bias_table,
    segment,
    expert,
    bucket,
    cotangent,
):
    rows, cols = lax.axis_size("row"), lax.axis_size("col")
    me, col = lax.axis_index("row"), lax.axis_index("col")
    part, seq_len = tokens.shape[1:]
    width = part * rows
    tok_rows = seq_len // rows
    buckets, all_heads = bias_table.shape
    heads = all_heads // rows
    head_dim = width // all_heads
    experts = w_router.shape[1] * cols
    hidden_width = w_expert_out.shape[0] * rows
    slots = (experts // rows) * CAPACITY
    out_cols = w_query.shape[1]
    share = cols // rows

    doc_ids = segment[0]
    expert_ids = expert[0, :, 0]

    tok_far = send(tokens[0], 2)
    tok_low = row_join(tokens[0], tok_far).reshape(width, seq_len)
    qkv_cols = col_gather(jnp.concatenate([w_query, w_key, w_value], axis=1))
    same_doc = own_rows(doc_ids, me, tok_rows)[:, None] == doc_ids[None, :]
    masked = jnp.where(same_doc, after(bucket, tok_far)[0], buckets).astype(BF16)
    idx_far = send(masked, 2)
    cot_own = cotangent[0]
    cot_far = send(cot_own, 2)
    lane_cut = lambda array, count, k: lax.dynamic_slice_in_dim(array, (me ^ k) * count, count, 1)
    half = part // 2
    in_first = send(lane_cut(after(w_in, tok_far)[:half], hidden_width, 2), 2)
    qkv_cols = after(qkv_cols, idx_far, cot_far, in_first)
    out_part = after(jnp.concatenate([w_out, w_router], axis=1), qkv_cols)
    out_gathered = col_gather(out_part)
    qkv_cols = qkv_cols.reshape(rows, share, part, 3 * out_cols)
    qkv_held = trade(lambda d: lax.dynamic_index_in_dim(qkv_cols, d, 0, keepdims=False))
    second_cut = lane_cut(after(w_in, idx_far)[half:], hidden_width, 2)
    in_second = send(after(second_cut, qkv_cols), 2)
    eout_cuts = [lane_cut(after(w_expert_out, qkv_cols), width, k) for k in range(rows)]
    qkv_held = after(tuple(qkv_held), in_second, *eout_cuts)
    qkv_own = jnp.transpose(
        lay(qkv_held).reshape(rows, share, part, 3, out_cols), (0, 2, 3, 1, 4)
    ).reshape(width, 3 * part)
    idx = row_join(masked, idx_far).reshape(seq_len, seq_len)
    cot_low = row_join(cot_own, cot_far).reshape(width, seq_len)

    picked = expert_ids[None, :] == jnp.arange(experts, dtype=I32)[:, None]
    picked_float = picked.astype(F32)
    steps = jnp.arange(seq_len, dtype=I32)
    upper = (steps[:, None] <= steps[None, :]).astype(BF16)
    ranks = mm(picked.astype(BF16), upper, NN) - 1.0
    slot_rank = jnp.sum(ranks * picked_float, axis=0).astype(I32)
    slot = (expert_ids % rows) * slots + (expert_ids // rows) * CAPACITY + slot_rank
    choose = (jnp.arange(slots, dtype=I32)[:, None] + me * slots == slot[None, :]).astype(BF16)

    x = tok_low.astype(F32)
    r1 = lax.rsqrt(jnp.mean(x * x, axis=0) + NORM_EPS)
    n1 = (x * r1 * gain_one[:, None]).astype(BF16)
    qkv = mm(qkv_own, n1, TN).astype(BF16)
    later_in = after(w_in, tok_low)
    in_places = ((0, 0), (2, 0), (2, half), (3, 0), (1, 0))
    in_held = [lane_cut(later_in, hidden_width, 0), in_first, in_second]
    for k in (3, 1):
        in_held.append(send(after(lane_cut(later_in, hidden_width, k), qkv), k))
    qkv, n1, qkv_own = lax.optimization_barrier((qkv, n1, qkv_own))
    q, k, v = qkv[:part], qkv[part : 2 * part], qkv[2 * part :]
    table = lax.dynamic_slice_in_dim(jnp.transpose(bias_table), me * heads, heads, 0)
    table = jnp.pad(
        table, ((0, 8 - heads), (0, LANES - buckets)), constant_values=NEG_FILL
    )
    o32, p = attend(q, k, v, idx, table, heads, 256)
    expert_at = lambda a: swap(a.reshape(cols, CAPACITY, width), "col").reshape(slots, width)
    dy_low = mm(choose, cot_low, NT).astype(BF16)
    o_low = after(o32.astype(BF16), in_held[3])
    dy_slots = expert_at(dy_low)
    o_far = send(o_low, 2)
    o_full = row_join(o_low, o_far).reshape(width, seq_len)
    out_gathered = after(out_gathered, o32)
    out_rows = jnp.transpose(out_gathered[:, :, :out_cols], (1, 0, 2)).reshape(part, width)
    router_rows = jnp.transpose(out_gathered[:, :, out_cols:], (1, 0, 2)).reshape(part, experts)
    out_router = jnp.concatenate([out_rows, router_rows], axis=1)
    out_router = row_gather(out_router).reshape(width, width + experts)
    out_full, router_full = out_router[:, :width], out_router[:, width:]
    eout_two = send(after(eout_cuts[2], o_far), 2)
    eout_one = send(after(eout_cuts[1], o_full), 1)
    eout_three = send(after(eout_cuts[3], o_full), 3)
    eout_held = [eout_cuts[0], eout_one, eout_two, eout_three]
    h1 = x + mm(out_full, o_full, TN)
    r2 = lax.rsqrt(jnp.mean(h1 * h1, axis=0) + NORM_EPS)
    n2 = (h1 * r2 * gain_two[:, None]).astype(BF16)
    logits = mm(router_full, n2, TN)
    g = jax.nn.softmax(logits, axis=0)
    gate = jnp.sum(g * picked_float, axis=0)

    n2_low = mm(choose, n2, NT).astype(BF16)
    slots_in = expert_at(after(n2_low, eout_two))
    place = jnp.stack([me, col * rows + me]).astype(I32)
    dys, hidden, slope, eout_pieces = expert_inner(
        place, slots_in, dy_slots, router_full, in_held, in_places, rows
    )
    hidden = after(hidden, *eout_pieces)
    back, in_pieces = expert_outer(
        place, slots_in, dys, hidden, slope, in_held, in_places, eout_held
    )
    eout_half = w_expert_out.shape[0] // 2
    grad_eout_half = send(eout_pieces[2][:eout_half], 2)
    back = after(back, grad_eout_half)
    grad_eout_held = [
        eout_pieces[0],
        send(after(eout_pieces[1], back), 1),
        send(after(eout_pieces[2][eout_half:], back), 2),
        send(after(eout_pieces[3], back), 3),
    ]
    home = swap(back.reshape(cols, CAPACITY, 2 * width), "col").reshape(slots, 2 * width)

    h1_s = mm(choose, h1.astype(BF16), NT).astype(BF16)
    h1_own = own_rows(h1, me, part)
    home = after(home, grad_eout_held[2], h1_own)
    scalars = lax.dot_general(
        choose.astype(F32),
        jnp.concatenate([g, gate[None], r2[None]], axis=0),
        NT,
        precision=lax.Precision.HIGHEST,
        preferred_element_type=F32,
    )
    parcel, gain_two_part = slot_work(
        place, home, dy_low, n2_low, h1_s, scalars, router_full, out_full, gain_two[None], rows
    )
    parcel = trade_pieces(after(tuple(parcel), grad_eout_held[3]))
    in_turn = lambda piece: after(piece, parcel[2], parcel[3])
    grad_in_held = [
        in_pieces[0],
        send(in_turn(in_pieces[1]), 1),
        send(in_turn(in_pieces[2]), 2),
    ]
    grad_in_half = send(in_turn(in_pieces[3][:half]), 3)

    layer_out, da, proj_parcel, dn1_parcel = attend_back(
        place,
        q,
        k,
        v,
        idx,
        p,
        o32,
        slot[None],
        h1_own,
        jnp.stack([r1, gate]),
        gain_one[:, None],
        tok_low,
        n1,
        o_full,
        qkv_own,
        gain_two_part,
        parcel,
        cols,
        buckets,
        256,
    )
    dn1_parcel, proj_parcel = after(
        (tuple(dn1_parcel), proj_parcel), grad_in_half, grad_in_held[2]
    )
    dn1_held = trade_pieces(dn1_parcel)
    grad_in_held.append(send(after(in_pieces[3][half:], dn1_held[2], dn1_held[3]), 3))
    dn1_sum = sum(piece.astype(F32) for piece in dn1_held)
    dn1 = dn1_sum[:part]
    inner_one = dn1_sum[part] + dn1_sum[part + 1]
    gain_own = own_rows(gain_one, me, part)
    grad_tokens = (
        da.astype(F32)
        + r1 * gain_own[:, None] * dn1
        - own_rows(x, me, part) * (r1**3 / width * inner_one)
    ).astype(BF16)

    band = width // cols
    proj_sum = jnp.sum(swap(proj_parcel, "col").astype(F32), axis=0)
    half = PAIR_ROWS // 2
    extra_sum = proj_sum[band : band + half] + proj_sum[band + half :]
    router_rows = experts // cols
    grad_router = jnp.transpose(extra_sum[:router_rows, :part])
    small = sum(trade_pieces([extra_sum[router_rows:]] * rows))
    gain_one_grad, gain_two_grad = small[0], small[1]
    table_grad = jnp.transpose(
        small[2:, : LOW_BINS // 2 * LANES]
        .reshape(LOW_BINS, LANES)[:, : bias_table.size // LOW_BINS]
        .reshape(LOW_BINS, all_heads, buckets // LOW_BINS),
        (2, 0, 1),
    ).reshape(bias_table.shape)
    pieces = []
    for turn in range(share):
        moves = [
            (r * cols + c, (c // share) * cols + share * r + (c + turn) % share)
            for r in range(rows)
            for c in range(cols)
        ]
        first = (col + turn) % share * 4 * out_cols
        piece = lax.dynamic_slice_in_dim(proj_sum[:band], first, 4 * out_cols, 1)
        pieces.append(lax.ppermute(piece, ("row", "col"), moves))
    pieces = jnp.stack(pieces)
    grad_four = jnp.concatenate(
        [
            lax.dynamic_index_in_dim(pieces, (col - half) % share, 0, keepdims=False)
            for half in range(share)
        ],
        axis=0,
    )
    grad_query, grad_key, grad_value, grad_out = [
        grad_four[:, w * out_cols : (w + 1) * out_cols] for w in range(4)
    ]
    last = after(grad_in_held[3], proj_sum)
    grad_in_held[3] = jnp.concatenate([grad_in_half, last], axis=0)
    grad_eout_held[2] = jnp.concatenate([grad_eout_half, grad_eout_held[2]], axis=0)
    grad_in, grad_eout = fill_columns(grad_in_held, 2), fill_columns(grad_eout_held, 2)
    return (
        layer_out[None],
        grad_tokens[None],
        gain_one_grad,
        gain_two_grad,
        grad_query,
        grad_key,
        grad_value,
        grad_out,
        grad_router,
        grad_in,
        grad_eout,
        table_grad,
    )


def solution(mesh):
    rows, cols = mesh.shape["row"], mesh.shape["col"]
    paired = rows == 4 and cols == 2 * rows and EXPERTS == rows * cols
    return jax.shard_map(
        expert_plan if paired else general_plan,
        mesh=mesh,
        in_specs=(
            P("col", "row", None),
            P(),
            P(),
            P("row", "col"),
            P("row", "col"),
            P("row", "col"),
            P("row", "col"),
            P("row", "col"),
            P("row", "col"),
            P("row", "col"),
            P(),
            P("col", None),
            P("col", None, None),
            P("col", "row", None),
            P("col", "row", None),
        ),
        out_specs=(
            P("col", "row", None),
            P("col", "row", None),
            P(),
            P(),
            P("row", "col"),
            P("row", "col"),
            P("row", "col"),
            P("row", "col"),
            P("row", "col"),
            P("row", "col"),
            P("row", "col"),
            P(),
        ),
        check_vma=False,
    )
```

```python
import functools

import jax
import jax.numpy as jnp
from jax import lax
from jax.experimental import pallas as pl
from jax.experimental.pallas import tpu as pltpu
from jax.sharding import PartitionSpec as P

EXPERTS = 32
CAPACITY = 48


NORM_EPS = 1e-06
NEG_FILL = -1e30


def row_totals(partial_values):
    return lax.psum(partial_values, "row")


def feature_split(partial_rows):
    return lax.psum_scatter(partial_rows, "row", scatter_dimension=1, tiled=True)


def feature_join(rows_low):
    return lax.all_gather(rows_low, "row", axis=1, tiled=True)


def norm_back(grad_normed, inputs_f, inverse_rms, gain_part, model_width):
    inner_sum = row_totals(jnp.sum(gain_part * grad_normed * inputs_f, axis=1))
    return (
        inverse_rms[:, None] * gain_part * grad_normed
        - inputs_f * (inverse_rms**3 / model_width * inner_sum)[:, None]
    )


def block_scores(
    query_heads, keys_all, bucket_rows, query_docs, doc_ids, bias_table, number, key_block
):
    head_count = bias_table.shape[1]
    head_dim = query_heads.shape[2]
    offset = number * key_block
    key_rows = lax.dynamic_slice_in_dim(keys_all, offset, key_block, 0).reshape(
        key_block, head_count, head_dim
    )
    bucket_cols = lax.dynamic_slice_in_dim(bucket_rows, offset, key_block, 1)
    key_docs = lax.dynamic_slice_in_dim(doc_ids, offset, key_block, 0)
    raw_scores = jnp.einsum(
        "ihd,jhd->hij", query_heads, key_rows, preferred_element_type=jnp.float32
    ) * head_dim ** (-0.5)
    one_hot = (bucket_cols[:, :, None] == jnp.arange(bias_table.shape[0], dtype=jnp.int32)).astype(
        jnp.float32
    )
    pair_bias = jnp.einsum("ijb,bh->hij", one_hot, bias_table, precision=lax.Precision.HIGHEST)
    allowed = (query_docs[:, None] == key_docs[None, :])[None]
    return (raw_scores + pair_bias, allowed, one_hot)


def attend_blocks(query_heads, keys_all, values_all, bucket_rows, query_docs, doc_ids, bias_table):
    tok_rows, head_count, head_dim = query_heads.shape
    seq_len = keys_all.shape[0]
    key_block = min(seq_len, 512)
    blocks = seq_len // key_block

    def first_pass(status, number):
        row_peak, row_total = status
        scores, allowed, one_hot = block_scores(
            query_heads, keys_all, bucket_rows, query_docs, doc_ids, bias_table, number, key_block
        )
        masked = jnp.where(allowed, scores, NEG_FILL)
        new_peak = jnp.maximum(row_peak, jnp.max(masked, axis=2))
        weights = jnp.where(allowed, jnp.exp(masked - new_peak[:, :, None]), 0.0)
        row_total = row_total * jnp.exp(row_peak - new_peak) + jnp.sum(weights, axis=2)
        return ((new_peak, row_total), None)

    start_status = (
        jnp.full((head_count, tok_rows), NEG_FILL, jnp.float32),
        jnp.zeros((head_count, tok_rows), jnp.float32),
    )
    (row_peak, row_total), unused = lax.scan(first_pass, start_status, jnp.arange(blocks))
    log_total = row_peak + jnp.log(row_total)

    def second_pass(running, number):
        scores, allowed, one_hot = block_scores(
            query_heads, keys_all, bucket_rows, query_docs, doc_ids, bias_table, number, key_block
        )
        soft_weights = jnp.where(allowed, jnp.exp(scores - log_total[:, :, None]), 0.0).astype(
            jnp.bfloat16
        )
        value_rows = lax.dynamic_slice_in_dim(values_all, number * key_block, key_block, 0).reshape(
            key_block, head_count, head_dim
        )
        return (
            running
            + jnp.einsum(
                "hij,jhd->ihd", soft_weights, value_rows, preferred_element_type=jnp.float32
            ),
            None,
        )

    start_acc = jnp.zeros((tok_rows, head_count, head_dim), jnp.float32)
    attended, unused = lax.scan(second_pass, start_acc, jnp.arange(blocks))
    return (attended, log_total)


def attend_blocks_back(
    query_heads,
    keys_all,
    values_all,
    bucket_rows,
    query_docs,
    doc_ids,
    bias_table,
    log_total,
    grad_heads,
    grad_dot,
):
    tok_rows, head_count, head_dim = query_heads.shape
    seq_len = keys_all.shape[0]
    model_width = head_count * head_dim
    key_block = min(seq_len, 512)
    blocks = seq_len // key_block
    scaling = head_dim ** (-0.5)

    def step_back(status, number):
        grad_query, grad_table = status
        scores, allowed, one_hot = block_scores(
            query_heads, keys_all, bucket_rows, query_docs, doc_ids, bias_table, number, key_block
        )
        key_rows = lax.dynamic_slice_in_dim(keys_all, number * key_block, key_block, 0).reshape(
            key_block, head_count, head_dim
        )
        value_rows = lax.dynamic_slice_in_dim(values_all, number * key_block, key_block, 0).reshape(
            key_block, head_count, head_dim
        )
        soft_weights = jnp.where(allowed, jnp.exp(scores - log_total[:, :, None]), 0.0)
        weights_low = soft_weights.astype(jnp.bfloat16)
        grad_soft = jnp.einsum(
            "ihd,jhd->hij", grad_heads, value_rows, preferred_element_type=jnp.float32
        )
        grad_scores = soft_weights * (grad_soft - grad_dot[:, :, None])
        grad_table = grad_table + jnp.einsum(
            "ijb,hij->bh", one_hot, grad_scores, precision=lax.Precision.HIGHEST
        )
        scores_low = grad_scores.astype(jnp.bfloat16)
        grad_query = grad_query + scaling * jnp.einsum(
            "hij,jhd->ihd", scores_low, key_rows, preferred_element_type=jnp.float32
        )
        grad_key = scaling * jnp.einsum(
            "hij,ihd->jhd", scores_low, query_heads, preferred_element_type=jnp.float32
        )
        grad_value = jnp.einsum(
            "hij,ihd->jhd", weights_low, grad_heads, preferred_element_type=jnp.float32
        )
        stacked = jnp.concatenate(
            [grad_key.reshape(key_block, model_width), grad_value.reshape(key_block, model_width)],
            axis=1,
        )
        return ((grad_query, grad_table), stacked)

    start_status = (
        jnp.zeros((tok_rows, head_count, head_dim), jnp.float32),
        jnp.zeros(bias_table.shape, jnp.float32),
    )
    (grad_query, grad_table), kv_terms = lax.scan(step_back, start_status, jnp.arange(blocks))
    return (grad_query, grad_table, kv_terms.reshape(seq_len, 2 * model_width))


def general_plan(
    tokens,
    gain_one,
    gain_two,
    w_query,
    w_key,
    w_value,
    w_out,
    w_router,
    w_in,
    w_expert_out,
    bias_table,
    segment,
    expert,
    bucket,
    cotangent,
):
    seq_len = tokens.shape[2]
    dim_rows = tokens.shape[1]
    row_count = lax.axis_size("row")
    model_width = dim_rows * row_count
    tok_rows = seq_len // row_count
    experts = EXPERTS
    hid_rows = w_expert_out.shape[0]
    ffn_width = hid_rows * row_count
    head_count = bias_table.shape[1]
    head_dim = model_width // head_count
    row_index = lax.axis_index("row")
    gathered = (
        lax.all_gather(w_query, "col", axis=1, tiled=True),
        lax.all_gather(w_key, "col", axis=1, tiled=True),
        lax.all_gather(w_value, "col", axis=1, tiled=True),
        lax.all_gather(w_out, "col", axis=1, tiled=True),
        lax.all_gather(w_router, "col", axis=1, tiled=True),
        lax.all_gather(w_in, "col", axis=1, tiled=True),
        lax.all_gather(w_expert_out, "col", axis=1, tiled=True),
    )
    query_full, key_full, value_full, out_proj_full, router_full, in_flat, out_flat = gathered
    in_full = in_flat.reshape(dim_rows, experts, ffn_width)
    out_full = out_flat.reshape(hid_rows, experts, model_width)
    stacked_weights = jnp.concatenate([query_full, key_full, value_full], axis=1)
    tok_float = jnp.transpose(tokens[0].astype(jnp.float32))
    doc_ids = segment[0]
    query_docs = lax.dynamic_slice_in_dim(doc_ids, row_index * tok_rows, tok_rows, 0)
    bucket_rows = bucket[0]
    expert_ids = expert[0, :, 0]
    gain_part_one = lax.dynamic_slice_in_dim(gain_one, row_index * dim_rows, dim_rows, 0)
    gain_part_two = lax.dynamic_slice_in_dim(gain_two, row_index * dim_rows, dim_rows, 0)
    inverse_one = lax.rsqrt(
        row_totals(jnp.sum(tok_float * tok_float, axis=1)) / model_width + NORM_EPS
    )
    normed_one = (tok_float * inverse_one[:, None] * gain_part_one).astype(jnp.bfloat16)
    projected = lax.psum_scatter(
        jnp.dot(normed_one, stacked_weights, preferred_element_type=jnp.float32),
        "row",
        scatter_dimension=0,
        tiled=True,
    ).astype(jnp.bfloat16)
    queries_low = projected[:, :model_width]
    keys_low = projected[:, model_width : 2 * model_width]
    values_low = projected[:, 2 * model_width :]
    keys_all, values_all = (
        lax.all_gather(keys_low, "row", axis=0, tiled=True),
        lax.all_gather(values_low, "row", axis=0, tiled=True),
    )
    query_heads = queries_low.reshape(tok_rows, head_count, head_dim)
    attended, log_total = attend_blocks(
        query_heads, keys_all, values_all, bucket_rows, query_docs, doc_ids, bias_table
    )
    attn_low = attended.reshape(tok_rows, model_width).astype(jnp.bfloat16)
    heads_home = lax.all_to_all(attn_low, "row", split_axis=1, concat_axis=0, tiled=True)
    attn_rows = feature_split(
        jnp.dot(heads_home, out_proj_full, preferred_element_type=jnp.float32)
    )
    residual = tok_float + attn_rows
    inverse_two = lax.rsqrt(
        row_totals(jnp.sum(residual * residual, axis=1)) / model_width + NORM_EPS
    )
    normed_two = (residual * inverse_two[:, None] * gain_part_two).astype(jnp.bfloat16)
    logits = row_totals(jnp.dot(normed_two, router_full, preferred_element_type=jnp.float32))
    gate_probs = jax.nn.softmax(logits, axis=1)
    picked = (expert_ids[:, None] == jnp.arange(experts, dtype=jnp.int32)[None, :]).astype(
        jnp.int32
    )
    picked_float = picked.astype(jnp.float32)
    slot_rank = jnp.sum((jnp.cumsum(picked, axis=0) - 1) * picked, axis=1)
    slot_index = expert_ids * CAPACITY + slot_rank
    token_gate = jnp.sum(gate_probs * picked_float, axis=1)
    slots_in = (
        jnp.zeros((experts * CAPACITY, dim_rows), jnp.bfloat16).at[slot_index].set(normed_two)
    )
    slots_own = slots_in.reshape(experts, CAPACITY, dim_rows)
    lead_count = slots_own.shape[0]
    slot_count = slots_own.shape[1]
    pre_partial = jnp.einsum("ecd,def->ecf", slots_own, in_full, preferred_element_type=jnp.float32)
    pre_act = feature_split(pre_partial.reshape(lead_count * slot_count, ffn_width))
    hidden = jax.nn.gelu(pre_act).astype(jnp.bfloat16)
    hidden_three = hidden.reshape(lead_count, slot_count, hid_rows)
    out_partial = jnp.einsum(
        "ecf,fed->ecd", hidden_three, out_full, preferred_element_type=jnp.float32
    )
    expert_local = feature_split(out_partial.reshape(lead_count * slot_count, model_width))
    expert_tok = expert_local[slot_index]
    layer_out = (residual + token_gate[:, None] * expert_tok).astype(jnp.bfloat16)
    grad_final = jnp.transpose(cotangent[0].astype(jnp.float32))
    grad_gate = row_totals(jnp.sum(grad_final * expert_tok, axis=1))
    grad_expert_tok = (token_gate[:, None] * grad_final).astype(jnp.bfloat16)
    grad_slots = (
        jnp.zeros((experts * CAPACITY, dim_rows), jnp.bfloat16).at[slot_index].set(grad_expert_tok)
    )
    grad_slots_local = grad_slots.reshape(experts, CAPACITY, dim_rows)
    grad_slots_full = feature_join(
        grad_slots_local.reshape(lead_count * slot_count, dim_rows)
    ).reshape(lead_count, slot_count, model_width)
    grad_hidden = jnp.einsum(
        "ecd,fed->ecf", grad_slots_full, out_full, preferred_element_type=jnp.float32
    )
    grad_out_weight = jnp.einsum(
        "ecf,ecd->fed", hidden_three, grad_slots_full, preferred_element_type=jnp.float32
    )
    unused, gelu_back = jax.vjp(jax.nn.gelu, pre_act)
    grad_pre = gelu_back(grad_hidden.reshape(lead_count * slot_count, hid_rows))[0].astype(
        jnp.bfloat16
    )
    grad_pre_full = feature_join(grad_pre).reshape(lead_count, slot_count, ffn_width)
    grad_slots_in = jnp.einsum(
        "ecf,def->ecd", grad_pre_full, in_full, preferred_element_type=jnp.float32
    )
    grad_in_weight = jnp.einsum(
        "ecd,ecf->def", slots_own, grad_pre_full, preferred_element_type=jnp.float32
    )
    grad_logits = ((grad_gate * token_gate)[:, None] * (picked_float - gate_probs)).astype(
        jnp.bfloat16
    )
    router_back = lax.dot_general(
        grad_logits, router_full, (((1,), (1,)), ((), ())), preferred_element_type=jnp.float32
    )
    grad_normed_two = grad_slots_in.reshape(experts * CAPACITY, dim_rows)[slot_index] + router_back
    grad_router = lax.dot_general(
        normed_two, grad_logits, (((0,), (0,)), ((), ())), preferred_element_type=jnp.float32
    )
    grad_res = grad_final + norm_back(
        grad_normed_two, residual, inverse_two, gain_part_two, model_width
    )
    grad_gain_two = jnp.sum(grad_normed_two * residual * inverse_two[:, None], axis=0)
    grad_attn_full = feature_join(grad_res.astype(jnp.bfloat16))
    grad_heads_home = lax.dot_general(
        grad_attn_full, out_proj_full, (((1,), (1,)), ((), ())), preferred_element_type=jnp.float32
    ).astype(jnp.bfloat16)
    grad_out_proj = lax.dot_general(
        heads_home, grad_attn_full, (((0,), (0,)), ((), ())), preferred_element_type=jnp.float32
    )
    grad_attn = lax.all_to_all(grad_heads_home, "row", split_axis=0, concat_axis=1, tiled=True)
    grad_heads = grad_attn.reshape(tok_rows, head_count, head_dim)
    grad_dot = jnp.einsum("ihd,ihd->hi", grad_heads.astype(jnp.float32), attended)
    grad_query, grad_table, kv_terms = attend_blocks_back(
        query_heads,
        keys_all,
        values_all,
        bucket_rows,
        query_docs,
        doc_ids,
        bias_table,
        log_total,
        grad_heads,
        grad_dot,
    )
    key_value_grads = lax.psum_scatter(kv_terms, "row", scatter_dimension=0, tiled=True)
    grad_qkv = jnp.concatenate(
        [
            grad_query.reshape(tok_rows, model_width).astype(jnp.bfloat16),
            key_value_grads.astype(jnp.bfloat16),
        ],
        axis=1,
    )
    portion = lax.all_gather(grad_qkv, "row", axis=0, tiled=True)
    grad_part = lax.dot_general(
        portion, stacked_weights, (((1,), (1,)), ((), ())), preferred_element_type=jnp.float32
    )
    grad_weights = lax.dot_general(
        normed_one, portion, (((0,), (0,)), ((), ())), preferred_element_type=jnp.float32
    )
    grad_input = grad_res + norm_back(grad_part, tok_float, inverse_one, gain_part_one, model_width)
    grad_gain_one = jnp.sum(grad_part * tok_float * inverse_one[:, None], axis=0)
    summed = (
        lax.psum_scatter(grad_weights[:, :model_width], "col", scatter_dimension=1, tiled=True),
        lax.psum_scatter(
            grad_weights[:, model_width : 2 * model_width], "col", scatter_dimension=1, tiled=True
        ),
        lax.psum_scatter(
            grad_weights[:, 2 * model_width :], "col", scatter_dimension=1, tiled=True
        ),
        lax.psum_scatter(grad_out_proj, "col", scatter_dimension=1, tiled=True),
        lax.psum_scatter(grad_router, "col", scatter_dimension=1, tiled=True),
        lax.psum_scatter(
            grad_in_weight.reshape(dim_rows, experts * ffn_width),
            "col",
            scatter_dimension=1,
            tiled=True,
        ),
        lax.psum_scatter(
            grad_out_weight.reshape(hid_rows, experts * model_width),
            "col",
            scatter_dimension=1,
            tiled=True,
        ),
    )
    grad_query_w, grad_key_w, grad_value_w, grad_out_w, grad_router_w, grad_in_w, grad_expert_w = (
        summed
    )
    place_one = lax.dynamic_update_slice_in_dim(
        jnp.zeros((model_width,), jnp.float32), grad_gain_one, row_index * dim_rows, 0
    )
    place_two = lax.dynamic_update_slice_in_dim(
        jnp.zeros((model_width,), jnp.float32), grad_gain_two, row_index * dim_rows, 0
    )
    gain_one_grad, gain_two_grad, table_grad = lax.psum(
        (place_one, place_two, grad_table), ("row", "col")
    )
    layer_out_t = jnp.transpose(layer_out)[None]
    grad_input_t = jnp.transpose(grad_input.astype(jnp.bfloat16))[None]
    return (
        layer_out_t,
        grad_input_t,
        gain_one_grad,
        gain_two_grad,
        grad_query_w,
        grad_key_w,
        grad_value_w,
        grad_out_w,
        grad_router_w,
        grad_in_w,
        grad_expert_w,
        table_grad,
    )


BF16 = jnp.bfloat16
F32 = jnp.float32
I32 = jnp.int32
NT = (((1,), (1,)), ((), ()))
NN = (((1,), (0,)), ((), ()))
TN = (((0,), (0,)), ((), ()))
LANES = 128
PAIR_ROWS = 16
LOW_BINS = 8
GELU_SCALE = 0.7978845608028654
GELU_CUBE = 0.044715
QUICK = pl.CostEstimate(flops=0, bytes_accessed=0, transcendentals=0)


def mm(left, right, dims):
    return lax.dot_general(left, right, dims, preferred_element_type=F32)


def two_parts(values):
    high = values.astype(BF16)
    return high, (values - high.astype(F32)).astype(BF16)


def attend_kernel(heads, head_dim, q_ref, k_ref, v_ref, idx_ref, tab_ref, o_ref, p_ref):
    rows, keys = idx_ref.shape
    idx = idx_ref[...].astype(F32).astype(I32)
    for h in range(heads):
        span = slice(h * head_dim, (h + 1) * head_dim)
        table = jnp.broadcast_to(tab_ref[h : h + 1, :], (rows, LANES))
        bias = jnp.concatenate(
            [
                jnp.take_along_axis(table, idx[:, c : c + LANES], axis=1)
                for c in range(0, keys, LANES)
            ],
            axis=1,
        )
        scores = mm(q_ref[span, :], k_ref[span, :], TN) * head_dim**-0.5 + bias
        weights = jnp.exp(scores - jnp.max(scores, axis=1, keepdims=True))
        soft = (weights * (1.0 / jnp.sum(weights, axis=1, keepdims=True))).astype(BF16)
        p_ref[h] = soft
        o_ref[span, :] = mm(v_ref[span, :], soft, NT)


def attend(q, k, v, idx, tab, heads, tile):
    width, keys = q.shape
    whole = lambda a: pl.BlockSpec(a.shape, lambda i: (0, 0))
    return pl.pallas_call(
        functools.partial(attend_kernel, heads, width // heads),
        grid=(keys // tile,),
        in_specs=[
            pl.BlockSpec((width, tile), lambda i: (0, i)),
            whole(k),
            whole(v),
            pl.BlockSpec((tile, keys), lambda i: (i, 0)),
            whole(tab),
        ],
        out_specs=[
            pl.BlockSpec((width, tile), lambda i: (0, i)),
            pl.BlockSpec((heads, tile, keys), lambda i: (0, i, 0)),
        ],
        out_shape=[
            jax.ShapeDtypeStruct((width, keys), F32),
            jax.ShapeDtypeStruct((heads, keys, keys), BF16),
        ],
        compiler_params=pltpu.CompilerParams(vmem_limit_bytes=48 * 2**20),
        cost_estimate=QUICK,
    )(q, k, v, idx, tab)


def back_kernel(
    heads,
    count,
    experts,
    cols,
    place_ref,
    q_ref,
    k_ref,
    v_ref,
    idx_ref,
    p_ref,
    o_ref,
    slot_ref,
    h1_ref,
    row_ref,
    col_ref,
    x_ref,
    n1_ref,
    ofull_ref,
    w_ref,
    gain_two_ref,
    *refs,
):
    pieces = refs[:count]
    layer_ref, da_ref, proj_ref = refs[count : count + 3]
    dn1_refs = refs[count + 3 : 2 * count + 3]
    g_aug, v_aug, dqkv, dk_acc, dv_acc, hist, router_acc, dn1_acc = refs[2 * count + 3 :]
    step, steps = pl.program_id(0), pl.num_programs(0)
    me = place_ref[0]
    part, tile = q_ref.shape
    keys = k_ref.shape[1]
    head_dim = part // heads
    aug = g_aug.shape[0] // heads
    width = x_ref.shape[0]
    slots = pieces[0].shape[0]
    scale = head_dim**-0.5

    @pl.when(step == 0)
    def _():
        dk_acc[...] = jnp.zeros_like(dk_acc)
        dv_acc[...] = jnp.zeros_like(dv_acc)
        hist[...] = jnp.zeros_like(hist)
        placed = jnp.zeros((3 * part, keys), F32)
        router = jnp.zeros((part, 2 * experts), F32)
        slot_row = lax.broadcasted_iota(I32, (slots, keys), 0)
        for k in range(count):
            spread = jnp.where(slot_row + (me ^ k) * slots == slot_ref[...], 1.0, 0.0).astype(BF16)
            placed = placed + mm(pieces[k][:, : 3 * part], spread, TN)
            router = router + pieces[k][:part, 3 * part :].astype(F32)
        router_acc[...] = router[:, :experts] + router[:, experts:]
        layer_ref[...] = (h1_ref[...] + row_ref[1:2, :] * placed[:part]).astype(BF16)
        da_ref[...] = placed[part : 2 * part].astype(BF16)
        fill = jnp.zeros((PAIR_ROWS - 2, keys), F32)
        ones = jnp.concatenate([jnp.ones((2, keys), F32), fill], axis=0).astype(BF16)
        for h in range(heads):
            span = slice(h * head_dim, (h + 1) * head_dim)
            do = placed[2 * part + h * head_dim : 2 * part + (h + 1) * head_dim]
            delta = jnp.sum(do * o_ref[span, :], axis=0, keepdims=True)
            high = delta.astype(BF16).astype(F32)
            rest = jnp.concatenate([-high, high - delta, fill], axis=0).astype(BF16)
            g_aug[h * aug : h * aug + head_dim, :] = do.astype(BF16)
            g_aug[h * aug + head_dim : (h + 1) * aug, :] = rest
            v_aug[h * aug : h * aug + head_dim, :] = v_ref[span, :]
            v_aug[h * aug + head_dim : (h + 1) * aug, :] = ones

    lanes = pl.ds(pl.multiple_of(step * tile, tile), tile)
    slopes = []
    for h in range(heads):
        span = slice(h * head_dim, (h + 1) * head_dim)
        soft = p_ref[h]
        g_part = g_aug[h * aug : (h + 1) * aug, lanes]
        diff = mm(g_part, v_aug[h * aug : (h + 1) * aug, :], TN)
        slope = (soft.astype(F32) * diff).astype(BF16)
        slopes.append(slope)
        dqkv[span, lanes] = (mm(k_ref[span, :], slope, NT) * scale).astype(BF16)
        dk_acc[span, :] += mm(q_ref[span, :], slope, NN) * scale
        dv_acc[span, :] += mm(g_part[:head_dim], soft, NN)
    idx = idx_ref[...].astype(F32).astype(I32)
    high = (idx // LOW_BINS).astype(F32).astype(BF16)
    low = (idx % LOW_BINS).astype(F32).astype(BF16)
    high_bins = hist.shape[1] // (heads * PAIR_ROWS)
    one = jnp.ones((), BF16)
    zero = jnp.zeros((), BF16)
    total = hist[...]
    for s in range(0, tile, PAIR_ROWS):
        rows = slice(s, s + PAIR_ROWS)
        left = jnp.concatenate(
            [jnp.where(low[rows] == n, one, zero) for n in range(LOW_BINS)], axis=0
        )
        right = jnp.concatenate(
            [
                jnp.where(high[rows] == n, slopes[h][rows], zero)
                for h in range(heads)
                for n in range(high_bins)
            ],
            axis=0,
        )
        total = total + mm(left, right, NT)
    hist[...] = total

    @pl.when(step == steps - 1)
    def _():
        dqkv[part : 2 * part, :] = dk_acc[...].astype(BF16)
        dqkv[2 * part :, :] = dv_acc[...].astype(BF16)
        r1 = row_ref[0:1, :]
        inner = jnp.zeros((1, keys), F32)
        gain_rows = []
        for d in range(count):
            rows = slice(d * part, (d + 1) * part)
            dn1 = mm(w_ref[rows, :], dqkv[...], NN)
            dn1_acc[d] = dn1.astype(BF16)
            dn1_x = dn1 * x_ref[rows, :].astype(F32)
            inner = inner + jnp.sum(dn1_x * col_ref[rows, :], axis=0, keepdims=True)
            gain = jnp.sum(dn1_x * r1, axis=1, keepdims=True)
            gain_rows.append(jnp.transpose(jnp.broadcast_to(gain, (part, LANES)))[:1])
        cells = hist[...]
        same = lax.broadcasted_iota(I32, cells.shape, 0) % PAIR_ROWS == (
            lax.broadcasted_iota(I32, cells.shape, 1) % PAIR_ROWS
        )
        cells = jnp.where(same, cells, 0.0)
        low_rows = (LOW_BINS, cells.shape[0])
        sum_rows = jnp.where(
            lax.broadcasted_iota(I32, low_rows, 1) // PAIR_ROWS
            == lax.broadcasted_iota(I32, low_rows, 0),
            1.0,
            0.0,
        )
        lane_cols = (cells.shape[1], LANES)
        bins = heads * high_bins
        sum_cols = jnp.where(
            lax.broadcasted_iota(I32, lane_cols, 0) // PAIR_ROWS + me * bins
            == lax.broadcasted_iota(I32, lane_cols, 1),
            1.0,
            0.0,
        )
        exact = functools.partial(
            lax.dot_general,
            dimension_numbers=NN,
            precision=lax.Precision.HIGHEST,
            preferred_element_type=F32,
        )
        table = exact(exact(sum_rows, cells), sum_cols)
        half = LOW_BINS // 2
        tail = jnp.zeros((1, width - half * LANES), F32)
        table_rows = [
            jnp.concatenate([table[n + m : n + m + 1] for m in range(half)] + [tail], axis=1)
            for n in (0, half)
        ]
        small = jnp.concatenate(
            [jnp.concatenate(gain_rows, axis=1), gain_two_ref[...]] + table_rows, axis=0
        )
        inner_high = inner.astype(BF16).astype(F32)
        extra = jnp.concatenate(
            [inner_high, inner - inner_high, jnp.zeros((PAIR_ROWS - 2, keys), F32)], axis=0
        ).astype(BF16)
        for k in range(count):
            dn1_refs[k][:part, :] = dn1_acc[me ^ k]
            dn1_refs[k][part:, :] = extra
        router = jnp.transpose(router_acc[...])
        band = width // cols
        share = experts // cols
        pad = jnp.zeros((share, width - part), F32)
        pieces_of = lambda a, first: a[first : first + band, :]
        halves = part // band
        for b in range(halves):
            three = jnp.concatenate(
                [pieces_of(dqkv, w * part + b * band) for w in range(3)], axis=0
            )
            da_part = pieces_of(da_ref, b * band)
            for c in range(cols):
                rows = slice(c * band, (c + 1) * band)
                proj_ref[c, :band, b * 4 * band : (b + 1) * 4 * band] = jnp.concatenate(
                    [mm(n1_ref[rows, :], three, NT), mm(ofull_ref[rows, :], da_part, NT)], axis=1
                ).astype(BF16)
        for c in range(cols):
            own = jnp.concatenate([router[c * share : (c + 1) * share], pad], axis=1)
            facts = jnp.concatenate([own, small], axis=0)
            facts_high = facts.astype(BF16).astype(F32)
            proj_ref[c, band:, :] = jnp.concatenate(
                [facts_high, facts - facts_high], axis=0
            ).astype(BF16)


def attend_back(
    place, q, k, v, idx, p, o, slot, h1, row_facts, gain, x, n1, o_full, w, gain_two, pieces, cols, buckets, tile
):
    part, keys = q.shape
    width = x.shape[0]
    count = len(pieces)
    heads = p.shape[0]
    experts = (pieces[0].shape[1] - 3 * part) // 2
    aug_width = part + heads * PAIR_ROWS
    hist_shape = (LOW_BINS * PAIR_ROWS, heads * (buckets // LOW_BINS) * PAIR_ROWS)
    fixed = lambda a: pl.BlockSpec(a.shape, lambda i, m: (0,) * len(a.shape))
    outs = [
        jax.ShapeDtypeStruct((part, keys), BF16),
        jax.ShapeDtypeStruct((part, keys), BF16),
        jax.ShapeDtypeStruct((cols, width // cols + PAIR_ROWS, width), BF16),
    ] + [jax.ShapeDtypeStruct((part + PAIR_ROWS, keys), BF16)] * count
    rest = (o, slot, h1, row_facts, gain, x, n1, o_full, w, gain_two, *pieces)
    out = pl.pallas_call(
        functools.partial(back_kernel, heads, count, experts, cols),
        grid_spec=pltpu.PrefetchScalarGridSpec(
            num_scalar_prefetch=1,
            grid=(keys // tile,),
            in_specs=[
                pl.BlockSpec((part, tile), lambda i, m: (0, i)),
                fixed(k),
                fixed(v),
                pl.BlockSpec((tile, keys), lambda i, m: (i, 0)),
                pl.BlockSpec((heads, tile, keys), lambda i, m: (0, i, 0)),
            ]
            + [fixed(a) for a in rest],
            out_specs=[fixed(a) for a in outs],
            scratch_shapes=[
                pltpu.VMEM((aug_width, keys), BF16),
                pltpu.VMEM((aug_width, keys), BF16),
                pltpu.VMEM((3 * part, keys), BF16),
                pltpu.VMEM((part, keys), F32),
                pltpu.VMEM((part, keys), F32),
                pltpu.VMEM(hist_shape, F32),
                pltpu.VMEM((part, experts), F32),
                pltpu.VMEM((count, part, keys), BF16),
            ],
        ),
        out_shape=outs,
        compiler_params=pltpu.CompilerParams(vmem_limit_bytes=56 * 2**20),
        cost_estimate=QUICK,
    )(place, q, k, v, idx, p, *rest)
    return out[0], out[1], out[2], out[3:]


def fill_rows(place_ref, places, in_refs, win, part):
    for in_ref, (k, offset) in zip(in_refs, places):
        first = pl.multiple_of((place_ref[0] ^ k) * part + offset, PAIR_ROWS)
        win[pl.ds(first, in_ref.shape[0]), :] = in_ref[...]


def inner_kernel(count, places, ge_places, place_ref, x_ref, dy_ref, router_ref, *refs):
    in_refs, refs = refs[: len(places)], refs[len(places) :]
    dys_ref, hidden_ref, slope_ref = refs[:3]
    ge_refs, win = refs[3:-1], refs[-1]
    step = pl.program_id(0)

    @pl.when(step == 0)
    def _():
        logits = mm(x_ref[...], router_ref[...], NN)
        probs = jnp.exp(logits - jnp.max(logits, axis=1, keepdims=True))
        own = lax.broadcasted_iota(I32, logits.shape, 1) == place_ref[1]
        gate = jnp.sum(jnp.where(own, probs, 0.0), axis=1, keepdims=True)
        gate = gate / jnp.sum(probs, axis=1, keepdims=True)
        dys_ref[...] = (gate * dy_ref[...].astype(F32)).astype(BF16)

    fill_rows(place_ref, places, in_refs, win, win.shape[0] // count)
    pre = mm(x_ref[...], win[...], NN)
    square = pre * pre
    curve = jnp.tanh(GELU_SCALE * pre * (1.0 + GELU_CUBE * square))
    half = 0.5 * (1.0 + curve)
    hidden = (pre * half).astype(BF16)
    hidden_ref[...] = hidden
    slope = half + 0.5 * pre * (1.0 - curve * curve) * (
        GELU_SCALE * (1.0 + 3.0 * GELU_CUBE * square)
    )
    slope_ref[...] = slope.astype(BF16)
    ge = mm(hidden, dys_ref[...], TN).astype(BF16)
    for ge_ref, (k, first, size) in zip(ge_refs, ge_places):

        @pl.when(step == k)
        def _(ge_ref=ge_ref, first=first, size=size):
            ge_ref[...] = ge[first : first + size]


def outer_kernel(
    count, places, eout_places, place_ref, x_ref, dys_ref, hidden_ref, slope_ref, *refs
):
    in_refs, refs = refs[: len(places)], refs[len(places) :]
    eout_refs, refs = refs[: len(eout_places)], refs[len(eout_places) :]
    back_ref, gi_refs = refs[0], refs[1 : count + 1]
    win, eout, y_acc, dx_acc, gi = refs[count + 1 :]
    step = pl.program_id(0)
    part = gi_refs[0].shape[0]

    @pl.when(step == 0)
    def _():
        y_acc[...] = jnp.zeros_like(y_acc)
        dx_acc[...] = jnp.zeros_like(dx_acc)

    fill_rows(place_ref, places, in_refs, win, part)
    for eout_ref, (k, first) in zip(eout_refs, eout_places):

        @pl.when(step == k)
        def _(eout_ref=eout_ref, first=first):
            eout[first : first + eout_ref.shape[0], :] = eout_ref[...]

    y_acc[...] += mm(hidden_ref[...], eout[...], NN)
    dpre = (mm(dys_ref[...], eout[...], NT) * slope_ref[...].astype(F32)).astype(BF16)
    dx_acc[...] += mm(dpre, win[...], NT)
    gi[...] = mm(x_ref[...], dpre, TN).astype(BF16)
    for k in range(count):
        gi_refs[k][...] = gi[pl.ds(pl.multiple_of((place_ref[0] ^ k) * part, part), part), :]

    @pl.when(step == count - 1)
    def _():
        width = y_acc.shape[1]
        back_ref[:, :width] = y_acc[...].astype(BF16)
        back_ref[:, width:] = dx_acc[...].astype(BF16)


def expert_inner(place, x, dy, router, in_held, places, ge_places, count):
    slots, width = x.shape
    hidden_width = in_held[0].shape[1]
    chunk = hidden_width // count
    fixed = lambda shape: pl.BlockSpec(shape, lambda i, m: (0, 0))
    wide = pl.BlockSpec((slots, chunk), lambda i, m: (0, i))
    shape = lambda s: jax.ShapeDtypeStruct(s, BF16)
    out = pl.pallas_call(
        functools.partial(inner_kernel, count, places, ge_places),
        grid_spec=pltpu.PrefetchScalarGridSpec(
            num_scalar_prefetch=1,
            grid=(count,),
            in_specs=[fixed(x.shape), fixed(dy.shape), fixed(router.shape)]
            + [pl.BlockSpec((a.shape[0], chunk), lambda i, m: (0, m[0] ^ i)) for a in in_held],
            out_specs=[fixed(x.shape), wide, wide]
            + [fixed((size, width)) for _, _, size in ge_places],
            scratch_shapes=[pltpu.VMEM((width, chunk), BF16)],
        ),
        out_shape=[shape(x.shape)]
        + [shape((slots, hidden_width))] * 2
        + [shape((size, width)) for _, _, size in ge_places],
        compiler_params=pltpu.CompilerParams(vmem_limit_bytes=56 * 2**20),
        cost_estimate=QUICK,
    )(place, x, dy, router, *in_held)
    return out[0], out[1], out[2], out[3:]


def expert_outer(place, x, dys, hidden, slope, in_held, places, eout_held, eout_places, count):
    slots, width = x.shape
    hidden_width = in_held[0].shape[1]
    part = width // count
    chunk = hidden_width // count
    fixed = lambda shape: pl.BlockSpec(shape, lambda i, m: (0, 0))
    wide = pl.BlockSpec((slots, chunk), lambda i, m: (0, i))
    lanes = lambda rows: pl.BlockSpec((rows, chunk), lambda i, m: (0, m[0] ^ i))
    out = pl.pallas_call(
        functools.partial(outer_kernel, count, places, eout_places),
        grid_spec=pltpu.PrefetchScalarGridSpec(
            num_scalar_prefetch=1,
            grid=(count,),
            in_specs=[fixed(x.shape), fixed(x.shape), wide, wide]
            + [lanes(a.shape[0]) for a in in_held]
            + [fixed(a.shape) for a in eout_held],
            out_specs=[fixed((slots, 2 * width))] + [lanes(part)] * count,
            scratch_shapes=[
                pltpu.VMEM((width, chunk), BF16),
                pltpu.VMEM((chunk, width), BF16),
                pltpu.VMEM((slots, width), F32),
                pltpu.VMEM((slots, width), F32),
                pltpu.VMEM((width, chunk), BF16),
            ],
        ),
        out_shape=[jax.ShapeDtypeStruct((slots, 2 * width), BF16)]
        + [jax.ShapeDtypeStruct((part, hidden_width), BF16)] * count,
        compiler_params=pltpu.CompilerParams(vmem_limit_bytes=56 * 2**20),
        cost_estimate=QUICK,
    )(place, x, dys, hidden, slope, *in_held, *eout_held)
    return out[0], out[1:]


def slot_kernel(
    count,
    experts,
    place_ref,
    home_ref,
    dy_ref,
    n2_ref,
    h1_ref,
    scalar_ref,
    router_ref,
    out_ref,
    gain_ref,
    gain_part_ref,
    *refs,
):
    me = place_ref[0]
    parcel_refs, parcel = refs[:count], refs[count]
    slots, width = dy_ref.shape
    part = width // count
    y = home_ref[:, :width]
    dy = dy_ref[...].astype(F32)
    h1 = h1_ref[...].astype(F32)
    scalars = scalar_ref[...]
    probs, gate, r2 = scalars[:, :experts], scalars[:, experts : experts + 1], scalars[:, experts + 1 :]
    dgate = jnp.sum(dy * y.astype(F32), axis=1, keepdims=True)
    row = lax.broadcasted_iota(I32, (slots, experts), 0)
    lane = lax.broadcasted_iota(I32, (slots, experts), 1)
    hot = jnp.where(row // CAPACITY * count + me == lane, 1.0, 0.0)
    dlogits = ((dgate * gate) * (hot - probs)).astype(BF16)
    dn2 = home_ref[:, width:].astype(F32) + mm(dlogits, router_ref[...], NT)
    scaled = dn2 * gain_ref[...]
    inner = jnp.sum(scaled * h1, axis=1, keepdims=True)
    dh1 = dy + r2 * scaled - h1 * (r2 * r2 * r2 * (1.0 / width) * inner)
    gain_part_ref[...] = jnp.sum(dn2 * h1 * r2, axis=0, keepdims=True)
    da = dh1.astype(BF16)
    do = mm(da, out_ref[...], NT).astype(BF16)
    router_high, router_low = two_parts(mm(n2_ref[...], dlogits, TN))
    fill = jnp.zeros((slots - part, 2 * experts), BF16)
    for d in range(count):
        span = slice(d * part, (d + 1) * part)
        router = jnp.concatenate([router_high[span], router_low[span]], axis=1)
        router = jnp.concatenate([router, fill], axis=0)
        parcel[me ^ d] = jnp.concatenate([y[:, span], da[:, span], do[:, span], router], axis=1)
    for k in range(count):
        parcel_refs[k][...] = parcel[k]


def slot_work(place, home, dy, n2, h1, scalars, router, out_proj, gain, count):
    slots, width = dy.shape
    experts = router.shape[1]
    lanes = 3 * width // count + 2 * experts
    fixed = lambda a: pl.BlockSpec(a.shape, lambda i, m: (0,) * len(a.shape))
    ins = (home, dy, n2, h1, scalars, router, out_proj, gain)
    outs = [jax.ShapeDtypeStruct((1, width), F32)]
    outs += [jax.ShapeDtypeStruct((slots, lanes), BF16)] * count
    out = pl.pallas_call(
        functools.partial(slot_kernel, count, experts),
        grid_spec=pltpu.PrefetchScalarGridSpec(
            num_scalar_prefetch=1,
            grid=(1,),
            in_specs=[fixed(a) for a in ins],
            out_specs=[fixed(a) for a in outs],
            scratch_shapes=[pltpu.VMEM((count, slots, lanes), BF16)],
        ),
        out_shape=outs,
        compiler_params=pltpu.CompilerParams(vmem_limit_bytes=48 * 2**20),
        cost_estimate=QUICK,
    )(place, *ins)
    return out[1:], out[0]


def send(piece, offset):
    count = lax.axis_size("row")
    return lax.ppermute(piece, "row", [(i, i ^ offset) for i in range(count)])


def row_join(block, far):
    me = lax.axis_index("row")
    count = lax.axis_size("row")
    near = send(jnp.stack([block, far]), 1)
    held = jnp.stack([block, near[0], far, near[1]])
    return jnp.concatenate(
        [lax.dynamic_index_in_dim(held, p ^ me, 0, keepdims=True) for p in range(count)]
    )


def row_gather(block):
    return row_join(block, send(block, 2))


def swap(blocks, axis):
    return lax.all_to_all(blocks, axis, 0, 0)


def col_gather(block):
    count = lax.axis_size("col")
    return swap(jnp.broadcast_to(block[None], (count,) + block.shape), "col")


def trade(piece_for):
    me = lax.axis_index("row")
    return trade_pieces([piece_for(me ^ k) for k in range(lax.axis_size("row"))])


def trade_pieces(pieces):
    count = len(pieces)
    held = {k: send(pieces[k], k) for k in (2, 3, 1)}
    return [pieces[0]] + [held[k] for k in range(1, count)]


def lay(held):
    me = lax.axis_index("row")
    out = jnp.zeros((len(held),) + held[0].shape, held[0].dtype)
    for k, piece in enumerate(held):
        out = lax.dynamic_update_slice_in_dim(out, piece[None], me ^ k, 0)
    return out


def after(value, *earlier):
    return lax.optimization_barrier((value,) + earlier)[0]


def fill_kernel(count, me_ref, *refs):
    step = pl.program_id(1)
    for k in range(count):

        @pl.when(step == k)
        def _(k=k):
            refs[count][...] = refs[k][...].astype(F32)


def fill_columns(held, splits):
    count = len(held)
    height, width = held[0].shape
    block = height // splits
    me = lax.axis_index("row").astype(I32).reshape(1)
    return pl.pallas_call(
        functools.partial(fill_kernel, count),
        grid_spec=pltpu.PrefetchScalarGridSpec(
            num_scalar_prefetch=1,
            grid=(splits, count),
            in_specs=[pl.BlockSpec((block, width), lambda i, k, m: (i, 0))] * count,
            out_specs=pl.BlockSpec((block, width), lambda i, k, m: (i, m[0] ^ k)),
        ),
        out_shape=jax.ShapeDtypeStruct((height, count * width), F32),
        compiler_params=pltpu.CompilerParams(vmem_limit_bytes=48 * 2**20),
        cost_estimate=QUICK,
    )(me, *held)


def own_rows(array, me, count):
    return lax.dynamic_slice_in_dim(array, me * count, count, 0)


def expert_plan(
    tokens,
    gain_one,
    gain_two,
    w_query,
    w_key,
    w_value,
    w_out,
    w_router,
    w_in,
    w_expert_out,
    bias_table,
    segment,
    expert,
    bucket,
    cotangent,
):
    rows, cols = lax.axis_size("row"), lax.axis_size("col")
    me, col = lax.axis_index("row"), lax.axis_index("col")
    part, seq_len = tokens.shape[1:]
    width = part * rows
    tok_rows = seq_len // rows
    buckets, all_heads = bias_table.shape
    heads = all_heads // rows
    head_dim = width // all_heads
    experts = w_router.shape[1] * cols
    hidden_width = w_expert_out.shape[0] * rows
    slots = (experts // rows) * CAPACITY
    out_cols = w_query.shape[1]
    share = cols // rows

    doc_ids = segment[0]
    expert_ids = expert[0, :, 0]

    tok_far = send(tokens[0], 2)
    tok_low = row_join(tokens[0], tok_far).reshape(width, seq_len)
    qkv_cols = col_gather(jnp.concatenate([w_query, w_key, w_value], axis=1))
    same_doc = own_rows(doc_ids, me, tok_rows)[:, None] == doc_ids[None, :]
    masked = jnp.where(same_doc, after(bucket, tok_far)[0], buckets).astype(BF16)
    idx_far = send(masked, 2)
    cot_own = cotangent[0]
    cot_far = send(cot_own, 2)
    lane_cut = lambda array, count, k: lax.dynamic_slice_in_dim(array, (me ^ k) * count, count, 1)
    half = part // 2
    in_first = send(lane_cut(after(w_in, tok_far)[:half], hidden_width, 2), 2)
    qkv_cols = after(qkv_cols, idx_far, cot_far, in_first)
    out_part = after(jnp.concatenate([w_out, w_router], axis=1), qkv_cols)
    out_gathered = col_gather(out_part)
    qkv_cols = qkv_cols.reshape(rows, share, part, 3 * out_cols)
    qkv_held = trade(lambda d: lax.dynamic_index_in_dim(qkv_cols, d, 0, keepdims=False))
    second_cut = lane_cut(after(w_in, qkv_cols)[half:], hidden_width, 2)
    eout_half = w_expert_out.shape[0] // 4
    later_eout = after(w_expert_out, qkv_cols)
    eout_cuts = [lane_cut(later_eout, width, k) for k in range(3)]
    eout_cuts.append(lane_cut(later_eout[:eout_half], width, 3))
    eout_cuts.append(lane_cut(later_eout[eout_half:], width, 3))
    qkv_held = after(tuple(qkv_held), *eout_cuts)
    qkv_own = jnp.transpose(
        lay(qkv_held).reshape(rows, share, part, 3, out_cols), (0, 2, 3, 1, 4)
    ).reshape(width, 3 * part)
    idx = row_join(masked, idx_far).reshape(seq_len, seq_len)
    cot_low = row_join(cot_own, cot_far).reshape(width, seq_len)

    picked = expert_ids[None, :] == jnp.arange(experts, dtype=I32)[:, None]
    picked_float = picked.astype(F32)
    steps = jnp.arange(seq_len, dtype=I32)
    upper = (steps[:, None] <= steps[None, :]).astype(BF16)
    ranks = mm(picked.astype(BF16), upper, NN) - 1.0
    slot_rank = jnp.sum(ranks * picked_float, axis=0).astype(I32)
    slot = (expert_ids % rows) * slots + (expert_ids // rows) * CAPACITY + slot_rank
    choose = (jnp.arange(slots, dtype=I32)[:, None] + me * slots == slot[None, :]).astype(BF16)

    x = tok_low.astype(F32)
    r1 = lax.rsqrt(jnp.mean(x * x, axis=0) + NORM_EPS)
    n1 = (x * r1 * gain_one[:, None]).astype(BF16)
    qkv = mm(qkv_own, n1, TN).astype(BF16)
    later_in = after(w_in, tok_low)
    in_places = ((0, 0), (2, 0), (2, half), (3, 0), (1, 0))
    in_second = send(after(second_cut, qkv), 2)
    in_held = [lane_cut(later_in, hidden_width, 0), in_first, in_second]
    for k in (3, 1):
        in_held.append(send(after(lane_cut(later_in, hidden_width, k), qkv), k))
    qkv, n1, qkv_own = lax.optimization_barrier((qkv, n1, qkv_own))
    q, k, v = qkv[:part], qkv[part : 2 * part], qkv[2 * part :]
    table = lax.dynamic_slice_in_dim(jnp.transpose(bias_table), me * heads, heads, 0)
    table = jnp.pad(
        table, ((0, 8 - heads), (0, LANES - buckets)), constant_values=NEG_FILL
    )
    o32, p = attend(q, k, v, idx, table, heads, 256)
    expert_at = lambda a: swap(a.reshape(cols, CAPACITY, width), "col").reshape(slots, width)
    dy_low = mm(choose, cot_low, NT).astype(BF16)
    o_low = after(o32.astype(BF16), in_second, in_held[3])
    dy_slots = expert_at(dy_low)
    o_far = send(o_low, 2)
    o_full = row_join(o_low, after(o_far, dy_slots)).reshape(width, seq_len)
    out_gathered = after(out_gathered, o32)
    out_rows = jnp.transpose(out_gathered[:, :, :out_cols], (1, 0, 2)).reshape(part, width)
    router_rows = jnp.transpose(out_gathered[:, :, out_cols:], (1, 0, 2)).reshape(part, experts)
    out_router = jnp.concatenate([out_rows, router_rows], axis=1)
    out_router = row_gather(out_router).reshape(width, width + experts)
    out_full, router_full = out_router[:, :width], out_router[:, width:]
    eout_two = send(after(eout_cuts[2], o_far), 2)
    eout_three = send(after(eout_cuts[3], o_far), 3)
    h1 = x + mm(out_full, o_full, TN)
    r2 = lax.rsqrt(jnp.mean(h1 * h1, axis=0) + NORM_EPS)
    n2 = (h1 * r2 * gain_two[:, None]).astype(BF16)
    logits = mm(router_full, n2, TN)
    g = jax.nn.softmax(logits, axis=0)
    gate = jnp.sum(g * picked_float, axis=0)

    n2_low = mm(choose, n2, NT).astype(BF16)
    slots_in = after(expert_at(n2_low), eout_two, eout_three)
    eout_last = send(after(eout_cuts[4], slots_in), 3)
    eout_one = send(after(eout_cuts[1], slots_in), 1)
    eout_held = [eout_cuts[0], eout_one, eout_two, eout_three, eout_last]
    eout_places = ((0, 0), (1, 0), (2, 0), (3, 0), (3, eout_half))
    place = jnp.stack([me, col * rows + me]).astype(I32)
    hid = w_expert_out.shape[0]
    ge_cut = hid // 4 * 3
    ge_places = ((0, 0, hid), (1, 0, hid), (2, 0, ge_cut), (2, ge_cut, hid - ge_cut), (3, 0, hid))
    dys, hidden, slope, ge = expert_inner(
        place, slots_in, dy_slots, router_full, in_held, in_places, ge_places, rows
    )
    hidden = after(hidden, *ge)
    back, in_pieces = expert_outer(
        place, slots_in, dys, hidden, slope, in_held, in_places, eout_held, eout_places, rows
    )
    grad_eout_first = send(ge[2], 2)
    back = after(back, grad_eout_first)
    grad_eout_held = [
        ge[0],
        send(after(ge[1], back), 1),
        send(after(ge[3], back), 2),
        send(after(ge[4], back), 3),
    ]
    home = swap(back.reshape(cols, CAPACITY, 2 * width), "col").reshape(slots, 2 * width)

    h1_s = mm(choose, h1.astype(BF16), NT).astype(BF16)
    h1_own = own_rows(h1, me, part)
    home = after(home, h1_own)
    scalars = lax.dot_general(
        choose.astype(F32),
        jnp.concatenate([g, gate[None], r2[None]], axis=0),
        NT,
        precision=lax.Precision.HIGHEST,
        preferred_element_type=F32,
    )
    parcel, gain_two_part = slot_work(
        place, home, dy_low, n2_low, h1_s, scalars, router_full, out_full, gain_two[None], rows
    )
    parcel = trade_pieces(after(tuple(parcel), *grad_eout_held[2:]))
    in_turn = lambda piece: after(piece, parcel[2], parcel[3])
    grad_in_held = [
        in_pieces[0],
        send(in_turn(in_pieces[1]), 1),
        send(in_turn(in_pieces[2]), 2),
    ]
    grad_in_half = send(in_turn(in_pieces[3][:half]), 3)

    layer_out, da, proj_parcel, dn1_parcel = attend_back(
        place,
        q,
        k,
        v,
        idx,
        p,
        o32,
        slot[None],
        h1_own,
        jnp.stack([r1, gate]),
        gain_one[:, None],
        tok_low,
        n1,
        o_full,
        qkv_own,
        gain_two_part,
        parcel,
        cols,
        buckets,
        256,
    )
    dn1_parcel, proj_parcel = after(
        (tuple(dn1_parcel), proj_parcel), grad_in_half, grad_in_held[2]
    )
    dn1_held = trade_pieces(dn1_parcel)
    grad_in_held.append(send(after(in_pieces[3][half:], dn1_held[2], dn1_held[3]), 3))
    dn1_sum = sum(piece.astype(F32) for piece in dn1_held)
    dn1 = dn1_sum[:part]
    inner_one = dn1_sum[part] + dn1_sum[part + 1]
    gain_own = own_rows(gain_one, me, part)
    grad_tokens = (
        da.astype(F32)
        + r1 * gain_own[:, None] * dn1
        - own_rows(x, me, part) * (r1**3 / width * inner_one)
    ).astype(BF16)

    band = width // cols
    proj_sum = jnp.sum(swap(proj_parcel, "col").astype(F32), axis=0)
    half = PAIR_ROWS // 2
    extra_sum = proj_sum[band : band + half] + proj_sum[band + half :]
    router_rows = experts // cols
    grad_router = jnp.transpose(extra_sum[:router_rows, :part])
    small = sum(trade_pieces([extra_sum[router_rows:]] * rows))
    gain_one_grad, gain_two_grad = small[0], small[1]
    table_grad = jnp.transpose(
        small[2:, : LOW_BINS // 2 * LANES]
        .reshape(LOW_BINS, LANES)[:, : bias_table.size // LOW_BINS]
        .reshape(LOW_BINS, all_heads, buckets // LOW_BINS),
        (2, 0, 1),
    ).reshape(bias_table.shape)
    pieces = []
    for turn in range(share):
        moves = [
            (r * cols + c, (c // share) * cols + share * r + (c + turn) % share)
            for r in range(rows)
            for c in range(cols)
        ]
        first = (col + turn) % share * 4 * out_cols
        piece = lax.dynamic_slice_in_dim(proj_sum[:band], first, 4 * out_cols, 1)
        pieces.append(lax.ppermute(piece, ("row", "col"), moves))
    pieces = jnp.stack(pieces)
    grad_four = jnp.concatenate(
        [
            lax.dynamic_index_in_dim(pieces, (col - half) % share, 0, keepdims=False)
            for half in range(share)
        ],
        axis=0,
    )
    grad_query, grad_key, grad_value, grad_out = [
        grad_four[:, w * out_cols : (w + 1) * out_cols] for w in range(4)
    ]
    last = after(grad_in_held[3], proj_sum)
    grad_in_held[3] = jnp.concatenate([grad_in_half, last], axis=0)
    grad_eout_held[2] = jnp.concatenate([grad_eout_first, grad_eout_held[2]], axis=0)
    grad_in, grad_eout = fill_columns(grad_in_held, 2), fill_columns(grad_eout_held, 2)
    return (
        layer_out[None],
        grad_tokens[None],
        gain_one_grad,
        gain_two_grad,
        grad_query,
        grad_key,
        grad_value,
        grad_out,
        grad_router,
        grad_in,
        grad_eout,
        table_grad,
    )


def solution(mesh):
    rows, cols = mesh.shape["row"], mesh.shape["col"]
    paired = rows == 4 and cols == 2 * rows and EXPERTS == rows * cols
    return jax.shard_map(
        expert_plan if paired else general_plan,
        mesh=mesh,
        in_specs=(
            P("col", "row", None),
            P(),
            P(),
            P("row", "col"),
            P("row", "col"),
            P("row", "col"),
            P("row", "col"),
            P("row", "col"),
            P("row", "col"),
            P("row", "col"),
            P(),
            P("col", None),
            P("col", None, None),
            P("col", "row", None),
            P("col", "row", None),
        ),
        out_specs=(
            P("col", "row", None),
            P("col", "row", None),
            P(),
            P(),
            P("row", "col"),
            P("row", "col"),
            P("row", "col"),
            P("row", "col"),
            P("row", "col"),
            P("row", "col"),
            P("row", "col"),
            P(),
        ),
        check_vma=False,
    )
```

```python
import functools

import jax
import jax.numpy as jnp
from jax import lax
from jax.experimental import pallas as pl
from jax.experimental.pallas import tpu as pltpu
from jax.sharding import PartitionSpec as P

EXPERTS = 32
CAPACITY = 48


NORM_EPS = 1e-06
NEG_FILL = -1e30


def row_totals(partial_values):
    return lax.psum(partial_values, "row")


def feature_split(partial_rows):
    return lax.psum_scatter(partial_rows, "row", scatter_dimension=1, tiled=True)


def feature_join(rows_low):
    return lax.all_gather(rows_low, "row", axis=1, tiled=True)


def norm_back(grad_normed, inputs_f, inverse_rms, gain_part, model_width):
    inner_sum = row_totals(jnp.sum(gain_part * grad_normed * inputs_f, axis=1))
    return (
        inverse_rms[:, None] * gain_part * grad_normed
        - inputs_f * (inverse_rms**3 / model_width * inner_sum)[:, None]
    )


def block_scores(
    query_heads, keys_all, bucket_rows, query_docs, doc_ids, bias_table, number, key_block
):
    head_count = bias_table.shape[1]
    head_dim = query_heads.shape[2]
    offset = number * key_block
    key_rows = lax.dynamic_slice_in_dim(keys_all, offset, key_block, 0).reshape(
        key_block, head_count, head_dim
    )
    bucket_cols = lax.dynamic_slice_in_dim(bucket_rows, offset, key_block, 1)
    key_docs = lax.dynamic_slice_in_dim(doc_ids, offset, key_block, 0)
    raw_scores = jnp.einsum(
        "ihd,jhd->hij", query_heads, key_rows, preferred_element_type=jnp.float32
    ) * head_dim ** (-0.5)
    one_hot = (bucket_cols[:, :, None] == jnp.arange(bias_table.shape[0], dtype=jnp.int32)).astype(
        jnp.float32
    )
    pair_bias = jnp.einsum("ijb,bh->hij", one_hot, bias_table, precision=lax.Precision.HIGHEST)
    allowed = (query_docs[:, None] == key_docs[None, :])[None]
    return (raw_scores + pair_bias, allowed, one_hot)


def attend_blocks(query_heads, keys_all, values_all, bucket_rows, query_docs, doc_ids, bias_table):
    tok_rows, head_count, head_dim = query_heads.shape
    seq_len = keys_all.shape[0]
    key_block = min(seq_len, 512)
    blocks = seq_len // key_block

    def first_pass(status, number):
        row_peak, row_total = status
        scores, allowed, one_hot = block_scores(
            query_heads, keys_all, bucket_rows, query_docs, doc_ids, bias_table, number, key_block
        )
        masked = jnp.where(allowed, scores, NEG_FILL)
        new_peak = jnp.maximum(row_peak, jnp.max(masked, axis=2))
        weights = jnp.where(allowed, jnp.exp(masked - new_peak[:, :, None]), 0.0)
        row_total = row_total * jnp.exp(row_peak - new_peak) + jnp.sum(weights, axis=2)
        return ((new_peak, row_total), None)

    start_status = (
        jnp.full((head_count, tok_rows), NEG_FILL, jnp.float32),
        jnp.zeros((head_count, tok_rows), jnp.float32),
    )
    (row_peak, row_total), unused = lax.scan(first_pass, start_status, jnp.arange(blocks))
    log_total = row_peak + jnp.log(row_total)

    def second_pass(running, number):
        scores, allowed, one_hot = block_scores(
            query_heads, keys_all, bucket_rows, query_docs, doc_ids, bias_table, number, key_block
        )
        soft_weights = jnp.where(allowed, jnp.exp(scores - log_total[:, :, None]), 0.0).astype(
            jnp.bfloat16
        )
        value_rows = lax.dynamic_slice_in_dim(values_all, number * key_block, key_block, 0).reshape(
            key_block, head_count, head_dim
        )
        return (
            running
            + jnp.einsum(
                "hij,jhd->ihd", soft_weights, value_rows, preferred_element_type=jnp.float32
            ),
            None,
        )

    start_acc = jnp.zeros((tok_rows, head_count, head_dim), jnp.float32)
    attended, unused = lax.scan(second_pass, start_acc, jnp.arange(blocks))
    return (attended, log_total)


def attend_blocks_back(
    query_heads,
    keys_all,
    values_all,
    bucket_rows,
    query_docs,
    doc_ids,
    bias_table,
    log_total,
    grad_heads,
    grad_dot,
):
    tok_rows, head_count, head_dim = query_heads.shape
    seq_len = keys_all.shape[0]
    model_width = head_count * head_dim
    key_block = min(seq_len, 512)
    blocks = seq_len // key_block
    scaling = head_dim ** (-0.5)

    def step_back(status, number):
        grad_query, grad_table = status
        scores, allowed, one_hot = block_scores(
            query_heads, keys_all, bucket_rows, query_docs, doc_ids, bias_table, number, key_block
        )
        key_rows = lax.dynamic_slice_in_dim(keys_all, number * key_block, key_block, 0).reshape(
            key_block, head_count, head_dim
        )
        value_rows = lax.dynamic_slice_in_dim(values_all, number * key_block, key_block, 0).reshape(
            key_block, head_count, head_dim
        )
        soft_weights = jnp.where(allowed, jnp.exp(scores - log_total[:, :, None]), 0.0)
        weights_low = soft_weights.astype(jnp.bfloat16)
        grad_soft = jnp.einsum(
            "ihd,jhd->hij", grad_heads, value_rows, preferred_element_type=jnp.float32
        )
        grad_scores = soft_weights * (grad_soft - grad_dot[:, :, None])
        grad_table = grad_table + jnp.einsum(
            "ijb,hij->bh", one_hot, grad_scores, precision=lax.Precision.HIGHEST
        )
        scores_low = grad_scores.astype(jnp.bfloat16)
        grad_query = grad_query + scaling * jnp.einsum(
            "hij,jhd->ihd", scores_low, key_rows, preferred_element_type=jnp.float32
        )
        grad_key = scaling * jnp.einsum(
            "hij,ihd->jhd", scores_low, query_heads, preferred_element_type=jnp.float32
        )
        grad_value = jnp.einsum(
            "hij,ihd->jhd", weights_low, grad_heads, preferred_element_type=jnp.float32
        )
        stacked = jnp.concatenate(
            [grad_key.reshape(key_block, model_width), grad_value.reshape(key_block, model_width)],
            axis=1,
        )
        return ((grad_query, grad_table), stacked)

    start_status = (
        jnp.zeros((tok_rows, head_count, head_dim), jnp.float32),
        jnp.zeros(bias_table.shape, jnp.float32),
    )
    (grad_query, grad_table), kv_terms = lax.scan(step_back, start_status, jnp.arange(blocks))
    return (grad_query, grad_table, kv_terms.reshape(seq_len, 2 * model_width))


def general_plan(
    tokens,
    gain_one,
    gain_two,
    w_query,
    w_key,
    w_value,
    w_out,
    w_router,
    w_in,
    w_expert_out,
    bias_table,
    segment,
    expert,
    bucket,
    cotangent,
):
    seq_len = tokens.shape[2]
    dim_rows = tokens.shape[1]
    row_count = lax.axis_size("row")
    model_width = dim_rows * row_count
    tok_rows = seq_len // row_count
    experts = EXPERTS
    hid_rows = w_expert_out.shape[0]
    ffn_width = hid_rows * row_count
    head_count = bias_table.shape[1]
    head_dim = model_width // head_count
    row_index = lax.axis_index("row")
    gathered = (
        lax.all_gather(w_query, "col", axis=1, tiled=True),
        lax.all_gather(w_key, "col", axis=1, tiled=True),
        lax.all_gather(w_value, "col", axis=1, tiled=True),
        lax.all_gather(w_out, "col", axis=1, tiled=True),
        lax.all_gather(w_router, "col", axis=1, tiled=True),
        lax.all_gather(w_in, "col", axis=1, tiled=True),
        lax.all_gather(w_expert_out, "col", axis=1, tiled=True),
    )
    query_full, key_full, value_full, out_proj_full, router_full, in_flat, out_flat = gathered
    in_full = in_flat.reshape(dim_rows, experts, ffn_width)
    out_full = out_flat.reshape(hid_rows, experts, model_width)
    stacked_weights = jnp.concatenate([query_full, key_full, value_full], axis=1)
    tok_float = jnp.transpose(tokens[0].astype(jnp.float32))
    doc_ids = segment[0]
    query_docs = lax.dynamic_slice_in_dim(doc_ids, row_index * tok_rows, tok_rows, 0)
    bucket_rows = bucket[0]
    expert_ids = expert[0, :, 0]
    gain_part_one = lax.dynamic_slice_in_dim(gain_one, row_index * dim_rows, dim_rows, 0)
    gain_part_two = lax.dynamic_slice_in_dim(gain_two, row_index * dim_rows, dim_rows, 0)
    inverse_one = lax.rsqrt(
        row_totals(jnp.sum(tok_float * tok_float, axis=1)) / model_width + NORM_EPS
    )
    normed_one = (tok_float * inverse_one[:, None] * gain_part_one).astype(jnp.bfloat16)
    projected = lax.psum_scatter(
        jnp.dot(normed_one, stacked_weights, preferred_element_type=jnp.float32),
        "row",
        scatter_dimension=0,
        tiled=True,
    ).astype(jnp.bfloat16)
    queries_low = projected[:, :model_width]
    keys_low = projected[:, model_width : 2 * model_width]
    values_low = projected[:, 2 * model_width :]
    keys_all, values_all = (
        lax.all_gather(keys_low, "row", axis=0, tiled=True),
        lax.all_gather(values_low, "row", axis=0, tiled=True),
    )
    query_heads = queries_low.reshape(tok_rows, head_count, head_dim)
    attended, log_total = attend_blocks(
        query_heads, keys_all, values_all, bucket_rows, query_docs, doc_ids, bias_table
    )
    attn_low = attended.reshape(tok_rows, model_width).astype(jnp.bfloat16)
    heads_home = lax.all_to_all(attn_low, "row", split_axis=1, concat_axis=0, tiled=True)
    attn_rows = feature_split(
        jnp.dot(heads_home, out_proj_full, preferred_element_type=jnp.float32)
    )
    residual = tok_float + attn_rows
    inverse_two = lax.rsqrt(
        row_totals(jnp.sum(residual * residual, axis=1)) / model_width + NORM_EPS
    )
    normed_two = (residual * inverse_two[:, None] * gain_part_two).astype(jnp.bfloat16)
    logits = row_totals(jnp.dot(normed_two, router_full, preferred_element_type=jnp.float32))
    gate_probs = jax.nn.softmax(logits, axis=1)
    picked = (expert_ids[:, None] == jnp.arange(experts, dtype=jnp.int32)[None, :]).astype(
        jnp.int32
    )
    picked_float = picked.astype(jnp.float32)
    slot_rank = jnp.sum((jnp.cumsum(picked, axis=0) - 1) * picked, axis=1)
    slot_index = expert_ids * CAPACITY + slot_rank
    token_gate = jnp.sum(gate_probs * picked_float, axis=1)
    slots_in = (
        jnp.zeros((experts * CAPACITY, dim_rows), jnp.bfloat16).at[slot_index].set(normed_two)
    )
    slots_own = slots_in.reshape(experts, CAPACITY, dim_rows)
    lead_count = slots_own.shape[0]
    slot_count = slots_own.shape[1]
    pre_partial = jnp.einsum("ecd,def->ecf", slots_own, in_full, preferred_element_type=jnp.float32)
    pre_act = feature_split(pre_partial.reshape(lead_count * slot_count, ffn_width))
    hidden = jax.nn.gelu(pre_act).astype(jnp.bfloat16)
    hidden_three = hidden.reshape(lead_count, slot_count, hid_rows)
    out_partial = jnp.einsum(
        "ecf,fed->ecd", hidden_three, out_full, preferred_element_type=jnp.float32
    )
    expert_local = feature_split(out_partial.reshape(lead_count * slot_count, model_width))
    expert_tok = expert_local[slot_index]
    layer_out = (residual + token_gate[:, None] * expert_tok).astype(jnp.bfloat16)
    grad_final = jnp.transpose(cotangent[0].astype(jnp.float32))
    grad_gate = row_totals(jnp.sum(grad_final * expert_tok, axis=1))
    grad_expert_tok = (token_gate[:, None] * grad_final).astype(jnp.bfloat16)
    grad_slots = (
        jnp.zeros((experts * CAPACITY, dim_rows), jnp.bfloat16).at[slot_index].set(grad_expert_tok)
    )
    grad_slots_local = grad_slots.reshape(experts, CAPACITY, dim_rows)
    grad_slots_full = feature_join(
        grad_slots_local.reshape(lead_count * slot_count, dim_rows)
    ).reshape(lead_count, slot_count, model_width)
    grad_hidden = jnp.einsum(
        "ecd,fed->ecf", grad_slots_full, out_full, preferred_element_type=jnp.float32
    )
    grad_out_weight = jnp.einsum(
        "ecf,ecd->fed", hidden_three, grad_slots_full, preferred_element_type=jnp.float32
    )
    unused, gelu_back = jax.vjp(jax.nn.gelu, pre_act)
    grad_pre = gelu_back(grad_hidden.reshape(lead_count * slot_count, hid_rows))[0].astype(
        jnp.bfloat16
    )
    grad_pre_full = feature_join(grad_pre).reshape(lead_count, slot_count, ffn_width)
    grad_slots_in = jnp.einsum(
        "ecf,def->ecd", grad_pre_full, in_full, preferred_element_type=jnp.float32
    )
    grad_in_weight = jnp.einsum(
        "ecd,ecf->def", slots_own, grad_pre_full, preferred_element_type=jnp.float32
    )
    grad_logits = ((grad_gate * token_gate)[:, None] * (picked_float - gate_probs)).astype(
        jnp.bfloat16
    )
    router_back = lax.dot_general(
        grad_logits, router_full, (((1,), (1,)), ((), ())), preferred_element_type=jnp.float32
    )
    grad_normed_two = grad_slots_in.reshape(experts * CAPACITY, dim_rows)[slot_index] + router_back
    grad_router = lax.dot_general(
        normed_two, grad_logits, (((0,), (0,)), ((), ())), preferred_element_type=jnp.float32
    )
    grad_res = grad_final + norm_back(
        grad_normed_two, residual, inverse_two, gain_part_two, model_width
    )
    grad_gain_two = jnp.sum(grad_normed_two * residual * inverse_two[:, None], axis=0)
    grad_attn_full = feature_join(grad_res.astype(jnp.bfloat16))
    grad_heads_home = lax.dot_general(
        grad_attn_full, out_proj_full, (((1,), (1,)), ((), ())), preferred_element_type=jnp.float32
    ).astype(jnp.bfloat16)
    grad_out_proj = lax.dot_general(
        heads_home, grad_attn_full, (((0,), (0,)), ((), ())), preferred_element_type=jnp.float32
    )
    grad_attn = lax.all_to_all(grad_heads_home, "row", split_axis=0, concat_axis=1, tiled=True)
    grad_heads = grad_attn.reshape(tok_rows, head_count, head_dim)
    grad_dot = jnp.einsum("ihd,ihd->hi", grad_heads.astype(jnp.float32), attended)
    grad_query, grad_table, kv_terms = attend_blocks_back(
        query_heads,
        keys_all,
        values_all,
        bucket_rows,
        query_docs,
        doc_ids,
        bias_table,
        log_total,
        grad_heads,
        grad_dot,
    )
    key_value_grads = lax.psum_scatter(kv_terms, "row", scatter_dimension=0, tiled=True)
    grad_qkv = jnp.concatenate(
        [
            grad_query.reshape(tok_rows, model_width).astype(jnp.bfloat16),
            key_value_grads.astype(jnp.bfloat16),
        ],
        axis=1,
    )
    portion = lax.all_gather(grad_qkv, "row", axis=0, tiled=True)
    grad_part = lax.dot_general(
        portion, stacked_weights, (((1,), (1,)), ((), ())), preferred_element_type=jnp.float32
    )
    grad_weights = lax.dot_general(
        normed_one, portion, (((0,), (0,)), ((), ())), preferred_element_type=jnp.float32
    )
    grad_input = grad_res + norm_back(grad_part, tok_float, inverse_one, gain_part_one, model_width)
    grad_gain_one = jnp.sum(grad_part * tok_float * inverse_one[:, None], axis=0)
    summed = (
        lax.psum_scatter(grad_weights[:, :model_width], "col", scatter_dimension=1, tiled=True),
        lax.psum_scatter(
            grad_weights[:, model_width : 2 * model_width], "col", scatter_dimension=1, tiled=True
        ),
        lax.psum_scatter(
            grad_weights[:, 2 * model_width :], "col", scatter_dimension=1, tiled=True
        ),
        lax.psum_scatter(grad_out_proj, "col", scatter_dimension=1, tiled=True),
        lax.psum_scatter(grad_router, "col", scatter_dimension=1, tiled=True),
        lax.psum_scatter(
            grad_in_weight.reshape(dim_rows, experts * ffn_width),
            "col",
            scatter_dimension=1,
            tiled=True,
        ),
        lax.psum_scatter(
            grad_out_weight.reshape(hid_rows, experts * model_width),
            "col",
            scatter_dimension=1,
            tiled=True,
        ),
    )
    grad_query_w, grad_key_w, grad_value_w, grad_out_w, grad_router_w, grad_in_w, grad_expert_w = (
        summed
    )
    place_one = lax.dynamic_update_slice_in_dim(
        jnp.zeros((model_width,), jnp.float32), grad_gain_one, row_index * dim_rows, 0
    )
    place_two = lax.dynamic_update_slice_in_dim(
        jnp.zeros((model_width,), jnp.float32), grad_gain_two, row_index * dim_rows, 0
    )
    gain_one_grad, gain_two_grad, table_grad = lax.psum(
        (place_one, place_two, grad_table), ("row", "col")
    )
    layer_out_t = jnp.transpose(layer_out)[None]
    grad_input_t = jnp.transpose(grad_input.astype(jnp.bfloat16))[None]
    return (
        layer_out_t,
        grad_input_t,
        gain_one_grad,
        gain_two_grad,
        grad_query_w,
        grad_key_w,
        grad_value_w,
        grad_out_w,
        grad_router_w,
        grad_in_w,
        grad_expert_w,
        table_grad,
    )


BF16 = jnp.bfloat16
F32 = jnp.float32
I32 = jnp.int32
NT = (((1,), (1,)), ((), ()))
NN = (((1,), (0,)), ((), ()))
TN = (((0,), (0,)), ((), ()))
LANES = 128
PAIR_ROWS = 16
LOW_BINS = 8
GELU_SCALE = 0.7978845608028654
GELU_CUBE = 0.044715
QUICK = pl.CostEstimate(flops=0, bytes_accessed=0, transcendentals=0)


def mm(left, right, dims):
    return lax.dot_general(left, right, dims, preferred_element_type=F32)


def two_parts(values):
    high = values.astype(BF16)
    return high, (values - high.astype(F32)).astype(BF16)


def attend_kernel(heads, head_dim, q_ref, k_ref, v_ref, idx_ref, tab_ref, o_ref, p_ref):
    rows, keys = idx_ref.shape
    idx = idx_ref[...].astype(F32).astype(I32)
    for h in range(heads):
        span = slice(h * head_dim, (h + 1) * head_dim)
        table = jnp.broadcast_to(tab_ref[h : h + 1, :], (rows, LANES))
        bias = jnp.concatenate(
            [
                jnp.take_along_axis(table, idx[:, c : c + LANES], axis=1)
                for c in range(0, keys, LANES)
            ],
            axis=1,
        )
        scores = mm(q_ref[span, :], k_ref[span, :], TN) * head_dim**-0.5 + bias
        weights = jnp.exp(scores - jnp.max(scores, axis=1, keepdims=True))
        soft = (weights * (1.0 / jnp.sum(weights, axis=1, keepdims=True))).astype(BF16)
        p_ref[h] = soft
        o_ref[span, :] = mm(v_ref[span, :], soft, NT)


def attend(q, k, v, idx, tab, heads, tile):
    width, keys = q.shape
    whole = lambda a: pl.BlockSpec(a.shape, lambda i: (0, 0))
    return pl.pallas_call(
        functools.partial(attend_kernel, heads, width // heads),
        grid=(keys // tile,),
        in_specs=[
            pl.BlockSpec((width, tile), lambda i: (0, i)),
            whole(k),
            whole(v),
            pl.BlockSpec((tile, keys), lambda i: (i, 0)),
            whole(tab),
        ],
        out_specs=[
            pl.BlockSpec((width, tile), lambda i: (0, i)),
            pl.BlockSpec((heads, tile, keys), lambda i: (0, i, 0)),
        ],
        out_shape=[
            jax.ShapeDtypeStruct((width, keys), F32),
            jax.ShapeDtypeStruct((heads, keys, keys), BF16),
        ],
        compiler_params=pltpu.CompilerParams(vmem_limit_bytes=48 * 2**20),
        cost_estimate=QUICK,
    )(q, k, v, idx, tab)


def back_kernel(
    heads,
    count,
    experts,
    cols,
    place_ref,
    q_ref,
    k_ref,
    v_ref,
    idx_ref,
    p_ref,
    o_ref,
    slot_ref,
    h1_ref,
    row_ref,
    col_ref,
    x_ref,
    n1_ref,
    ofull_ref,
    w_ref,
    gain_two_ref,
    *refs,
):
    pieces = refs[:count]
    layer_ref, da_ref, proj_ref = refs[count : count + 3]
    dn1_refs = refs[count + 3 : 2 * count + 3]
    g_aug, v_aug, dqkv, dk_acc, dv_acc, hist, router_acc, dn1_acc = refs[2 * count + 3 :]
    step, steps = pl.program_id(0), pl.num_programs(0)
    me = place_ref[0]
    part, tile = q_ref.shape
    keys = k_ref.shape[1]
    head_dim = part // heads
    aug = g_aug.shape[0] // heads
    width = x_ref.shape[0]
    slots = pieces[0].shape[0]
    scale = head_dim**-0.5

    @pl.when(step == 0)
    def _():
        dk_acc[...] = jnp.zeros_like(dk_acc)
        dv_acc[...] = jnp.zeros_like(dv_acc)
        hist[...] = jnp.zeros_like(hist)
        placed = jnp.zeros((3 * part, keys), F32)
        router = jnp.zeros((part, 2 * experts), F32)
        slot_row = lax.broadcasted_iota(I32, (slots, keys), 0)
        for k in range(count):
            spread = jnp.where(slot_row + (me ^ k) * slots == slot_ref[...], 1.0, 0.0).astype(BF16)
            placed = placed + mm(pieces[k][:, : 3 * part], spread, TN)
            router = router + pieces[k][:part, 3 * part :].astype(F32)
        router_acc[...] = router[:, :experts] + router[:, experts:]
        layer_ref[...] = (h1_ref[...] + row_ref[1:2, :] * placed[:part]).astype(BF16)
        da_ref[...] = placed[part : 2 * part].astype(BF16)
        fill = jnp.zeros((PAIR_ROWS - 2, keys), F32)
        ones = jnp.concatenate([jnp.ones((2, keys), F32), fill], axis=0).astype(BF16)
        for h in range(heads):
            span = slice(h * head_dim, (h + 1) * head_dim)
            do = placed[2 * part + h * head_dim : 2 * part + (h + 1) * head_dim]
            delta = jnp.sum(do * o_ref[span, :], axis=0, keepdims=True)
            high = delta.astype(BF16).astype(F32)
            rest = jnp.concatenate([-high, high - delta, fill], axis=0).astype(BF16)
            g_aug[h * aug : h * aug + head_dim, :] = do.astype(BF16)
            g_aug[h * aug + head_dim : (h + 1) * aug, :] = rest
            v_aug[h * aug : h * aug + head_dim, :] = v_ref[span, :]
            v_aug[h * aug + head_dim : (h + 1) * aug, :] = ones

    lanes = pl.ds(pl.multiple_of(step * tile, tile), tile)
    slopes = []
    for h in range(heads):
        span = slice(h * head_dim, (h + 1) * head_dim)
        soft = p_ref[h]
        g_part = g_aug[h * aug : (h + 1) * aug, lanes]
        diff = mm(g_part, v_aug[h * aug : (h + 1) * aug, :], TN)
        slope = (soft.astype(F32) * diff).astype(BF16)
        slopes.append(slope)
        dqkv[span, lanes] = (mm(k_ref[span, :], slope, NT) * scale).astype(BF16)
        dk_acc[span, :] += mm(q_ref[span, :], slope, NN) * scale
        dv_acc[span, :] += mm(g_part[:head_dim], soft, NN)
    idx = idx_ref[...].astype(F32).astype(I32)
    high = (idx // LOW_BINS).astype(F32).astype(BF16)
    low = (idx % LOW_BINS).astype(F32).astype(BF16)
    high_bins = hist.shape[1] // (heads * PAIR_ROWS)
    one = jnp.ones((), BF16)
    zero = jnp.zeros((), BF16)
    total = hist[...]
    for s in range(0, tile, PAIR_ROWS):
        rows = slice(s, s + PAIR_ROWS)
        left = jnp.concatenate(
            [jnp.where(low[rows] == n, one, zero) for n in range(LOW_BINS)], axis=0
        )
        right = jnp.concatenate(
            [
                jnp.where(high[rows] == n, slopes[h][rows], zero)
                for h in range(heads)
                for n in range(high_bins)
            ],
            axis=0,
        )
        total = total + mm(left, right, NT)
    hist[...] = total

    @pl.when(step == steps - 1)
    def _():
        dqkv[part : 2 * part, :] = dk_acc[...].astype(BF16)
        dqkv[2 * part :, :] = dv_acc[...].astype(BF16)
        r1 = row_ref[0:1, :]
        inner = jnp.zeros((1, keys), F32)
        gain_rows = []
        for d in range(count):
            rows = slice(d * part, (d + 1) * part)
            dn1 = mm(w_ref[rows, :], dqkv[...], NN)
            dn1_acc[d] = dn1.astype(BF16)
            dn1_x = dn1 * x_ref[rows, :].astype(F32)
            inner = inner + jnp.sum(dn1_x * col_ref[rows, :], axis=0, keepdims=True)
            gain = jnp.sum(dn1_x * r1, axis=1, keepdims=True)
            gain_rows.append(jnp.transpose(jnp.broadcast_to(gain, (part, LANES)))[:1])
        cells = hist[...]
        same = lax.broadcasted_iota(I32, cells.shape, 0) % PAIR_ROWS == (
            lax.broadcasted_iota(I32, cells.shape, 1) % PAIR_ROWS
        )
        cells = jnp.where(same, cells, 0.0)
        low_rows = (LOW_BINS, cells.shape[0])
        sum_rows = jnp.where(
            lax.broadcasted_iota(I32, low_rows, 1) // PAIR_ROWS
            == lax.broadcasted_iota(I32, low_rows, 0),
            1.0,
            0.0,
        )
        lane_cols = (cells.shape[1], LANES)
        bins = heads * high_bins
        sum_cols = jnp.where(
            lax.broadcasted_iota(I32, lane_cols, 0) // PAIR_ROWS + me * bins
            == lax.broadcasted_iota(I32, lane_cols, 1),
            1.0,
            0.0,
        )
        exact = functools.partial(
            lax.dot_general,
            dimension_numbers=NN,
            precision=lax.Precision.HIGHEST,
            preferred_element_type=F32,
        )
        table = exact(exact(sum_rows, cells), sum_cols)
        half = LOW_BINS // 2
        tail = jnp.zeros((1, width - half * LANES), F32)
        table_rows = [
            jnp.concatenate([table[n + m : n + m + 1] for m in range(half)] + [tail], axis=1)
            for n in (0, half)
        ]
        small = jnp.concatenate(
            [jnp.concatenate(gain_rows, axis=1), gain_two_ref[...]] + table_rows, axis=0
        )
        inner_high = inner.astype(BF16).astype(F32)
        extra = jnp.concatenate(
            [inner_high, inner - inner_high, jnp.zeros((PAIR_ROWS - 2, keys), F32)], axis=0
        ).astype(BF16)
        for k in range(count):
            dn1_refs[k][:part, :] = dn1_acc[me ^ k]
            dn1_refs[k][part:, :] = extra
        router = jnp.transpose(router_acc[...])
        band = width // cols
        share = experts // cols
        pad = jnp.zeros((share, width - part), F32)
        pieces_of = lambda a, first: a[first : first + band, :]
        halves = part // band
        for b in range(halves):
            three = jnp.concatenate(
                [pieces_of(dqkv, w * part + b * band) for w in range(3)], axis=0
            )
            da_part = pieces_of(da_ref, b * band)
            whole = jnp.concatenate(
                [mm(n1_ref[...], three, NT), mm(ofull_ref[...], da_part, NT)], axis=1
            ).astype(BF16)
            for c in range(cols):
                proj_ref[c, :band, b * 4 * band : (b + 1) * 4 * band] = whole[
                    c * band : (c + 1) * band
                ]
        for c in range(cols):
            own = jnp.concatenate([router[c * share : (c + 1) * share], pad], axis=1)
            facts = jnp.concatenate([own, small], axis=0)
            facts_high = facts.astype(BF16).astype(F32)
            proj_ref[c, band:, :] = jnp.concatenate(
                [facts_high, facts - facts_high], axis=0
            ).astype(BF16)


def attend_back(
    place, q, k, v, idx, p, o, slot, h1, row_facts, gain, x, n1, o_full, w, gain_two, pieces, cols, buckets, tile
):
    part, keys = q.shape
    width = x.shape[0]
    count = len(pieces)
    heads = p.shape[0]
    experts = (pieces[0].shape[1] - 3 * part) // 2
    aug_width = part + heads * PAIR_ROWS
    hist_shape = (LOW_BINS * PAIR_ROWS, heads * (buckets // LOW_BINS) * PAIR_ROWS)
    fixed = lambda a: pl.BlockSpec(a.shape, lambda i, m: (0,) * len(a.shape))
    outs = [
        jax.ShapeDtypeStruct((part, keys), BF16),
        jax.ShapeDtypeStruct((part, keys), BF16),
        jax.ShapeDtypeStruct((cols, width // cols + PAIR_ROWS, width), BF16),
    ] + [jax.ShapeDtypeStruct((part + PAIR_ROWS, keys), BF16)] * count
    rest = (o, slot, h1, row_facts, gain, x, n1, o_full, w, gain_two, *pieces)
    out = pl.pallas_call(
        functools.partial(back_kernel, heads, count, experts, cols),
        grid_spec=pltpu.PrefetchScalarGridSpec(
            num_scalar_prefetch=1,
            grid=(keys // tile,),
            in_specs=[
                pl.BlockSpec((part, tile), lambda i, m: (0, i)),
                fixed(k),
                fixed(v),
                pl.BlockSpec((tile, keys), lambda i, m: (i, 0)),
                pl.BlockSpec((heads, tile, keys), lambda i, m: (0, i, 0)),
            ]
            + [fixed(a) for a in rest],
            out_specs=[fixed(a) for a in outs],
            scratch_shapes=[
                pltpu.VMEM((aug_width, keys), BF16),
                pltpu.VMEM((aug_width, keys), BF16),
                pltpu.VMEM((3 * part, keys), BF16),
                pltpu.VMEM((part, keys), F32),
                pltpu.VMEM((part, keys), F32),
                pltpu.VMEM(hist_shape, F32),
                pltpu.VMEM((part, experts), F32),
                pltpu.VMEM((count, part, keys), BF16),
            ],
        ),
        out_shape=outs,
        compiler_params=pltpu.CompilerParams(vmem_limit_bytes=56 * 2**20),
        cost_estimate=QUICK,
    )(place, q, k, v, idx, p, *rest)
    return out[0], out[1], out[2], out[3:]


def fill_rows(place_ref, places, in_refs, win, part):
    for in_ref, (k, offset) in zip(in_refs, places):
        first = pl.multiple_of((place_ref[0] ^ k) * part + offset, PAIR_ROWS)
        win[pl.ds(first, in_ref.shape[0]), :] = in_ref[...]


def inner_kernel(count, places, ge_places, place_ref, x_ref, dy_ref, router_ref, *refs):
    in_refs, refs = refs[: len(places)], refs[len(places) :]
    dys_ref, hidden_ref, slope_ref = refs[:3]
    ge_refs, win = refs[3:-1], refs[-1]
    step = pl.program_id(0)

    @pl.when(step == 0)
    def _():
        logits = mm(x_ref[...], router_ref[...], NN)
        probs = jnp.exp(logits - jnp.max(logits, axis=1, keepdims=True))
        own = lax.broadcasted_iota(I32, logits.shape, 1) == place_ref[1]
        gate = jnp.sum(jnp.where(own, probs, 0.0), axis=1, keepdims=True)
        gate = gate / jnp.sum(probs, axis=1, keepdims=True)
        dys_ref[...] = (gate * dy_ref[...].astype(F32)).astype(BF16)

    fill_rows(place_ref, places, in_refs, win, win.shape[0] // count)
    pre = mm(x_ref[...], win[...], NN)
    square = pre * pre
    curve = jnp.tanh(GELU_SCALE * pre * (1.0 + GELU_CUBE * square))
    half = 0.5 * (1.0 + curve)
    hidden = (pre * half).astype(BF16)
    hidden_ref[...] = hidden
    slope = half + 0.5 * pre * (1.0 - curve * curve) * (
        GELU_SCALE * (1.0 + 3.0 * GELU_CUBE * square)
    )
    slope_ref[...] = slope.astype(BF16)
    ge = mm(hidden, dys_ref[...], TN).astype(BF16)
    for ge_ref, (k, first, size) in zip(ge_refs, ge_places):

        @pl.when(step == k)
        def _(ge_ref=ge_ref, first=first, size=size):
            ge_ref[...] = ge[first : first + size]


def outer_kernel(
    count, places, eout_places, place_ref, x_ref, dys_ref, hidden_ref, slope_ref, *refs
):
    in_refs, refs = refs[: len(places)], refs[len(places) :]
    eout_refs, refs = refs[: len(eout_places)], refs[len(eout_places) :]
    back_ref, gi_refs = refs[0], refs[1 : count + 1]
    win, eout, y_acc, dx_acc, gi = refs[count + 1 :]
    step = pl.program_id(0)
    part = gi_refs[0].shape[0]

    @pl.when(step == 0)
    def _():
        y_acc[...] = jnp.zeros_like(y_acc)
        dx_acc[...] = jnp.zeros_like(dx_acc)

    fill_rows(place_ref, places, in_refs, win, part)
    for eout_ref, (k, first) in zip(eout_refs, eout_places):

        @pl.when(step == k)
        def _(eout_ref=eout_ref, first=first):
            eout[first : first + eout_ref.shape[0], :] = eout_ref[...]

    y_acc[...] += mm(hidden_ref[...], eout[...], NN)
    dpre = (mm(dys_ref[...], eout[...], NT) * slope_ref[...].astype(F32)).astype(BF16)
    dx_acc[...] += mm(dpre, win[...], NT)
    gi[...] = mm(x_ref[...], dpre, TN).astype(BF16)
    for k in range(count):
        gi_refs[k][...] = gi[pl.ds(pl.multiple_of((place_ref[0] ^ k) * part, part), part), :]

    @pl.when(step == count - 1)
    def _():
        width = y_acc.shape[1]
        back_ref[:, :width] = y_acc[...].astype(BF16)
        back_ref[:, width:] = dx_acc[...].astype(BF16)


def expert_inner(place, x, dy, router, in_held, places, ge_places, count):
    slots, width = x.shape
    hidden_width = in_held[0].shape[1]
    chunk = hidden_width // count
    fixed = lambda shape: pl.BlockSpec(shape, lambda i, m: (0, 0))
    wide = pl.BlockSpec((slots, chunk), lambda i, m: (0, i))
    shape = lambda s: jax.ShapeDtypeStruct(s, BF16)
    out = pl.pallas_call(
        functools.partial(inner_kernel, count, places, ge_places),
        grid_spec=pltpu.PrefetchScalarGridSpec(
            num_scalar_prefetch=1,
            grid=(count,),
            in_specs=[fixed(x.shape), fixed(dy.shape), fixed(router.shape)]
            + [pl.BlockSpec((a.shape[0], chunk), lambda i, m: (0, m[0] ^ i)) for a in in_held],
            out_specs=[fixed(x.shape), wide, wide]
            + [fixed((size, width)) for _, _, size in ge_places],
            scratch_shapes=[pltpu.VMEM((width, chunk), BF16)],
        ),
        out_shape=[shape(x.shape)]
        + [shape((slots, hidden_width))] * 2
        + [shape((size, width)) for _, _, size in ge_places],
        compiler_params=pltpu.CompilerParams(vmem_limit_bytes=56 * 2**20),
        cost_estimate=QUICK,
    )(place, x, dy, router, *in_held)
    return out[0], out[1], out[2], out[3:]


def expert_outer(place, x, dys, hidden, slope, in_held, places, eout_held, eout_places, count):
    slots, width = x.shape
    hidden_width = in_held[0].shape[1]
    part = width // count
    chunk = hidden_width // count
    fixed = lambda shape: pl.BlockSpec(shape, lambda i, m: (0, 0))
    wide = pl.BlockSpec((slots, chunk), lambda i, m: (0, i))
    lanes = lambda rows: pl.BlockSpec((rows, chunk), lambda i, m: (0, m[0] ^ i))
    out = pl.pallas_call(
        functools.partial(outer_kernel, count, places, eout_places),
        grid_spec=pltpu.PrefetchScalarGridSpec(
            num_scalar_prefetch=1,
            grid=(count,),
            in_specs=[fixed(x.shape), fixed(x.shape), wide, wide]
            + [lanes(a.shape[0]) for a in in_held]
            + [fixed(a.shape) for a in eout_held],
            out_specs=[fixed((slots, 2 * width))] + [lanes(part)] * count,
            scratch_shapes=[
                pltpu.VMEM((width, chunk), BF16),
                pltpu.VMEM((chunk, width), BF16),
                pltpu.VMEM((slots, width), F32),
                pltpu.VMEM((slots, width), F32),
                pltpu.VMEM((width, chunk), BF16),
            ],
        ),
        out_shape=[jax.ShapeDtypeStruct((slots, 2 * width), BF16)]
        + [jax.ShapeDtypeStruct((part, hidden_width), BF16)] * count,
        compiler_params=pltpu.CompilerParams(vmem_limit_bytes=56 * 2**20),
        cost_estimate=QUICK,
    )(place, x, dys, hidden, slope, *in_held, *eout_held)
    return out[0], out[1:]


def slot_kernel(
    count,
    experts,
    place_ref,
    home_ref,
    dy_ref,
    n2_ref,
    h1_ref,
    scalar_ref,
    router_ref,
    out_ref,
    gain_ref,
    gain_part_ref,
    *refs,
):
    me = place_ref[0]
    parcel_refs, parcel = refs[:count], refs[count]
    slots, width = dy_ref.shape
    part = width // count
    y = home_ref[:, :width]
    dy = dy_ref[...].astype(F32)
    h1 = h1_ref[...].astype(F32)
    scalars = scalar_ref[...]
    probs, gate, r2 = scalars[:, :experts], scalars[:, experts : experts + 1], scalars[:, experts + 1 :]
    dgate = jnp.sum(dy * y.astype(F32), axis=1, keepdims=True)
    row = lax.broadcasted_iota(I32, (slots, experts), 0)
    lane = lax.broadcasted_iota(I32, (slots, experts), 1)
    hot = jnp.where(row // CAPACITY * count + me == lane, 1.0, 0.0)
    dlogits = ((dgate * gate) * (hot - probs)).astype(BF16)
    dn2 = home_ref[:, width:].astype(F32) + mm(dlogits, router_ref[...], NT)
    scaled = dn2 * gain_ref[...]
    inner = jnp.sum(scaled * h1, axis=1, keepdims=True)
    dh1 = dy + r2 * scaled - h1 * (r2 * r2 * r2 * (1.0 / width) * inner)
    gain_part_ref[...] = jnp.sum(dn2 * h1 * r2, axis=0, keepdims=True)
    da = dh1.astype(BF16)
    do = mm(da, out_ref[...], NT).astype(BF16)
    router_high, router_low = two_parts(mm(n2_ref[...], dlogits, TN))
    fill = jnp.zeros((slots - part, 2 * experts), BF16)
    for d in range(count):
        span = slice(d * part, (d + 1) * part)
        router = jnp.concatenate([router_high[span], router_low[span]], axis=1)
        router = jnp.concatenate([router, fill], axis=0)
        parcel[me ^ d] = jnp.concatenate([y[:, span], da[:, span], do[:, span], router], axis=1)
    for k in range(count):
        parcel_refs[k][...] = parcel[k]


def slot_work(place, home, dy, n2, h1, scalars, router, out_proj, gain, count):
    slots, width = dy.shape
    experts = router.shape[1]
    lanes = 3 * width // count + 2 * experts
    fixed = lambda a: pl.BlockSpec(a.shape, lambda i, m: (0,) * len(a.shape))
    ins = (home, dy, n2, h1, scalars, router, out_proj, gain)
    outs = [jax.ShapeDtypeStruct((1, width), F32)]
    outs += [jax.ShapeDtypeStruct((slots, lanes), BF16)] * count
    out = pl.pallas_call(
        functools.partial(slot_kernel, count, experts),
        grid_spec=pltpu.PrefetchScalarGridSpec(
            num_scalar_prefetch=1,
            grid=(1,),
            in_specs=[fixed(a) for a in ins],
            out_specs=[fixed(a) for a in outs],
            scratch_shapes=[pltpu.VMEM((count, slots, lanes), BF16)],
        ),
        out_shape=outs,
        compiler_params=pltpu.CompilerParams(vmem_limit_bytes=48 * 2**20),
        cost_estimate=QUICK,
    )(place, *ins)
    return out[1:], out[0]


def send(piece, offset):
    count = lax.axis_size("row")
    return lax.ppermute(piece, "row", [(i, i ^ offset) for i in range(count)])


def row_join(block, far):
    me = lax.axis_index("row")
    count = lax.axis_size("row")
    near = send(jnp.stack([block, far]), 1)
    held = jnp.stack([block, near[0], far, near[1]])
    return jnp.concatenate(
        [lax.dynamic_index_in_dim(held, p ^ me, 0, keepdims=True) for p in range(count)]
    )


def row_gather(block):
    return row_join(block, send(block, 2))


def swap(blocks, axis):
    return lax.all_to_all(blocks, axis, 0, 0)


def col_gather(block):
    count = lax.axis_size("col")
    return swap(jnp.broadcast_to(block[None], (count,) + block.shape), "col")


def trade(piece_for):
    me = lax.axis_index("row")
    return trade_pieces([piece_for(me ^ k) for k in range(lax.axis_size("row"))])


def trade_pieces(pieces):
    count = len(pieces)
    held = {k: send(pieces[k], k) for k in (2, 3, 1)}
    return [pieces[0]] + [held[k] for k in range(1, count)]


def lay(held):
    me = lax.axis_index("row")
    out = jnp.zeros((len(held),) + held[0].shape, held[0].dtype)
    for k, piece in enumerate(held):
        out = lax.dynamic_update_slice_in_dim(out, piece[None], me ^ k, 0)
    return out


def after(value, *earlier):
    return lax.optimization_barrier((value,) + earlier)[0]


def fill_kernel(count, me_ref, *refs):
    step = pl.program_id(1)
    for k in range(count):

        @pl.when(step == k)
        def _(k=k):
            refs[count][...] = refs[k][...].astype(F32)


def fill_columns(held, splits):
    count = len(held)
    height, width = held[0].shape
    block = height // splits
    me = lax.axis_index("row").astype(I32).reshape(1)
    return pl.pallas_call(
        functools.partial(fill_kernel, count),
        grid_spec=pltpu.PrefetchScalarGridSpec(
            num_scalar_prefetch=1,
            grid=(splits, count),
            in_specs=[pl.BlockSpec((block, width), lambda i, k, m: (i, 0))] * count,
            out_specs=pl.BlockSpec((block, width), lambda i, k, m: (i, m[0] ^ k)),
        ),
        out_shape=jax.ShapeDtypeStruct((height, count * width), F32),
        compiler_params=pltpu.CompilerParams(vmem_limit_bytes=48 * 2**20),
        cost_estimate=QUICK,
    )(me, *held)


def own_rows(array, me, count):
    return lax.dynamic_slice_in_dim(array, me * count, count, 0)


def expert_plan(
    tokens,
    gain_one,
    gain_two,
    w_query,
    w_key,
    w_value,
    w_out,
    w_router,
    w_in,
    w_expert_out,
    bias_table,
    segment,
    expert,
    bucket,
    cotangent,
):
    rows, cols = lax.axis_size("row"), lax.axis_size("col")
    me, col = lax.axis_index("row"), lax.axis_index("col")
    part, seq_len = tokens.shape[1:]
    width = part * rows
    tok_rows = seq_len // rows
    buckets, all_heads = bias_table.shape
    heads = all_heads // rows
    head_dim = width // all_heads
    experts = w_router.shape[1] * cols
    hidden_width = w_expert_out.shape[0] * rows
    slots = (experts // rows) * CAPACITY
    out_cols = w_query.shape[1]
    share = cols // rows

    doc_ids = segment[0]
    expert_ids = expert[0, :, 0]

    tok_far = send(tokens[0], 2)
    tok_low = row_join(tokens[0], tok_far).reshape(width, seq_len)
    qkv_cols = col_gather(jnp.concatenate([w_query, w_key, w_value], axis=1))
    same_doc = own_rows(doc_ids, me, tok_rows)[:, None] == doc_ids[None, :]
    masked = jnp.where(same_doc, after(bucket, tok_far)[0], buckets).astype(BF16)
    idx_far = send(masked, 2)
    cot_own = cotangent[0]
    cot_far = send(cot_own, 2)
    lane_cut = lambda array, count, k: lax.dynamic_slice_in_dim(array, (me ^ k) * count, count, 1)
    half = part // 2
    in_first = send(lane_cut(after(w_in, tok_far)[:half], hidden_width, 2), 2)
    eout_half = w_expert_out.shape[0] // 4
    later_eout = after(w_expert_out, tok_far)
    eout_cuts = [lane_cut(later_eout, width, k) for k in range(3)]
    eout_cuts.append(lane_cut(later_eout[:eout_half], width, 3))
    eout_cuts.append(lane_cut(later_eout[eout_half:], width, 3))
    later_in = after(w_in, tok_far)
    second_cut = lane_cut(later_in[half:], hidden_width, 2)
    in_cuts = {k: lane_cut(later_in, hidden_width, k) for k in (1, 3)}
    cuts = (*eout_cuts, second_cut, in_cuts[1], in_cuts[3])
    qkv_cols = after(qkv_cols, idx_far, cot_far, in_first, *cuts)
    out_part = after(jnp.concatenate([w_out, w_router], axis=1), qkv_cols)
    out_gathered = col_gather(out_part)
    qkv_cols = qkv_cols.reshape(rows, share, part, 3 * out_cols)
    qkv_held = trade(lambda d: lax.dynamic_index_in_dim(qkv_cols, d, 0, keepdims=False))
    qkv_own = jnp.transpose(
        lay(qkv_held).reshape(rows, share, part, 3, out_cols), (0, 2, 3, 1, 4)
    ).reshape(width, 3 * part)
    idx = row_join(masked, idx_far).reshape(seq_len, seq_len)
    cot_low = row_join(cot_own, cot_far).reshape(width, seq_len)

    picked = expert_ids[None, :] == jnp.arange(experts, dtype=I32)[:, None]
    picked_float = picked.astype(F32)
    steps = jnp.arange(seq_len, dtype=I32)
    upper = (steps[:, None] <= steps[None, :]).astype(BF16)
    ranks = mm(picked.astype(BF16), upper, NN) - 1.0
    slot_rank = jnp.sum(ranks * picked_float, axis=0).astype(I32)
    slot = (expert_ids % rows) * slots + (expert_ids // rows) * CAPACITY + slot_rank
    choose = (jnp.arange(slots, dtype=I32)[:, None] + me * slots == slot[None, :]).astype(BF16)

    x = after(tok_low, qkv_cols).astype(F32)
    r1 = lax.rsqrt(jnp.mean(x * x, axis=0) + NORM_EPS)
    n1 = (x * r1 * gain_one[:, None]).astype(BF16)
    qkv = mm(qkv_own, n1, TN).astype(BF16)
    in_places = ((0, 0), (2, 0), (2, half), (3, 0), (1, 0))
    in_second = send(after(second_cut, qkv), 2)
    in_held = [lane_cut(after(w_in, qkv), hidden_width, 0), in_first, in_second]
    for k in (3, 1):
        in_held.append(send(after(in_cuts[k], qkv), k))
    qkv, n1, qkv_own = lax.optimization_barrier((qkv, n1, qkv_own))
    q, k, v = qkv[:part], qkv[part : 2 * part], qkv[2 * part :]
    table = lax.dynamic_slice_in_dim(jnp.transpose(bias_table), me * heads, heads, 0)
    table = jnp.pad(
        table, ((0, 8 - heads), (0, LANES - buckets)), constant_values=NEG_FILL
    )
    o32, p = attend(q, k, v, idx, table, heads, 256)
    expert_at = lambda a: swap(a.reshape(cols, CAPACITY, width), "col").reshape(slots, width)
    dy_low = mm(choose, after(cot_low, qkv), NT).astype(BF16)
    o_low = after(o32.astype(BF16), in_second, in_held[3])
    dy_slots = expert_at(dy_low)
    o_far = send(o_low, 2)
    o_full = row_join(o_low, after(o_far, dy_slots)).reshape(width, seq_len)
    out_gathered = after(out_gathered, o32)
    out_rows = jnp.transpose(out_gathered[:, :, :out_cols], (1, 0, 2)).reshape(part, width)
    router_rows = jnp.transpose(out_gathered[:, :, out_cols:], (1, 0, 2)).reshape(part, experts)
    out_router = jnp.concatenate([out_rows, router_rows], axis=1)
    out_router = row_gather(out_router).reshape(width, width + experts)
    out_full, router_full = out_router[:, :width], out_router[:, width:]
    eout_two = send(after(eout_cuts[2], o_far), 2)
    eout_three = send(after(eout_cuts[3], o_far), 3)
    h1 = x + mm(out_full, o_full, TN)
    r2 = lax.rsqrt(jnp.mean(h1 * h1, axis=0) + NORM_EPS)
    n2 = (h1 * r2 * gain_two[:, None]).astype(BF16)
    logits = mm(router_full, n2, TN)
    g = jax.nn.softmax(logits, axis=0)
    gate = jnp.sum(g * picked_float, axis=0)

    n2_low = mm(choose, n2, NT).astype(BF16)
    slots_in = after(expert_at(n2_low), eout_two, eout_three)
    eout_last = send(after(eout_cuts[4], slots_in), 3)
    eout_one = send(after(eout_cuts[1], slots_in), 1)
    eout_held = [eout_cuts[0], eout_one, eout_two, eout_three, eout_last]
    eout_places = ((0, 0), (1, 0), (2, 0), (3, 0), (3, eout_half))
    place = jnp.stack([me, col * rows + me]).astype(I32)
    hid = w_expert_out.shape[0]
    ge_cut = hid // 4 * 3
    ge_places = ((0, 0, hid), (1, 0, hid), (2, 0, ge_cut), (2, ge_cut, hid - ge_cut), (3, 0, hid))
    dys, hidden, slope, ge = expert_inner(
        place, slots_in, dy_slots, router_full, in_held, in_places, ge_places, rows
    )
    hidden = after(hidden, *ge)
    back, in_pieces = expert_outer(
        place, slots_in, dys, hidden, slope, in_held, in_places, eout_held, eout_places, rows
    )
    grad_eout_first = send(ge[2], 2)
    back = after(back, grad_eout_first)
    grad_eout_held = [
        ge[0],
        send(after(ge[1], back), 1),
        send(after(ge[3], back), 2),
        send(after(ge[4], back), 3),
    ]
    home = swap(back.reshape(cols, CAPACITY, 2 * width), "col").reshape(slots, 2 * width)

    h1_s = mm(choose, h1.astype(BF16), NT).astype(BF16)
    h1_own = own_rows(h1, me, part)
    home = after(home, h1_own)
    scalars = lax.dot_general(
        choose.astype(F32),
        jnp.concatenate([g, gate[None], r2[None]], axis=0),
        NT,
        precision=lax.Precision.HIGHEST,
        preferred_element_type=F32,
    )
    parcel, gain_two_part = slot_work(
        place, home, dy_low, n2_low, h1_s, scalars, router_full, out_full, gain_two[None], rows
    )
    parcel = trade_pieces(after(tuple(parcel), *grad_eout_held[2:]))
    in_turn = lambda piece: after(piece, parcel[2], parcel[3])
    grad_in_held = [
        in_pieces[0],
        send(in_turn(in_pieces[1]), 1),
        send(in_turn(in_pieces[2]), 2),
    ]
    grad_in_half = send(in_turn(in_pieces[3][:half]), 3)

    layer_out, da, proj_parcel, dn1_parcel = attend_back(
        place,
        q,
        k,
        v,
        idx,
        p,
        o32,
        slot[None],
        h1_own,
        jnp.stack([r1, gate]),
        gain_one[:, None],
        tok_low,
        n1,
        o_full,
        qkv_own,
        gain_two_part,
        parcel,
        cols,
        buckets,
        256,
    )
    dn1_parcel, proj_parcel = after(
        (tuple(dn1_parcel), proj_parcel), grad_in_half, grad_in_held[2]
    )
    dn1_held = trade_pieces(dn1_parcel)
    grad_in_held.append(send(after(in_pieces[3][half:], dn1_held[2], dn1_held[3]), 3))
    dn1_sum = sum(piece.astype(F32) for piece in dn1_held)
    dn1 = dn1_sum[:part]
    inner_one = dn1_sum[part] + dn1_sum[part + 1]
    gain_own = own_rows(gain_one, me, part)
    grad_tokens = (
        da.astype(F32)
        + r1 * gain_own[:, None] * dn1
        - own_rows(x, me, part) * (r1**3 / width * inner_one)
    ).astype(BF16)

    band = width // cols
    proj_sum = jnp.sum(swap(proj_parcel, "col").astype(F32), axis=0)
    half = PAIR_ROWS // 2
    extra_sum = proj_sum[band : band + half] + proj_sum[band + half :]
    router_rows = experts // cols
    grad_router = jnp.transpose(extra_sum[:router_rows, :part])
    small = sum(trade_pieces([extra_sum[router_rows:]] * rows))
    gain_one_grad, gain_two_grad = small[0], small[1]
    table_grad = jnp.transpose(
        small[2:, : LOW_BINS // 2 * LANES]
        .reshape(LOW_BINS, LANES)[:, : bias_table.size // LOW_BINS]
        .reshape(LOW_BINS, all_heads, buckets // LOW_BINS),
        (2, 0, 1),
    ).reshape(bias_table.shape)
    pieces = []
    for turn in range(share):
        moves = [
            (r * cols + c, (c // share) * cols + share * r + (c + turn) % share)
            for r in range(rows)
            for c in range(cols)
        ]
        first = (col + turn) % share * 4 * out_cols
        piece = lax.dynamic_slice_in_dim(proj_sum[:band], first, 4 * out_cols, 1)
        pieces.append(lax.ppermute(piece, ("row", "col"), moves))
    pieces = jnp.stack(pieces)
    grad_four = jnp.concatenate(
        [
            lax.dynamic_index_in_dim(pieces, (col - half) % share, 0, keepdims=False)
            for half in range(share)
        ],
        axis=0,
    )
    grad_query, grad_key, grad_value, grad_out = [
        grad_four[:, w * out_cols : (w + 1) * out_cols] for w in range(4)
    ]
    last = after(grad_in_held[3], proj_sum)
    grad_in_held[3] = jnp.concatenate([grad_in_half, last], axis=0)
    grad_eout_held[2] = jnp.concatenate([grad_eout_first, grad_eout_held[2]], axis=0)
    grad_in, grad_eout = fill_columns(grad_in_held, 2), fill_columns(grad_eout_held, 2)
    return (
        layer_out[None],
        grad_tokens[None],
        gain_one_grad,
        gain_two_grad,
        grad_query,
        grad_key,
        grad_value,
        grad_out,
        grad_router,
        grad_in,
        grad_eout,
        table_grad,
    )


def solution(mesh):
    rows, cols = mesh.shape["row"], mesh.shape["col"]
    paired = rows == 4 and cols == 2 * rows and EXPERTS == rows * cols
    return jax.shard_map(
        expert_plan if paired else general_plan,
        mesh=mesh,
        in_specs=(
            P("col", "row", None),
            P(),
            P(),
            P("row", "col"),
            P("row", "col"),
            P("row", "col"),
            P("row", "col"),
            P("row", "col"),
            P("row", "col"),
            P("row", "col"),
            P(),
            P("col", None),
            P("col", None, None),
            P("col", "row", None),
            P("col", "row", None),
        ),
        out_specs=(
            P("col", "row", None),
            P("col", "row", None),
            P(),
            P(),
            P("row", "col"),
            P("row", "col"),
            P("row", "col"),
            P("row", "col"),
            P("row", "col"),
            P("row", "col"),
            P("row", "col"),
            P(),
        ),
        check_vma=False,
    )
```
